32 devices in a mesh: space: 8 (over z, x), mode: 4 (over y, core).
Axes of the slice: x: 2, y: 2, z: 4, core: 2. Of those that a mesh axis runs over, the one named last changes fastest.
Arguments:
- chaos_field: float32 [84, 8, 128, 128], P('mode', 'space'), may hold values from -6 to 6
- mean_field: float32 [8, 128, 128], P('space'), may hold values from 0.5 to 2
- kl_fields: float32 [6, 8, 128, 128], P(None, 'space'), may hold values from -1.8 to 1.8
- pattern: int32 [7, 84, 84], replicated, may hold values from 0 to 1, as said below
- coupling: float32 [7, 84, 84], replicated, as said below
- slot_mode: int32 [84], replicated, may hold values from 0 to 83, each once
Outputs:
- product: float32 [84, 8, 128, 128], P('mode', 'space')
The draws below stay inside these ranges and needn't reach their ends.
Inputs may be any that keep to these rules, and one draw needn't show every extreme that they name: Modes are the 84 multi-indices of total degree at most 3 in 6 variables; pattern[0] is the identity; each term k >= 1 belongs to one variable, each variable to one term, and pattern[k, a, b] is 1 exactly where the multi-indices of modes a and b differ by one in that variable and agree elsewhere. coupling[0] is the identity; for k >= 1, coupling[k, a, b] is the square root of the larger of the two degrees in the term's variable where pattern[k, a, b] is 1, and zero elsewhere; pattern and coupling name the same variable for each term. `slot_mode`: each slot holds a different chaos mode.
All inputs are finite; a program needn't handle non-finite values.
Results may differ from the reference program's by a relative error of at most 0.000082.
Values sent between devices are 32-bit elements; how exact they have to be, the bound alone decides.
No kernel may reach another device: no remote copies, remote signals or barrier semaphores. Data moves between devices by JAX's collectives and lax.ppermute only.
A program may use at most 320 MiB of HBM per device.

```python
import math
import jax
import jax.numpy as jnp
import numpy as np
from jax import lax

P_SIZE = 84
KL = 6
NXY = 128
NZ = 8


def compositions(variables, degree):
    if variables == 1:
        return [(degree,)]
    listing = []
    for leading in range(degree, -1, -1):
        for remainder in compositions(variables - 1, degree - leading):
            listing.append((leading,) + remainder)
    return listing


def chaos_tables(variables, number_modes):
    indices = []
    for degree in range(0, 4):
        indices = indices + compositions(variables, degree)
    indices = indices[:number_modes]
    values = np.zeros((variables, number_modes, number_modes), np.float32)
    marks = np.zeros((variables, number_modes, number_modes), np.int32)
    for first_mode in range(number_modes):
        for second_mode in range(number_modes):
            differ = np.array(indices[first_mode]) - np.array(indices[second_mode])
            if int(np.sum(np.abs(differ))) == 1:
                variable = int(np.argmax(np.abs(differ)))
                larger = max(indices[first_mode][variable], indices[second_mode][variable])
                values[variable, first_mode, second_mode] = math.sqrt(larger)
                marks[variable, first_mode, second_mode] = 1
    return (values, marks)


def term_variables(key):
    return jax.random.permutation(jax.random.fold_in(key, 11), KL)


def draw_pattern(key, part):
    shuffle = term_variables(key)
    values, marks = chaos_tables(KL, P_SIZE)
    linear = jnp.asarray(marks)[shuffle]
    identity = jnp.eye(P_SIZE, dtype=jnp.int32)
    return jnp.concatenate([identity[None], linear], 0).astype(jnp.int32)


def draw_coupling(key, part):
    shuffle = term_variables(key)
    values, marks = chaos_tables(KL, P_SIZE)
    linear = jnp.asarray(values)[shuffle]
    identity = jnp.eye(P_SIZE, dtype=jnp.float32)
    return jnp.concatenate([identity[None], linear], 0).astype(jnp.float32)


def block_scale(rng, dims, split, low, largest):
    loudness, own = 1.0, jax.random.fold_in(rng, 6)
    for dim, shards_of in split:
        heights = jnp.exp(jax.random.uniform(jax.random.fold_in(own, dim), (shards_of,), jnp.float32, low / len(split), largest / len(split)))
        loudness = loudness * jnp.repeat(heights, dims[dim] // shards_of).reshape([-1 if axis == dim else 1 for axis in range(len(dims))])
    return loudness


def normal_values(own_key, shape, deviation, reach, pieces=(), held_as=jnp.bfloat16):
    loudness = block_scale(own_key, shape, pieces, -0.22, 0.18) if pieces else 1.0
    drawn = jax.random.normal(own_key, shape, jnp.float32) * deviation * loudness
    return jnp.minimum(jnp.maximum(drawn, -reach), reach).astype(held_as)


def setup_inputs(seed: int = 0) -> dict:
    keys = jax.random.split(jax.random.key(seed), 7)
    chaos_field = normal_values(keys[0], (P_SIZE, NZ, NXY, NXY), 1.0, 6.0, ((0, 4), (1, 8)), jnp.float32)
    mean_field = jnp.clip(jnp.exp(math.log(2.0) - 1.3862944 * jax.random.uniform(keys[1], (NZ, NXY, NXY), jnp.float32) ** block_scale(keys[1], (NZ, NXY, NXY), ((0, 8),), -0.2, 0.2)), 0.5, 2.0)
    kl_fields = normal_values(keys[2], (KL, NZ, NXY, NXY), 0.3, 1.8, ((1, 8),), jnp.float32)
    pattern = draw_pattern(jax.random.fold_in(keys[6], 71), 0)
    coupling = draw_coupling(jax.random.fold_in(keys[6], 71), 0)
    slot_mode = jax.random.permutation(keys[5], P_SIZE).astype(jnp.int32)
    return dict(chaos_field=chaos_field, mean_field=mean_field, kl_fields=kl_fields, pattern=pattern, coupling=coupling, slot_mode=slot_mode)


def face_weights(coef_ext):
    coef_here = coef_ext[:, 1:-1]
    height = coef_here.shape[2]
    breadth = coef_here.shape[3]
    coef_pad = jnp.pad(coef_here, ((0, 0), (0, 0), (1, 1), (1, 1)))
    weights = [0.5 * (coef_here + coef_ext[:, 2:]), 0.5 * (coef_here + coef_ext[:, :-2])]
    for shift_y, shift_x in ((2, 1), (0, 1), (1, 2), (1, 0)):
        weights.append(0.5 * (coef_here + coef_pad[:, :, shift_y:shift_y + height, shift_x:shift_x + breadth]))
    diagonal = weights[0] + weights[1] + weights[2] + weights[3] + weights[4] + weights[5]
    return diagonal, weights


def apply_operator(coef_ext, field_ext):
    diagonal, weights = face_weights(coef_ext)
    field_here = field_ext[:, 1:-1]
    height = field_here.shape[2]
    breadth = field_here.shape[3]
    field_pad = jnp.pad(field_here, ((0, 0), (0, 0), (1, 1), (1, 1)))
    total = diagonal * field_here - weights[0] * field_ext[:, 2:] - weights[1] * field_ext[:, :-2]
    index = 2
    for shift_y, shift_x in ((2, 1), (0, 1), (1, 2), (1, 0)):
        total = total - weights[index] * field_pad[:, :, shift_y:shift_y + height, shift_x:shift_x + breadth]
        index = index + 1
    return total


def slot_coupling(pattern, coupling, slot_mode):
    masked = coupling * pattern.astype(jnp.float32)
    return masked[:, slot_mode][:, :, slot_mode]


def reference(chaos_field, mean_field, kl_fields, pattern, coupling, slot_mode):
    coupled = slot_coupling(pattern, coupling, slot_mode)
    coefs = jnp.concatenate([mean_field[None], kl_fields], 0)
    coef_ext = jnp.pad(coefs, ((0, 0), (1, 1), (0, 0), (0, 0)))

    def one_slot(slot):
        weights = lax.dynamic_index_in_dim(coupled, slot, 1, keepdims=False)
        mixed = jnp.einsum('kt,tzyx->kzyx', weights, chaos_field, precision=lax.Precision.HIGHEST)
        mixed_ext = jnp.pad(mixed, ((0, 0), (1, 1), (0, 0), (0, 0)))
        return jnp.sum(apply_operator(coef_ext, mixed_ext), axis=0)

    return lax.map(one_slot, jnp.arange(P_SIZE, dtype=jnp.int32))
```

```python
import jax
import jax.numpy as jnp
from jax import lax
from jax.experimental import pallas as pl
from jax.experimental.pallas import tpu as pltpu
from jax.sharding import PartitionSpec as P

VMEM_LIMIT = 48 * 1024 * 1024
PLANES = 2


class Layout:
    def __init__(self, quota, terms, modes, height):
        self.modes = modes
        self.group = PLANES * modes
        self.rows = height // self.group
        self.quota = quota
        self.share = -(-terms // modes)
        self.fields = quota + self.share
        self.main = self.fields * self.rows
        self.block = -(-(self.main + 2 * self.fields) // 8) * 8

    def coef(self, term):
        return term // self.share, self.quota + term % self.share


def vmem(count):
    return [pl.BlockSpec(memory_space=pltpu.VMEM)] * count


def smem(count):
    return [pl.BlockSpec(memory_space=pltpu.SMEM)] * count


def pack(field, mean, kl, mode, lay):
    kl_terms = kl.shape[0]
    width = field.shape[2]
    zero_row = (1, width)

    def kernel(mode_ref, field_ref, mean_ref, kl_ref, out_ref):
        for i in range(lay.fields):
            if i < lay.quota:
                value = field_ref[i]
            else:
                term = mode_ref[0] * lay.share + (i - lay.quota)
                other = kl_ref[jnp.clip(term - 1, 0, kl_terms - 1)]
                value = jnp.where(term == 0, mean_ref[0], other)
            for j in range(lay.group):
                first = j * lay.rows
                last = first + lay.rows
                out_ref[j, i * lay.rows : (i + 1) * lay.rows, :] = value[first:last]
                low = value[first - 1 : first] if j > 0 else jnp.zeros(zero_row, jnp.float32)
                high = value[last : last + 1] if j < lay.group - 1 else jnp.zeros(zero_row, jnp.float32)
                at = lay.main + 2 * i
                out_ref[j, at : at + 1, :] = low
                out_ref[j, at + 1 : at + 2, :] = high
        spare = lay.block - lay.main - 2 * lay.fields
        if spare:
            for j in range(lay.group):
                out_ref[j, lay.block - spare :, :] = jnp.zeros((spare, width), jnp.float32)

    return pl.pallas_call(
        kernel,
        out_shape=jax.ShapeDtypeStruct((lay.group, lay.block, width), jnp.float32),
        in_specs=smem(1) + vmem(3),
        out_specs=vmem(1)[0],
        compiler_params=pltpu.CompilerParams(vmem_limit_bytes=VMEM_LIMIT),
        name="pack",
    )(mode, field, mean, kl)


def coupling_entries(pattern, coupling, slot_mode, lay):
    masked = (coupling * pattern.astype(jnp.float32))[1:]
    terms, modes = masked.shape[0], masked.shape[1]
    per_term = 56
    number = jnp.arange(modes, dtype=jnp.int32)
    slot_of = jnp.sum(jnp.where(slot_mode[:, None] == number[None, :], number[:, None], 0), 0)
    column = number[None, None, :]
    there = pattern[1:] != 0
    first = jnp.min(jnp.where(there, column, modes), 2)
    last = jnp.max(jnp.where(there, column, -1), 2)
    mode_t = jnp.concatenate([first, last], 1)
    valid = jnp.concatenate([first < modes, last > first], 1)
    value = jnp.concatenate(
        [
            jnp.sum(jnp.where(column == first[:, :, None], masked, 0.0), 2),
            jnp.sum(jnp.where(column == last[:, :, None], masked, 0.0), 2),
        ],
        1,
    )
    slot_s = jnp.concatenate([slot_of, slot_of])
    slot_t = jnp.sum(jnp.where(mode_t[:, :, None] == column, slot_of[None, None, :], 0), 2)
    candidates = 2 * modes
    index = jnp.arange(candidates, dtype=jnp.int32)
    before = index[None, None, :] < index[None, :, None]
    rank = jnp.sum(jnp.where(valid[:, None, :] & before, 1, 0), 2)
    place = jnp.arange(per_term, dtype=jnp.int32)
    chosen = (rank[:, None, :] == place[None, :, None]) & valid[:, None, :]
    entry_s = jnp.sum(jnp.where(chosen, slot_s[None, None, :], 0), 2)
    entry_t = jnp.sum(jnp.where(chosen, slot_t[:, None, :], 0), 2)
    entry_v = jnp.sum(jnp.where(chosen, value[:, None, :], 0.0), 2)
    return entry_s.reshape(-1), entry_t.reshape(-1), entry_v.reshape(-1), per_term


def inner(gathered, entries, terms, lay):
    entry_s, entry_t, entry_v, per_term = entries
    slots = lay.quota * lay.modes
    rows = lay.rows
    width = gathered.shape[2]
    full = (rows, width)

    def kernel(s_ref, t_ref, v_ref, g_ref, out_ref, near_ref):
        lane = lax.broadcasted_iota(jnp.int32, full, 1)
        line = lax.broadcasted_iota(jnp.int32, full, 0)

        def neighbours(p, block, i):
            at = block * lay.block
            here = g_ref[p, pl.ds(at + i * rows, rows), :]
            low = g_ref[p, pl.ds(at + lay.main + 2 * i, 1), :]
            high = g_ref[p, pl.ds(at + lay.main + 2 * i + 1, 1), :]
            right = pltpu.roll(here, width - 1, 1)
            left = pltpu.roll(here, 1, 1)
            above = jnp.where(line == rows - 1, high, pltpu.roll(here, rows - 1, 0))
            below = jnp.where(line == 0, low, pltpu.roll(here, 1, 0))
            return here, right, left, above, below

        for block in range(lay.modes):

            def spread(i, carry, block=block):
                for p in range(PLANES):
                    for n, value in enumerate(neighbours(p, block, i)):
                        near_ref[block * lay.quota + i, p, n] = value
                return carry

            lax.fori_loop(0, lay.quota, spread, 0)

        for term in range(terms):
            block, i = lay.coef(term)
            weights = []
            centres = []
            for p in range(PLANES):
                here, right, left, above, below = neighbours(p, block, i)
                right = jnp.where(lane == width - 1, 0.0, right)
                left = jnp.where(lane == 0, 0.0, left)
                faces = [0.5 * (here + n) for n in (right, left, above, below)]
                centres.append(here)
                diagonal = faces[0] + faces[1] + faces[2] + faces[3] + 0.5 * here
                faces[0] = jnp.where(lane == width - 1, 0.0, faces[0])
                faces[1] = jnp.where(lane == 0, 0.0, faces[1])
                weights.append([diagonal] + [-f for f in faces])
            between = 0.5 * (centres[0] + centres[1])
            for p in range(PLANES):
                weights[p][0] = weights[p][0] + between

            def operator(t, weights=weights, between=between):
                outs = []
                for p in range(PLANES):
                    total = weights[p][0] * near_ref[t, p, 0]
                    for n in range(1, 5):
                        total = total + weights[p][n] * near_ref[t, p, n]
                    outs.append(total - between * near_ref[t, 1 - p, 0])
                return outs

            if term == 0:

                def own(s, carry, operator=operator):
                    for p, total in enumerate(operator(s)):
                        out_ref[p, s] = total
                    return carry

                lax.fori_loop(0, slots, own, 0)
            else:

                def mix(e, carry, operator=operator):
                    s, t, v = s_ref[e], t_ref[e], v_ref[e]
                    for p, total in enumerate(operator(t)):
                        out_ref[p, s] += v * total
                    return carry

                lax.fori_loop((term - 1) * per_term, term * per_term, mix, 0)

    return pl.pallas_call(
        kernel,
        out_shape=jax.ShapeDtypeStruct((PLANES, slots, rows, width), jnp.float32),
        in_specs=smem(3) + vmem(1),
        out_specs=vmem(1)[0],
        scratch_shapes=[pltpu.VMEM((slots, PLANES, 5, rows, width), jnp.float32)],
        compiler_params=pltpu.CompilerParams(vmem_limit_bytes=VMEM_LIMIT),
        name="inner",
    )(entry_s, entry_t, entry_v, gathered)


def outer(gathered, below, above, partial, entries, terms, lay):
    entry_s, entry_t, entry_v, per_term = entries
    slots = lay.quota * lay.modes
    rows = lay.rows
    width = gathered.shape[2]
    quota = lay.quota

    def kernel(s_ref, t_ref, v_ref, g_ref, below_ref, above_ref, part_ref, out_ref):
        far_refs = (below_ref, above_ref)

        for term in range(terms):
            block, i = lay.coef(term)
            weights = []
            for p in range(PLANES):
                here = g_ref[p, pl.ds(block * lay.block + i * rows, rows), :]
                far = far_refs[p][pl.ds(block * lay.main + i * rows, rows), :]
                weights.append((0.5 * far, 0.5 * (here + far)))

            def operator(t, weights=weights):
                block = t // quota
                i = t - block * quota
                near_at = pl.multiple_of(block * lay.block + i * rows, 8)
                far_at = pl.multiple_of(block * lay.main + i * rows, 8)
                outs = []
                for p in range(PLANES):
                    here = g_ref[p, pl.ds(near_at, rows), :]
                    far = far_refs[p][pl.ds(far_at, rows), :]
                    outs.append(weights[p][0] * here - weights[p][1] * far)
                return outs

            if term == 0:

                def own(s, carry, operator=operator):
                    for p, total in enumerate(operator(s)):
                        out_ref[p, s] = part_ref[p, s] + total
                    return carry

                lax.fori_loop(0, slots, own, 0)
            else:

                def mix(e, carry, operator=operator):
                    s, t, v = s_ref[e], t_ref[e], v_ref[e]
                    for p, total in enumerate(operator(t)):
                        out_ref[p, s] += v * total
                    return carry

                lax.fori_loop((term - 1) * per_term, term * per_term, mix, 0)

    return pl.pallas_call(
        kernel,
        out_shape=jax.ShapeDtypeStruct((PLANES, slots, rows, width), jnp.float32),
        in_specs=smem(3) + vmem(4),
        out_specs=vmem(1)[0],
        compiler_params=pltpu.CompilerParams(vmem_limit_bytes=VMEM_LIMIT),
        name="outer",
    )(entry_s, entry_t, entry_v, gathered, below, above, partial)


def on_device(chaos_field, mean_field, kl_fields, pattern, coupling, slot_mode):
    spaces, modes = lax.axis_size("space"), lax.axis_size("mode")
    quota, _, height, width = chaos_field.shape
    terms = kl_fields.shape[0] + 1
    lay = Layout(quota, terms, modes, height)
    groups = [
        list(range(start, start + lay.group)) for start in range(0, spaces * modes, lay.group)
    ]

    def exchange(blocks):
        return lax.all_to_all(
            blocks, ("space", "mode"), 0, 0, axis_index_groups=groups, tiled=True
        )

    mode = lax.axis_index("mode").astype(jnp.int32).reshape(1)
    blocks = pack(chaos_field[:, 0], mean_field, kl_fields[:, 0], mode, lay)
    entries = coupling_entries(pattern, coupling, slot_mode, lay)
    gathered = exchange(blocks)

    main = gathered.reshape(PLANES, modes, lay.block, width)[:, :, : lay.main]
    main = main.reshape(PLANES, modes * lay.main, width)
    up = [(i, i + PLANES) for i in range(spaces - PLANES)]
    down = [(target, source) for source, target in up]
    below = lax.ppermute(main[PLANES - 1], "space", up)
    above = lax.ppermute(main[0], "space", down)

    planes = gathered.reshape(PLANES, modes * lay.block, width)
    partial = inner(planes, entries, terms, lay)
    total = outer(planes, below, above, partial, entries, terms, lay)

    back = exchange(total.reshape(lay.group, quota * lay.rows, width))
    back = back.reshape(lay.group, quota, lay.rows, width).transpose(1, 0, 2, 3)
    return back.reshape(chaos_field.shape)


def solution(mesh):
    in_specs = (
        P("mode", "space", None, None),
        P("space", None, None),
        P(None, "space", None, None),
        P(),
        P(),
        P(),
    )
    out_specs = P("mode", "space", None, None)
    return jax.shard_map(
        on_device, mesh=mesh, in_specs=in_specs, out_specs=out_specs, check_vma=False
    )
```

```python
import jax
import jax.numpy as jnp
from jax import lax
from jax.experimental import pallas as pl
from jax.experimental.pallas import tpu as pltpu
from jax.sharding import PartitionSpec as P

VMEM_LIMIT = 48 * 1024 * 1024
PLANES = 2
ACTIVE = 49
MOST = 8
UNROLL = 7


class Layout:
    def __init__(self, quota, terms, modes, height):
        self.modes = modes
        self.group = PLANES * modes
        self.rows = height // self.group
        self.quota = quota
        self.slots = quota * modes
        self.share = -(-terms // modes)
        self.fields = quota + self.share
        self.parts = self.fields + -(-2 * self.fields // self.rows)
        self.main = self.fields * self.rows
        self.block = self.parts * self.rows

    def coef(self, term):
        return term // self.share, self.quota + term % self.share

    def edge(self, i, side):
        at = 2 * i + side
        return self.fields + at // self.rows, at % self.rows


def vmem(count):
    return [pl.BlockSpec(memory_space=pltpu.VMEM)] * count


def smem(count):
    return [pl.BlockSpec(memory_space=pltpu.SMEM)] * count


def pack(field, mean, kl, mode, lay):
    kl_terms = kl.shape[0]
    width = field.shape[2]
    rows = lay.rows

    def kernel(mode_ref, field_ref, mean_ref, kl_ref, out_ref, mean_here, kl_here, sems):
        copies = [
            pltpu.make_async_copy(mean_ref, mean_here, sems.at[lay.group]),
            pltpu.make_async_copy(kl_ref, kl_here, sems.at[lay.group + 1]),
        ]
        for j in range(lay.group):
            copies.append(
                pltpu.make_async_copy(
                    field_ref.at[:, pl.ds(j * rows, rows), :],
                    out_ref.at[j, pl.ds(0, lay.quota)],
                    sems.at[j],
                )
            )
        for copy in copies:
            copy.start()
        copies[0].wait()
        copies[1].wait()
        for i in range(lay.share):
            term = mode_ref[0] * lay.share + i
            value = jnp.where(
                term == 0, mean_here[0], kl_here[jnp.clip(term - 1, 0, kl_terms - 1)]
            )
            for j in range(lay.group):
                out_ref[j, lay.quota + i] = value[j * rows : (j + 1) * rows]
        for copy in copies[2:]:
            copy.wait()
        none = jnp.zeros((1, width), jnp.float32)
        for j in range(lay.group):
            for i in range(lay.fields):
                low = out_ref[j - 1, i, rows - 1 :] if j > 0 else none
                high = out_ref[j + 1, i, :1] if j < lay.group - 1 else none
                for side, value in enumerate((low, high)):
                    part, line = lay.edge(i, side)
                    out_ref[j, part, line : line + 1] = value
            part, line = lay.edge(lay.fields, 0)
            if part < lay.parts:
                out_ref[j, part, line:] = jnp.zeros((rows - line, width), jnp.float32)

    return pl.pallas_call(
        kernel,
        out_shape=jax.ShapeDtypeStruct((lay.group, lay.parts, rows, width), jnp.float32),
        in_specs=smem(1) + [pl.BlockSpec(memory_space=pl.ANY)] * 3,
        out_specs=vmem(1)[0],
        scratch_shapes=[
            pltpu.VMEM(mean.shape, jnp.float32),
            pltpu.VMEM(kl.shape, jnp.float32),
            pltpu.SemaphoreType.DMA((lay.group + 2,)),
        ],
        compiler_params=pltpu.CompilerParams(vmem_limit_bytes=VMEM_LIMIT),
        name="pack",
    )(mode, field, mean, kl)


def coupling_lists(pattern, coupling, slot_mode):
    masked = (coupling * pattern.astype(jnp.float32))[1:]
    terms, modes = masked.shape[0], masked.shape[1]
    number = jnp.arange(modes, dtype=jnp.int32)
    one_hot = (slot_mode[:, None] == number[None, :]).astype(jnp.float32)
    coupled = jnp.einsum(
        "sa,kab,tb->kst", one_hot, masked, one_hot, precision=lax.Precision.HIGHEST
    )
    there = coupled != 0.0
    column = number[None, None, :]
    first = jnp.min(jnp.where(there, column, modes), 2)
    last = jnp.max(jnp.where(there, column, -1), 2)
    active = first < modes
    earlier = column < number[None, :, None]
    rank = jnp.sum(jnp.where(active[:, None, :] & earlier, 1, 0), 2)
    place = jnp.arange(ACTIVE, dtype=jnp.int32)[None, :, None]
    chosen = active[:, None, :] & (rank[:, None, :] == place)
    sources = jnp.sum(jnp.where(chosen, column, 0), 2)

    base = ACTIVE * jnp.arange(terms, dtype=jnp.int32)[:, None]
    products, factors, valid = [], [], []
    for chosen_t, is_valid in ((first, active), (last, last > first)):
        before = active[:, None, :] & (column < chosen_t[:, :, None])
        products.append(base + jnp.sum(jnp.where(before, 1, 0), 2))
        factors.append(jnp.sum(jnp.where(column == chosen_t[:, :, None], coupled, 0.0), 2))
        valid.append(is_valid)
    products = jnp.concatenate(products, 0)
    factors = jnp.concatenate(factors, 0)
    valid = jnp.concatenate(valid, 0)
    index = jnp.arange(2 * terms, dtype=jnp.int32)
    order = index[None, :] < index[:, None]
    rank = jnp.sum(jnp.where(valid[None] & order[:, :, None], 1, 0), 1)
    place = jnp.arange(MOST, dtype=jnp.int32)[:, None, None]
    chosen = valid[None] & (rank[None] == place)
    take = jnp.sum(jnp.where(chosen, products[None], 0), 1)
    factor = jnp.sum(jnp.where(chosen, factors[None], 0.0), 1)
    return sources.reshape(-1), take.T.reshape(-1), factor.T.reshape(-1)


def gather_products(s, take_ref, factor_ref, product_ref, p, total):
    for n in range(MOST):
        e = s * MOST + n
        total = total + factor_ref[e] * product_ref[take_ref[e], p]
    return total


def inner(gathered, lists, terms, lay):
    rows = lay.rows
    width = gathered.shape[2]
    full = (rows, width)

    def kernel(source_ref, take_ref, factor_ref, g_ref, out_ref, near_ref, product_ref):
        lane = lax.broadcasted_iota(jnp.int32, full, 1)
        line = lax.broadcasted_iota(jnp.int32, full, 0)

        def neighbours(p, block, i):
            at = block * lay.block
            here = g_ref[p, pl.ds(at + i * rows, rows), :]
            low = g_ref[p, pl.ds(at + lay.main + 2 * i, 1), :]
            high = g_ref[p, pl.ds(at + lay.main + 2 * i + 1, 1), :]
            right = pltpu.roll(here, width - 1, 1)
            left = pltpu.roll(here, 1, 1)
            above = jnp.where(line == rows - 1, high, pltpu.roll(here, rows - 1, 0))
            below = jnp.where(line == 0, low, pltpu.roll(here, 1, 0))
            return here, right, left, above, below

        for block in range(lay.modes):

            def spread(i, carry, block=block):
                for p in range(PLANES):
                    for n, value in enumerate(neighbours(p, block, i)):
                        near_ref[block * lay.quota + i, p, n] = value
                return carry

            lax.fori_loop(0, lay.quota, spread, 0, unroll=UNROLL)

        def operator_of(term):
            block, i = lay.coef(term)
            weights = []
            centres = []
            for p in range(PLANES):
                here, right, left, above, below = neighbours(p, block, i)
                right = jnp.where(lane == width - 1, 0.0, right)
                left = jnp.where(lane == 0, 0.0, left)
                faces = [0.5 * (here + n) for n in (right, left, above, below)]
                centres.append(here)
                diagonal = faces[0] + faces[1] + faces[2] + faces[3] + 0.5 * here
                faces[0] = jnp.where(lane == width - 1, 0.0, faces[0])
                faces[1] = jnp.where(lane == 0, 0.0, faces[1])
                weights.append([diagonal] + [-f for f in faces])
            between = 0.5 * (centres[0] + centres[1])
            for p in range(PLANES):
                weights[p][0] = weights[p][0] + between

            def operator(t, p):
                total = weights[p][0] * near_ref[t, p, 0]
                for n in range(1, 5):
                    total = total + weights[p][n] * near_ref[t, p, n]
                return total - between * near_ref[t, 1 - p, 0]

            return operator

        for term in range(1, terms):
            operator = operator_of(term)

            def apply(n, carry, operator=operator, term=term):
                e = (term - 1) * ACTIVE + n
                t = source_ref[e]
                for p in range(PLANES):
                    product_ref[e, p] = operator(t, p)
                return carry

            lax.fori_loop(0, ACTIVE, apply, 0, unroll=UNROLL)

        operator = operator_of(0)

        def collect(s, carry):
            for p in range(PLANES):
                out_ref[p, s] = gather_products(
                    s, take_ref, factor_ref, product_ref, p, operator(s, p)
                )
            return carry

        lax.fori_loop(0, lay.slots, collect, 0, unroll=UNROLL)

    return pl.pallas_call(
        kernel,
        out_shape=jax.ShapeDtypeStruct((PLANES, lay.slots, rows, width), jnp.float32),
        in_specs=smem(3) + vmem(1),
        out_specs=vmem(1)[0],
        scratch_shapes=[
            pltpu.VMEM((lay.slots, PLANES, 5, rows, width), jnp.float32),
            pltpu.VMEM(((terms - 1) * ACTIVE, PLANES, rows, width), jnp.float32),
        ],
        compiler_params=pltpu.CompilerParams(vmem_limit_bytes=VMEM_LIMIT),
        name="inner",
    )(*lists, gathered)


def outer(gathered, below, above, partial, lists, terms, lay):
    rows = lay.rows
    width = gathered.shape[2]

    def kernel(
        source_ref, take_ref, factor_ref, g_ref, below_ref, above_ref, part_ref, out_ref, product_ref
    ):
        far_refs = (below_ref, above_ref)

        def operator_of(term):
            block, i = lay.coef(term)
            weights = []
            for p in range(PLANES):
                here = g_ref[p, pl.ds(block * lay.block + i * rows, rows), :]
                far = far_refs[p][pl.ds(block * lay.main + i * rows, rows), :]
                weights.append((0.5 * far, 0.5 * (here + far)))

            def operator(t, p):
                block = t // lay.quota
                i = t - block * lay.quota
                near_at = pl.multiple_of(block * lay.block + i * rows, 8)
                far_at = pl.multiple_of(block * lay.main + i * rows, 8)
                here = g_ref[p, pl.ds(near_at, rows), :]
                far = far_refs[p][pl.ds(far_at, rows), :]
                return weights[p][0] * here - weights[p][1] * far

            return operator

        for term in range(1, terms):
            operator = operator_of(term)

            def apply(n, carry, operator=operator, term=term):
                e = (term - 1) * ACTIVE + n
                t = source_ref[e]
                for p in range(PLANES):
                    product_ref[e, p] = operator(t, p)
                return carry

            lax.fori_loop(0, ACTIVE, apply, 0, unroll=UNROLL)

        operator = operator_of(0)

        def collect(s, carry):
            for p in range(PLANES):
                out_ref[p, s] = gather_products(
                    s, take_ref, factor_ref, product_ref, p, part_ref[p, s] + operator(s, p)
                )
            return carry

        lax.fori_loop(0, lay.slots, collect, 0, unroll=UNROLL)

    return pl.pallas_call(
        kernel,
        out_shape=jax.ShapeDtypeStruct((PLANES, lay.slots, rows, width), jnp.float32),
        in_specs=smem(3) + vmem(4),
        out_specs=vmem(1)[0],
        scratch_shapes=[pltpu.VMEM(((terms - 1) * ACTIVE, PLANES, rows, width), jnp.float32)],
        compiler_params=pltpu.CompilerParams(vmem_limit_bytes=VMEM_LIMIT),
        name="outer",
    )(*lists, gathered, below, above, partial)


def on_device(chaos_field, mean_field, kl_fields, pattern, coupling, slot_mode):
    spaces, modes = lax.axis_size("space"), lax.axis_size("mode")
    quota, _, height, width = chaos_field.shape
    terms = kl_fields.shape[0] + 1
    lay = Layout(quota, terms, modes, height)
    groups = [
        list(range(start, start + lay.group)) for start in range(0, spaces * modes, lay.group)
    ]

    def exchange(blocks):
        return lax.all_to_all(
            blocks, ("space", "mode"), 0, 0, axis_index_groups=groups, tiled=True
        )

    mode = lax.axis_index("mode").astype(jnp.int32).reshape(1)
    blocks = pack(chaos_field[:, 0], mean_field, kl_fields[:, 0], mode, lay)
    lists = coupling_lists(pattern, coupling, slot_mode)
    gathered = exchange(blocks.reshape(lay.group, lay.block, width))

    main = gathered.reshape(PLANES, modes, lay.block, width)[:, :, : lay.main]
    main = main.reshape(PLANES, modes * lay.main, width)
    up = [(i, i + PLANES) for i in range(spaces - PLANES)]
    down = [(target, source) for source, target in up]
    below = lax.ppermute(main[PLANES - 1], "space", up)
    above = lax.ppermute(main[0], "space", down)

    planes = gathered.reshape(PLANES, modes * lay.block, width)
    partial = inner(planes, lists, terms, lay)
    total = outer(planes, below, above, partial, lists, terms, lay)

    back = exchange(total.reshape(lay.group, quota * lay.rows, width))
    back = back.reshape(lay.group, quota, lay.rows, width).transpose(1, 0, 2, 3)
    return back.reshape(chaos_field.shape)


def solution(mesh):
    in_specs = (
        P("mode", "space", None, None),
        P("space", None, None),
        P(None, "space", None, None),
        P(),
        P(),
        P(),
    )
    out_specs = P("mode", "space", None, None)
    return jax.shard_map(
        on_device, mesh=mesh, in_specs=in_specs, out_specs=out_specs, check_vma=False
    )
```

```python
import jax
import jax.numpy as jnp
from jax import lax
from jax.experimental import pallas as pl
from jax.experimental.pallas import tpu as pltpu
from jax.sharding import PartitionSpec as P

VMEM_LIMIT = 48 * 1024 * 1024
PLANES = 2
ACTIVE = 49
MOST = 8
CHUNKS = 2
UNROLL = 7


class Layout:
    def __init__(self, quota, terms, modes, height):
        self.modes = modes
        self.group = PLANES * modes
        self.rows = height // (CHUNKS * self.group)
        self.quota = quota
        self.slots = quota * modes
        self.share = -(-terms // modes)
        self.fields = quota + self.share
        self.parts = self.fields + -(-2 * self.fields // self.rows)
        self.main = self.fields * self.rows
        self.block = self.parts * self.rows

    def coef(self, term):
        return term // self.share, self.quota + term % self.share

    def edge(self, i, side):
        at = 2 * i + side
        return self.fields + at // self.rows, at % self.rows


def vmem(count):
    return [pl.BlockSpec(memory_space=pltpu.VMEM)] * count


def smem(count):
    return [pl.BlockSpec(memory_space=pltpu.SMEM)] * count


def pack(field, mean, kl, mode, chunk, lay):
    kl_terms = kl.shape[0]
    height, width = field.shape[1:]
    rows = lay.rows
    start = chunk * lay.group * rows
    end = start + lay.group * rows
    before, after = start > 0, end < height

    def kernel(mode_ref, field_ref, mean_ref, kl_ref, out_ref, mean_here, kl_here, low_here, high_here, sems):
        def copy(source, target, n):
            made = pltpu.make_async_copy(source, target, sems.at[n])
            made.start()
            return made

        coefs = [copy(mean_ref, mean_here, lay.group), copy(kl_ref, kl_here, lay.group + 1)]
        fields = [
            copy(
                field_ref.at[:, pl.ds(start + j * rows, rows), :],
                out_ref.at[j, pl.ds(0, lay.quota)],
                j,
            )
            for j in range(lay.group)
        ]
        if before:
            fields.append(copy(field_ref.at[:, pl.ds(start - 8, 8), :], low_here, lay.group + 2))
        if after:
            fields.append(copy(field_ref.at[:, pl.ds(end, 8), :], high_here, lay.group + 3))
        for made in coefs:
            made.wait()
        values = []
        for i in range(lay.share):
            term = mode_ref[0] * lay.share + i
            value = jnp.where(
                term == 0, mean_here[0], kl_here[jnp.clip(term - 1, 0, kl_terms - 1)]
            )
            values.append(value)
            for j in range(lay.group):
                out_ref[j, lay.quota + i] = value[start + j * rows : start + (j + 1) * rows]
        for made in fields:
            made.wait()
        none = jnp.zeros((1, width), jnp.float32)
        for j in range(lay.group):
            for i in range(lay.fields):
                own = i < lay.quota
                low, high = none, none
                if j > 0:
                    low = out_ref[j - 1, i, rows - 1 :]
                elif before:
                    low = low_here[i, 7:] if own else values[i - lay.quota][start - 1 : start]
                if j < lay.group - 1:
                    high = out_ref[j + 1, i, :1]
                elif after:
                    high = high_here[i, :1] if own else values[i - lay.quota][end : end + 1]
                for side, value in enumerate((low, high)):
                    part, line = lay.edge(i, side)
                    out_ref[j, part, line : line + 1] = value
            part, line = lay.edge(lay.fields, 0)
            if part < lay.parts:
                out_ref[j, part, line:] = jnp.zeros((rows - line, width), jnp.float32)

    return pl.pallas_call(
        kernel,
        out_shape=jax.ShapeDtypeStruct((lay.group, lay.parts, rows, width), jnp.float32),
        in_specs=smem(1) + [pl.BlockSpec(memory_space=pltpu.HBM)] * 3,
        out_specs=vmem(1)[0],
        scratch_shapes=[
            pltpu.VMEM(mean.shape, jnp.float32),
            pltpu.VMEM(kl.shape, jnp.float32),
            pltpu.VMEM((lay.quota, 8, width), jnp.float32),
            pltpu.VMEM((lay.quota, 8, width), jnp.float32),
            pltpu.SemaphoreType.DMA((lay.group + 4,)),
        ],
        compiler_params=pltpu.CompilerParams(vmem_limit_bytes=VMEM_LIMIT),
        name="pack",
    )(mode, field, mean, kl)


def unpack(parts, shape, lay):
    rows = lay.rows

    def kernel(*refs):
        part_refs, out_ref, sems = refs[:-2], refs[-2], refs[-1]
        copies = []
        for c, part_ref in enumerate(part_refs):
            for j in range(lay.group):
                n = c * lay.group + j
                made = pltpu.make_async_copy(
                    part_ref.at[j], out_ref.at[:, pl.ds(n * rows, rows), :], sems.at[n]
                )
                made.start()
                copies.append(made)
        for made in copies:
            made.wait()

    return pl.pallas_call(
        kernel,
        out_shape=jax.ShapeDtypeStruct(shape, jnp.float32),
        in_specs=[pl.BlockSpec(memory_space=pl.ANY)] * len(parts),
        out_specs=pl.BlockSpec(memory_space=pl.ANY),
        scratch_shapes=[pltpu.SemaphoreType.DMA((CHUNKS * lay.group,))],
        name="unpack",
    )(*parts)


def coupling_lists(pattern, coupling, slot_mode, lay):
    masked = (coupling * pattern.astype(jnp.float32))[1:]
    terms, modes = masked.shape[0], masked.shape[1]
    number = jnp.arange(modes, dtype=jnp.int32)
    one_hot = (slot_mode[:, None] == number[None, :]).astype(jnp.float32)
    coupled = jnp.einsum(
        "sa,kab,tb->kst", one_hot, masked, one_hot, precision=lax.Precision.HIGHEST
    )
    there = coupled != 0.0
    column = number[None, None, :]
    first = jnp.min(jnp.where(there, column, modes), 2)
    last = jnp.max(jnp.where(there, column, -1), 2)
    active = first < modes
    earlier = column < number[None, :, None]
    rank = jnp.sum(jnp.where(active[:, None, :] & earlier, 1, 0), 2)
    place = jnp.arange(ACTIVE, dtype=jnp.int32)[None, :, None]
    chosen = active[:, None, :] & (rank[:, None, :] == place)
    sources = jnp.sum(jnp.where(chosen, column, 0), 2)

    base = ACTIVE * jnp.arange(terms, dtype=jnp.int32)[:, None]
    products, factors, valid = [], [], []
    for chosen_t, is_valid in ((first, active), (last, last > first)):
        before = active[:, None, :] & (column < chosen_t[:, :, None])
        products.append(base + jnp.sum(jnp.where(before, 1, 0), 2))
        factors.append(jnp.sum(jnp.where(column == chosen_t[:, :, None], coupled, 0.0), 2))
        valid.append(is_valid)
    products = jnp.concatenate(products, 0)
    factors = jnp.concatenate(factors, 0)
    valid = jnp.concatenate(valid, 0)
    index = jnp.arange(2 * terms, dtype=jnp.int32)
    order = index[None, :] < index[:, None]
    rank = jnp.sum(jnp.where(valid[None] & order[:, :, None], 1, 0), 1)
    place = jnp.arange(MOST, dtype=jnp.int32)[:, None, None]
    chosen = valid[None] & (rank[None] == place)
    take = jnp.sum(jnp.where(chosen, products[None], 0), 1)
    factor = jnp.sum(jnp.where(chosen, factors[None], 0.0), 1)
    sources = sources.reshape(-1)
    block = jnp.zeros_like(sources)
    for n in range(1, lay.modes):
        block = block + jnp.where(sources >= n * lay.quota, 1, 0)
    far = sources * lay.rows + block * (lay.main - lay.quota * lay.rows)
    near = far + block * (lay.block - lay.main)
    return sources, near, far, take.T.reshape(-1), factor.T.reshape(-1)


def gather_products(s, take_ref, factor_ref, product_ref, p, total):
    for n in range(MOST):
        e = s * MOST + n
        total = total + factor_ref[e] * product_ref[take_ref[e], p]
    return total


def inner(gathered, lists, terms, lay):
    rows = lay.rows
    width = gathered.shape[2]
    full = (rows, width)

    def kernel(source_ref, take_ref, factor_ref, g_ref, out_ref, near_ref, product_ref):
        lane = lax.broadcasted_iota(jnp.int32, full, 1)
        line = lax.broadcasted_iota(jnp.int32, full, 0)

        def neighbours(p, block, i):
            at = block * lay.block
            here = g_ref[p, pl.ds(at + i * rows, rows), :]
            low = g_ref[p, pl.ds(at + lay.main + 2 * i, 1), :]
            high = g_ref[p, pl.ds(at + lay.main + 2 * i + 1, 1), :]
            right = pltpu.roll(here, width - 1, 1)
            left = pltpu.roll(here, 1, 1)
            above = jnp.where(line == rows - 1, high, pltpu.roll(here, rows - 1, 0))
            below = jnp.where(line == 0, low, pltpu.roll(here, 1, 0))
            return here, right, left, above, below

        for block in range(lay.modes):

            def spread(i, carry, block=block):
                for p in range(PLANES):
                    for n, value in enumerate(neighbours(p, block, i)):
                        near_ref[block * lay.quota + i, p, n] = value
                return carry

            lax.fori_loop(0, lay.quota, spread, 0, unroll=UNROLL)

        def operator_of(term):
            block, i = lay.coef(term)
            weights = []
            centres = []
            for p in range(PLANES):
                here, right, left, above, below = neighbours(p, block, i)
                right = jnp.where(lane == width - 1, 0.0, right)
                left = jnp.where(lane == 0, 0.0, left)
                faces = [0.5 * (here + n) for n in (right, left, above, below)]
                centres.append(here)
                diagonal = faces[0] + faces[1] + faces[2] + faces[3] + 0.5 * here
                faces[0] = jnp.where(lane == width - 1, 0.0, faces[0])
                faces[1] = jnp.where(lane == 0, 0.0, faces[1])
                weights.append([diagonal] + [-f for f in faces])
            between = 0.5 * (centres[0] + centres[1])
            for p in range(PLANES):
                weights[p][0] = weights[p][0] + between

            def operator(t, p):
                total = weights[p][0] * near_ref[t, p, 0]
                for n in range(1, 5):
                    total = total + weights[p][n] * near_ref[t, p, n]
                return total - between * near_ref[t, 1 - p, 0]

            return operator

        for term in range(1, terms):
            operator = operator_of(term)

            def apply(n, carry, operator=operator, term=term):
                e = (term - 1) * ACTIVE + n
                t = source_ref[e]
                for p in range(PLANES):
                    product_ref[e, p] = operator(t, p)
                return carry

            lax.fori_loop(0, ACTIVE, apply, 0, unroll=UNROLL)

        operator = operator_of(0)

        def collect(s, carry):
            for p in range(PLANES):
                out_ref[p, s] = gather_products(
                    s, take_ref, factor_ref, product_ref, p, operator(s, p)
                )
            return carry

        lax.fori_loop(0, lay.slots, collect, 0, unroll=UNROLL)

    return pl.pallas_call(
        kernel,
        out_shape=jax.ShapeDtypeStruct((PLANES, lay.slots, rows, width), jnp.float32),
        in_specs=smem(3) + vmem(1),
        out_specs=vmem(1)[0],
        scratch_shapes=[
            pltpu.VMEM((lay.slots, PLANES, 5, rows, width), jnp.float32),
            pltpu.VMEM(((terms - 1) * ACTIVE, PLANES, rows, width), jnp.float32),
        ],
        compiler_params=pltpu.CompilerParams(vmem_limit_bytes=VMEM_LIMIT),
        name="inner",
    )(lists[0], *lists[3:], gathered)


def outer(gathered, below, above, partial, lists, terms, lay):
    rows = lay.rows
    width = gathered.shape[2]

    def kernel(
        near_ref, far_ref, take_ref, factor_ref, g_ref, below_ref, above_ref, part_ref, out_ref, product_ref
    ):
        other_refs = (below_ref, above_ref)

        def operator_of(term):
            block, i = lay.coef(term)
            weights = []
            for p in range(PLANES):
                here = g_ref[p, pl.ds(block * lay.block + i * rows, rows), :]
                other = other_refs[p][pl.ds(block * lay.main + i * rows, rows), :]
                weights.append((0.5 * other, 0.5 * (here + other)))

            def operator(near, far, p):
                here = g_ref[p, pl.ds(pl.multiple_of(near, 8), rows), :]
                other = other_refs[p][pl.ds(pl.multiple_of(far, 8), rows), :]
                return weights[p][0] * here - weights[p][1] * other

            return operator

        for term in range(1, terms):
            operator = operator_of(term)

            def apply(n, carry, operator=operator, term=term):
                e = (term - 1) * ACTIVE + n
                near, far = near_ref[e], far_ref[e]
                for p in range(PLANES):
                    product_ref[e, p] = operator(near, far, p)
                return carry

            lax.fori_loop(0, ACTIVE, apply, 0, unroll=UNROLL)

        operator = operator_of(0)
        for block in range(lay.modes):

            def collect(i, carry, block=block):
                s = block * lay.quota + i
                near = block * lay.block + i * rows
                far = block * lay.main + i * rows
                for p in range(PLANES):
                    total = part_ref[p, s] + operator(near, far, p)
                    out_ref[p, s] = gather_products(s, take_ref, factor_ref, product_ref, p, total)
                return carry

            lax.fori_loop(0, lay.quota, collect, 0, unroll=UNROLL)

    return pl.pallas_call(
        kernel,
        out_shape=jax.ShapeDtypeStruct((PLANES, lay.slots, rows, width), jnp.float32),
        in_specs=smem(4) + vmem(4),
        out_specs=vmem(1)[0],
        scratch_shapes=[pltpu.VMEM(((terms - 1) * ACTIVE, PLANES, rows, width), jnp.float32)],
        compiler_params=pltpu.CompilerParams(vmem_limit_bytes=VMEM_LIMIT),
        name="outer",
    )(*lists[1:], gathered, below, above, partial)


def on_device(chaos_field, mean_field, kl_fields, pattern, coupling, slot_mode):
    spaces, modes = lax.axis_size("space"), lax.axis_size("mode")
    quota, _, height, width = chaos_field.shape
    terms = kl_fields.shape[0] + 1
    lay = Layout(quota, terms, modes, height)
    groups = [
        list(range(start, start + lay.group)) for start in range(0, spaces * modes, lay.group)
    ]

    def exchange(blocks):
        return lax.all_to_all(
            blocks, ("space", "mode"), 0, 0, axis_index_groups=groups, tiled=True
        )

    mode = lax.axis_index("mode").astype(jnp.int32).reshape(1)
    up = [(i, i + PLANES) for i in range(spaces - PLANES)]
    down = [(target, source) for source, target in up]
    field, kl = chaos_field[:, 0], kl_fields[:, 0]

    gathered = []
    for chunk in range(CHUNKS):
        blocks = pack(field, mean_field, kl, mode, chunk, lay)
        gathered.append(exchange(blocks.reshape(lay.group, lay.block, width)))
    lists = coupling_lists(pattern, coupling, slot_mode, lay)
    parts = []
    for chunk in range(CHUNKS):
        main = gathered[chunk].reshape(PLANES, modes, lay.block, width)[:, :, : lay.main]
        main = main.reshape(PLANES, modes * lay.main, width)
        below = lax.ppermute(main[PLANES - 1], "space", up)
        above = lax.ppermute(main[0], "space", down)
        planes = gathered[chunk].reshape(PLANES, modes * lay.block, width)
        partial = inner(planes, lists, terms, lay)
        total = outer(planes, below, above, partial, lists, terms, lay)
        back = exchange(total.reshape(lay.group, quota * lay.rows, width))
        parts.append(back.reshape(lay.group, quota, lay.rows, width))
    return unpack(parts, field.shape, lay).reshape(chaos_field.shape)


def solution(mesh):
    in_specs = (
        P("mode", "space", None, None),
        P("space", None, None),
        P(None, "space", None, None),
        P(),
        P(),
        P(),
    )
    out_specs = P("mode", "space", None, None)
    return jax.shard_map(
        on_device, mesh=mesh, in_specs=in_specs, out_specs=out_specs, check_vma=False
    )
```

```python
import jax
import jax.numpy as jnp
from jax import lax
from jax.experimental import pallas as pl
from jax.experimental.pallas import tpu as pltpu
from jax.sharding import PartitionSpec as P

VMEM_LIMIT = 40 * 1024 * 1024
PACK_LIMIT = 60 * 1024 * 1024
PLANES = 2
ACTIVE = 49
MOST = 8
UNROLL = 7


class Layout:
    def __init__(self, quota, terms, modes, height, width):
        self.modes = modes
        self.group = PLANES * modes
        self.rows = height // self.group
        self.width = width
        self.terms = terms
        self.quota = quota
        self.slots = quota * modes
        self.share = -(-terms // modes)
        self.fields = quota + self.share
        self.main = self.fields * self.rows
        edges = -(-2 * self.fields // 8) * 8
        self.piece = self.main + edges
        self.places = self.fields * modes

    def origin(self, j, r):
        other = jnp.bitwise_xor(j, r)
        plane = other // self.modes
        return plane, other - plane * self.modes

    def place(self, block, i):
        return jnp.where(
            i < self.quota,
            block * self.quota + i,
            self.slots + block * self.share + (i - self.quota),
        )


def vmem(count):
    return [pl.BlockSpec(memory_space=pltpu.VMEM)] * count


def smem(count):
    return [pl.BlockSpec(memory_space=pltpu.SMEM)] * count


def pack(field, mean, kl, j, lay):
    kl_terms = kl.shape[0]
    rows, width = lay.rows, lay.width
    height = field.shape[1]

    def kernel(j_ref, field_ref, mean_ref, kl_ref, *refs):
        out_refs, (stage_ref, mean_here, kl_here, sems) = refs[: lay.group], refs[lay.group :]
        copies = [
            pltpu.make_async_copy(field_ref, stage_ref.at[pl.ds(0, lay.quota)], sems.at[0]),
            pltpu.make_async_copy(mean_ref, mean_here, sems.at[1]),
            pltpu.make_async_copy(kl_ref, kl_here, sems.at[2]),
        ]
        for made in copies:
            made.start()
        me = j_ref[0]
        mode = lax.rem(me, lay.modes)
        copies[1].wait()
        copies[2].wait()
        for i in range(lay.share):
            term = mode * lay.share + i
            other = kl_here[jnp.clip(term - 1, 0, kl_terms - 1)]
            stage_ref[lay.quota + i] = jnp.where(term == 0, mean_here[0], other)
        copies[0].wait()
        for r in range(lay.group):
            other = jnp.bitwise_xor(me, r)
            start = pl.multiple_of(other * rows, 8)
            lower = jnp.maximum(start - 1, 0)
            upper = jnp.minimum(start + rows, height - 1)
            for i in range(lay.fields):
                out_refs[r][i * rows : (i + 1) * rows, :] = stage_ref[i, pl.ds(start, rows), :]
                low = stage_ref[i, pl.ds(lower, 1), :]
                high = stage_ref[i, pl.ds(upper, 1), :]
                at = lay.main + 2 * i
                out_refs[r][at : at + 1, :] = jnp.where(other == 0, 0.0, low)
                out_refs[r][at + 1 : at + 2, :] = jnp.where(other == lay.group - 1, 0.0, high)
            spare = lay.piece - lay.main - 2 * lay.fields
            if spare:
                out_refs[r][lay.piece - spare :, :] = jnp.zeros((spare, width), jnp.float32)

    return pl.pallas_call(
        kernel,
        out_shape=[jax.ShapeDtypeStruct((lay.piece, width), jnp.float32)] * lay.group,
        in_specs=smem(1) + [pl.BlockSpec(memory_space=pltpu.HBM)] * 3,
        out_specs=vmem(lay.group),
        scratch_shapes=[
            pltpu.VMEM((lay.fields, height, width), jnp.float32),
            pltpu.VMEM(mean.shape, jnp.float32),
            pltpu.VMEM(kl.shape, jnp.float32),
            pltpu.SemaphoreType.DMA((3,)),
        ],
        compiler_params=pltpu.CompilerParams(vmem_limit_bytes=PACK_LIMIT),
        name="pack",
    )(j, field, mean, kl)


def unpack(pieces, j, shape, lay):
    rows = lay.rows

    def kernel(j_ref, *refs):
        piece_refs, out_ref, sems = refs[:-2], refs[-2], refs[-1]
        copies = []
        for r, piece_ref in enumerate(piece_refs):
            start = pl.multiple_of(jnp.bitwise_xor(j_ref[0], r) * rows, 8)
            made = pltpu.make_async_copy(
                piece_ref, out_ref.at[:, pl.ds(start, rows), :], sems.at[r]
            )
            made.start()
            copies.append(made)
        for made in copies:
            made.wait()

    return pl.pallas_call(
        kernel,
        out_shape=jax.ShapeDtypeStruct(shape, jnp.float32),
        in_specs=smem(1) + vmem(lay.group),
        out_specs=pl.BlockSpec(memory_space=pltpu.HBM),
        scratch_shapes=[pltpu.SemaphoreType.DMA((lay.group,))],
        compiler_params=pltpu.CompilerParams(vmem_limit_bytes=VMEM_LIMIT),
        name="unpack",
    )(j, *pieces)


def coupling_lists(pattern, coupling, slot_mode):
    masked = (coupling * pattern.astype(jnp.float32))[1:]
    terms, modes = masked.shape[0], masked.shape[1]
    number = jnp.arange(modes, dtype=jnp.int32)
    one_hot = (slot_mode[:, None] == number[None, :]).astype(jnp.float32)
    coupled = jnp.einsum(
        "sa,kab,tb->kst", one_hot, masked, one_hot, precision=lax.Precision.HIGHEST
    )
    there = coupled != 0.0
    column = number[None, None, :]
    first = jnp.min(jnp.where(there, column, modes), 2)
    last = jnp.max(jnp.where(there, column, -1), 2)
    active = first < modes
    earlier = column < number[None, :, None]
    rank = jnp.sum(jnp.where(active[:, None, :] & earlier, 1, 0), 2)
    place = jnp.arange(ACTIVE, dtype=jnp.int32)[None, :, None]
    chosen = active[:, None, :] & (rank[:, None, :] == place)
    sources = jnp.sum(jnp.where(chosen, column, 0), 2)

    base = ACTIVE * jnp.arange(terms, dtype=jnp.int32)[:, None]
    products, factors, valid = [], [], []
    for chosen_t, is_valid in ((first, active), (last, last > first)):
        before = active[:, None, :] & (column < chosen_t[:, :, None])
        products.append(base + jnp.sum(jnp.where(before, 1, 0), 2))
        factors.append(jnp.sum(jnp.where(column == chosen_t[:, :, None], coupled, 0.0), 2))
        valid.append(is_valid)
    products = jnp.concatenate(products, 0)
    factors = jnp.concatenate(factors, 0)
    valid = jnp.concatenate(valid, 0)
    index = jnp.arange(2 * terms, dtype=jnp.int32)
    order = index[None, :] < index[:, None]
    rank = jnp.sum(jnp.where(valid[None] & order[:, :, None], 1, 0), 1)
    place = jnp.arange(MOST, dtype=jnp.int32)[:, None, None]
    chosen = valid[None] & (rank[None] == place)
    take = jnp.sum(jnp.where(chosen, products[None], 0), 1)
    factor = jnp.sum(jnp.where(chosen, factors[None], 0.0), 1)
    return sources.reshape(-1), take.T.reshape(-1), factor.T.reshape(-1)


def gather_products(s, take_ref, factor_ref, product_ref, where, total):
    for n in range(MOST):
        e = s * MOST + n
        total = total + factor_ref[e] * product_ref[(take_ref[e], *where)]
    return total


def inner(pieces, lists, j, lay):
    rows, width = lay.rows, lay.width
    full = (rows, width)

    def kernel(j_ref, source_ref, take_ref, factor_ref, *refs):
        piece_refs, (out_ref, centre_ref, near_ref, product_ref) = refs[: lay.group], refs[lay.group :]
        lane = lax.broadcasted_iota(jnp.int32, full, 1)
        line = lax.broadcasted_iota(jnp.int32, full, 0)

        for r in range(lay.group):
            plane, block = lay.origin(j_ref[0], r)

            def spread(i, carry, piece_ref=piece_refs[r], plane=plane, block=block):
                here = piece_ref[pl.ds(i * rows, rows), :]
                low = piece_ref[pl.ds(lay.main + 2 * i, 1), :]
                high = piece_ref[pl.ds(lay.main + 2 * i + 1, 1), :]
                at = lay.place(block, i)
                centre_ref[at, plane] = here
                near_ref[at, plane, 0] = pltpu.roll(here, width - 1, 1)
                near_ref[at, plane, 1] = pltpu.roll(here, 1, 1)
                near_ref[at, plane, 2] = jnp.where(
                    line == rows - 1, high, pltpu.roll(here, rows - 1, 0)
                )
                near_ref[at, plane, 3] = jnp.where(line == 0, low, pltpu.roll(here, 1, 0))
                return carry

            lax.fori_loop(0, lay.fields, spread, 0, unroll=UNROLL)

        def operator_of(term):
            at = lay.slots + term
            weights = []
            centres = []
            for p in range(PLANES):
                here = centre_ref[at, p]
                beside = [near_ref[at, p, n] for n in range(4)]
                beside[0] = jnp.where(lane == width - 1, 0.0, beside[0])
                beside[1] = jnp.where(lane == 0, 0.0, beside[1])
                faces = [0.5 * (here + n) for n in beside]
                centres.append(here)
                diagonal = faces[0] + faces[1] + faces[2] + faces[3] + 0.5 * here
                faces[0] = jnp.where(lane == width - 1, 0.0, faces[0])
                faces[1] = jnp.where(lane == 0, 0.0, faces[1])
                weights.append([diagonal] + [-f for f in faces])
            between = 0.5 * (centres[0] + centres[1])
            for p in range(PLANES):
                weights[p][0] = weights[p][0] + between

            def operator(t, p):
                total = weights[p][0] * centre_ref[t, p]
                for n in range(4):
                    total = total + weights[p][n + 1] * near_ref[t, p, n]
                return total - between * centre_ref[t, 1 - p]

            return operator

        for term in range(1, lay.terms):
            operator = operator_of(term)

            def apply(n, carry, operator=operator, term=term):
                e = (term - 1) * ACTIVE + n
                t = source_ref[e]
                for p in range(PLANES):
                    product_ref[e, p] = operator(t, p)
                return carry

            lax.fori_loop(0, ACTIVE, apply, 0, unroll=UNROLL)

        operator = operator_of(0)

        def collect(s, carry):
            for p in range(PLANES):
                out_ref[s, p] = gather_products(
                    s, take_ref, factor_ref, product_ref, (p,), operator(s, p)
                )
            return carry

        lax.fori_loop(0, lay.slots, collect, 0, unroll=UNROLL)

    return pl.pallas_call(
        kernel,
        out_shape=[
            jax.ShapeDtypeStruct((lay.slots, PLANES, rows, width), jnp.float32),
            jax.ShapeDtypeStruct((lay.places, PLANES, rows, width), jnp.float32),
        ],
        in_specs=smem(4) + vmem(lay.group),
        out_specs=vmem(2),
        scratch_shapes=[
            pltpu.VMEM((lay.places, PLANES, 4, rows, width), jnp.float32),
            pltpu.VMEM(((lay.terms - 1) * ACTIVE, PLANES, rows, width), jnp.float32),
        ],
        compiler_params=pltpu.CompilerParams(vmem_limit_bytes=VMEM_LIMIT),
        name="inner",
    )(j, *lists, *pieces)


def outer(centre, partial, halos, lists, j, crossing, lay):
    rows, width = lay.rows, lay.width
    first = lay.modes if crossing else 0

    def kernel(j_ref, source_ref, take_ref, factor_ref, centre_ref, part_ref, *refs):
        halo_refs, refs = refs[: len(halos)], refs[len(halos) :]
        out_refs, (far_ref, product_ref) = refs[: lay.modes], refs[lay.modes :]
        plane, _ = lay.origin(j_ref[0], first)
        n = 0
        for halo_ref in halo_refs:
            for at in range(halo_ref.shape[0]):
                _, block = lay.origin(j_ref[0], n)
                n += 1

                def spread(i, carry, halo_ref=halo_ref, at=at, block=block):
                    far_ref[lay.place(block, i)] = halo_ref[at, pl.ds(i * rows, rows), :]
                    return carry

                lax.fori_loop(0, lay.fields, spread, 0, unroll=UNROLL)

        def operator_of(term):
            at = lay.slots + term
            far = far_ref[at]
            half, whole = 0.5 * far, 0.5 * (centre_ref[at, plane] + far)
            return lambda t: half * centre_ref[t, plane] - whole * far_ref[t]

        for term in range(1, lay.terms):
            operator = operator_of(term)

            def apply(n, carry, operator=operator, term=term):
                e = (term - 1) * ACTIVE + n
                product_ref[e] = operator(source_ref[e])
                return carry

            lax.fori_loop(0, ACTIVE, apply, 0, unroll=UNROLL)

        operator = operator_of(0)
        for n in range(lay.modes):
            _, block = lay.origin(j_ref[0], first + n)

            def collect(i, carry, out_ref=out_refs[n], block=block):
                s = block * lay.quota + i
                total = part_ref[s, plane] + operator(s)
                out_ref[i] = gather_products(s, take_ref, factor_ref, product_ref, (), total)
                return carry

            lax.fori_loop(0, lay.quota, collect, 0, unroll=UNROLL)

    return pl.pallas_call(
        kernel,
        out_shape=[jax.ShapeDtypeStruct((lay.quota, rows, width), jnp.float32)] * lay.modes,
        in_specs=smem(4) + vmem(2 + len(halos)),
        out_specs=vmem(lay.modes),
        scratch_shapes=[
            pltpu.VMEM((lay.places, rows, width), jnp.float32),
            pltpu.VMEM(((lay.terms - 1) * ACTIVE, rows, width), jnp.float32),
        ],
        compiler_params=pltpu.CompilerParams(vmem_limit_bytes=VMEM_LIMIT),
        name="outer_crossing" if crossing else "outer_own",
    )(j, *lists, centre, partial, *halos)


def on_device(chaos_field, mean_field, kl_fields, pattern, coupling, slot_mode):
    spaces, modes = lax.axis_size("space"), lax.axis_size("mode")
    quota, _, height, width = chaos_field.shape
    terms = kl_fields.shape[0] + 1
    lay = Layout(quota, terms, modes, height, width)
    axes = ("space", "mode")
    devices = spaces * modes
    space = lax.axis_index("space").astype(jnp.int32)
    mode = lax.axis_index("mode").astype(jnp.int32)
    j = (lax.rem(space, PLANES) * modes + mode).reshape(1)

    def swap(piece, r):
        if r == 0:
            return piece
        return lax.ppermute(piece, axes, [(d, d ^ r) for d in range(devices)])

    def shift(pieces, crossing):
        pairs = []
        for d in range(devices):
            upper = (d // modes) % PLANES == (0 if crossing else 1)
            other = d + lay.group if upper else d - lay.group
            if 0 <= other < devices:
                pairs.append((d, other))
        main = jnp.stack([piece[: lay.main] for piece in pieces])
        return lax.ppermute(main, axes, pairs)

    sent = pack(chaos_field[:, 0], mean_field, kl_fields[:, 0], j, lay)
    pieces = [swap(piece, r) for r, piece in enumerate(sent)]
    half = modes + modes // 2
    far_own = shift(pieces[:modes], False)
    far_first = shift(pieces[modes:half], True)
    far_second = shift(pieces[half:], True)
    lists = coupling_lists(pattern, coupling, slot_mode)
    partial, centre = inner(pieces, lists, j, lay)
    crossing = outer(centre, partial, [far_own], lists, j, True, lay)
    own = outer(centre, partial, [far_first, far_second], lists, j, False, lay)
    back = [swap(piece, r) for r, piece in enumerate(own + crossing)]
    return unpack(back, j, (quota, height, width), lay).reshape(chaos_field.shape)


def solution(mesh):
    in_specs = (
        P("mode", "space", None, None),
        P("space", None, None),
        P(None, "space", None, None),
        P(),
        P(),
        P(),
    )
    out_specs = P("mode", "space", None, None)
    return jax.shard_map(
        on_device, mesh=mesh, in_specs=in_specs, out_specs=out_specs, check_vma=False
    )
```

```python
import jax
import jax.numpy as jnp
from jax import lax
from jax.experimental import pallas as pl
from jax.experimental.pallas import tpu as pltpu
from jax.sharding import PartitionSpec as P

VMEM_LIMIT = 40 * 1024 * 1024
PACK_LIMIT = 60 * 1024 * 1024
PLANES = 2
ACTIVE = 49
MOST = 8
UNROLL = 7


class Layout:
    def __init__(self, quota, terms, modes, height, width):
        self.modes = modes
        self.group = PLANES * modes
        self.rows = height // self.group
        self.width = width
        self.terms = terms
        self.quota = quota
        self.slots = quota * modes
        self.share = -(-terms // modes)
        self.fields = quota + self.share
        self.main = self.fields * self.rows
        edges = -(-2 * self.fields // 8) * 8
        self.piece = self.main + edges
        self.places = self.fields * modes

    def place(self, block, i):
        if i < self.quota:
            return block * self.quota + i
        return self.slots + block * self.share + (i - self.quota)

    def term_place(self, term, mode):
        block = jnp.bitwise_xor(term // self.share, mode)
        return self.slots + block * self.share + term % self.share


def vmem(count):
    return [pl.BlockSpec(memory_space=pltpu.VMEM)] * count


def smem(count):
    return [pl.BlockSpec(memory_space=pltpu.SMEM)] * count


def pack(field, mean, kl, j, crossing, lay):
    kl_terms = kl.shape[0]
    rows, width = lay.rows, lay.width
    height = field.shape[1]
    first = lay.modes if crossing else 0

    def kernel(j_ref, field_ref, mean_ref, kl_ref, *refs):
        out_refs, (stage_ref, mean_here, kl_here, sems) = refs[: lay.modes], refs[lay.modes :]
        copies = [
            pltpu.make_async_copy(field_ref, stage_ref.at[pl.ds(0, lay.quota)], sems.at[0]),
            pltpu.make_async_copy(mean_ref, mean_here, sems.at[1]),
            pltpu.make_async_copy(kl_ref, kl_here, sems.at[2]),
        ]
        for made in copies:
            made.start()
        me = j_ref[0]
        mode = lax.rem(me, lay.modes)
        copies[1].wait()
        copies[2].wait()
        for i in range(lay.share):
            term = mode * lay.share + i
            other = kl_here[jnp.clip(term - 1, 0, kl_terms - 1)]
            stage_ref[lay.quota + i] = jnp.where(term == 0, mean_here[0], other)
        copies[0].wait()
        for n, out_ref in enumerate(out_refs):
            other = jnp.bitwise_xor(me, first + n)
            start = pl.multiple_of(other * rows, 8)
            lower = jnp.maximum(start - 1, 0)
            upper = jnp.minimum(start + rows, height - 1)
            keep_low = jnp.where(other == 0, 0.0, 1.0)
            keep_high = jnp.where(other == lay.group - 1, 0.0, 1.0)
            for i in range(lay.fields):
                out_ref[i * rows : (i + 1) * rows, :] = stage_ref[i, pl.ds(start, rows), :]
                at = lay.main + 2 * i
                out_ref[at : at + 1, :] = stage_ref[i, pl.ds(lower, 1), :] * keep_low
                out_ref[at + 1 : at + 2, :] = stage_ref[i, pl.ds(upper, 1), :] * keep_high
            spare = lay.piece - lay.main - 2 * lay.fields
            if spare:
                out_ref[lay.piece - spare :, :] = jnp.zeros((spare, width), jnp.float32)

    return pl.pallas_call(
        kernel,
        out_shape=[jax.ShapeDtypeStruct((lay.piece, width), jnp.float32)] * lay.modes,
        in_specs=smem(1) + [pl.BlockSpec(memory_space=pltpu.HBM)] * 3,
        out_specs=vmem(lay.modes),
        scratch_shapes=[
            pltpu.VMEM((lay.fields, height, width), jnp.float32),
            pltpu.VMEM(mean.shape, jnp.float32),
            pltpu.VMEM(kl.shape, jnp.float32),
            pltpu.SemaphoreType.DMA((3,)),
        ],
        compiler_params=pltpu.CompilerParams(vmem_limit_bytes=PACK_LIMIT),
        name="pack_crossing" if crossing else "pack_own",
    )(j, field, mean, kl)


def unpack(pieces, j, shape, lay):
    rows = lay.rows

    def kernel(j_ref, *refs):
        piece_refs, out_ref, sems = refs[:-2], refs[-2], refs[-1]
        copies = []
        for r, piece_ref in zip(pieces, piece_refs):
            start = pl.multiple_of(jnp.bitwise_xor(j_ref[0], r) * rows, 8)
            made = pltpu.make_async_copy(
                piece_ref, out_ref.at[:, pl.ds(start, rows), :], sems.at[r]
            )
            made.start()
            copies.append(made)
        for made in copies:
            made.wait()

    return pl.pallas_call(
        kernel,
        out_shape=jax.ShapeDtypeStruct(shape, jnp.float32),
        in_specs=smem(1) + vmem(lay.group),
        out_specs=pl.BlockSpec(memory_space=pltpu.HBM),
        scratch_shapes=[pltpu.SemaphoreType.DMA((lay.group,))],
        compiler_params=pltpu.CompilerParams(vmem_limit_bytes=VMEM_LIMIT),
        name="unpack",
    )(j, *pieces.values())


def coupling_lists(pattern, coupling, slot_mode):
    masked = (coupling * pattern.astype(jnp.float32))[1:]
    terms, modes = masked.shape[0], masked.shape[1]
    number = jnp.arange(modes, dtype=jnp.int32)
    one_hot = (slot_mode[:, None] == number[None, :]).astype(jnp.float32)
    coupled = jnp.einsum(
        "sa,kab,tb->kst", one_hot, masked, one_hot, precision=lax.Precision.HIGHEST
    )
    there = coupled != 0.0
    column = number[None, None, :]
    first = jnp.min(jnp.where(there, column, modes), 2)
    last = jnp.max(jnp.where(there, column, -1), 2)
    active = first < modes
    earlier = column < number[None, :, None]
    rank = jnp.sum(jnp.where(active[:, None, :] & earlier, 1, 0), 2)
    place = jnp.arange(ACTIVE, dtype=jnp.int32)[None, :, None]
    chosen = active[:, None, :] & (rank[:, None, :] == place)
    sources = jnp.sum(jnp.where(chosen, column, 0), 2)

    base = ACTIVE * jnp.arange(terms, dtype=jnp.int32)[:, None]
    products, factors, valid = [], [], []
    for chosen_t, is_valid in ((first, active), (last, last > first)):
        before = active[:, None, :] & (column < chosen_t[:, :, None])
        products.append(base + jnp.sum(jnp.where(before, 1, 0), 2))
        factors.append(jnp.sum(jnp.where(column == chosen_t[:, :, None], coupled, 0.0), 2))
        valid.append(is_valid)
    products = jnp.concatenate(products, 0)
    factors = jnp.concatenate(factors, 0)
    valid = jnp.concatenate(valid, 0)
    index = jnp.arange(2 * terms, dtype=jnp.int32)
    order = index[None, :] < index[:, None]
    rank = jnp.sum(jnp.where(valid[None] & order[:, :, None], 1, 0), 1)
    place = jnp.arange(MOST, dtype=jnp.int32)[:, None, None]
    chosen = valid[None] & (rank[None] == place)
    take = jnp.sum(jnp.where(chosen, products[None], 0), 1)
    factor = jnp.sum(jnp.where(chosen, factors[None], 0.0), 1)
    return sources.reshape(-1), take.T.reshape(-1), factor.T.reshape(-1)


def gather_products(s, take_ref, factor_ref, product_ref, total):
    for n in range(MOST):
        e = s * MOST + n
        total = total + factor_ref[e] * product_ref[take_ref[e]]
    return total


def inner(pieces, others, lists, j, name, lay):
    rows, width = lay.rows, lay.width
    full = (rows, width)

    def kernel(j_ref, source_ref, take_ref, factor_ref, *refs):
        piece_refs, refs = refs[: lay.modes], refs[lay.modes :]
        other_refs, refs = refs[: lay.modes], refs[lay.modes :]
        out_ref, centre_ref, near_ref, beyond_ref, product_ref = refs
        lane = lax.broadcasted_iota(jnp.int32, full, 1)
        line = lax.broadcasted_iota(jnp.int32, full, 0)
        mode = lax.rem(j_ref[0], lay.modes)

        for block in range(lay.modes):

            def spread(i, at, piece_ref=piece_refs[block], other_ref=other_refs[block]):
                here = piece_ref[pl.ds(i * rows, rows), :]
                low = piece_ref[pl.ds(lay.main + 2 * i, 1), :]
                high = piece_ref[pl.ds(lay.main + 2 * i + 1, 1), :]
                centre_ref[at] = here
                beyond_ref[at] = other_ref[pl.ds(i * rows, rows), :]
                near_ref[at, 0] = pltpu.roll(here, width - 1, 1)
                near_ref[at, 1] = pltpu.roll(here, 1, 1)
                near_ref[at, 2] = jnp.where(line == rows - 1, high, pltpu.roll(here, rows - 1, 0))
                near_ref[at, 3] = jnp.where(line == 0, low, pltpu.roll(here, 1, 0))

            def spread_slot(i, carry, spread=spread, block=block):
                spread(i, block * lay.quota + i)
                return carry

            lax.fori_loop(0, lay.quota, spread_slot, 0, unroll=UNROLL)
            for i in range(lay.quota, lay.fields):
                spread(i, lay.place(block, i))

        def operator_of(term):
            at = lay.term_place(term, mode)
            here = centre_ref[at]
            beside = [near_ref[at, n] for n in range(4)]
            beside[0] = jnp.where(lane == width - 1, 0.0, beside[0])
            beside[1] = jnp.where(lane == 0, 0.0, beside[1])
            faces = [0.5 * (here + n) for n in beside]
            between = 0.5 * (here + beyond_ref[at])
            diagonal = faces[0] + faces[1] + faces[2] + faces[3] + between + 0.5 * here
            faces[0] = jnp.where(lane == width - 1, 0.0, faces[0])
            faces[1] = jnp.where(lane == 0, 0.0, faces[1])

            def operator(t):
                total = diagonal * centre_ref[t] - between * beyond_ref[t]
                for n in range(4):
                    total = total - faces[n] * near_ref[t, n]
                return total

            return operator

        for term in range(1, lay.terms):
            operator = operator_of(term)

            def apply(n, carry, operator=operator, term=term):
                e = (term - 1) * ACTIVE + n
                product_ref[e] = operator(source_ref[e])
                return carry

            lax.fori_loop(0, ACTIVE, apply, 0, unroll=UNROLL)

        operator = operator_of(0)

        def collect(s, carry):
            out_ref[s] = gather_products(s, take_ref, factor_ref, product_ref, operator(s))
            return carry

        lax.fori_loop(0, lay.slots, collect, 0, unroll=UNROLL)

    return pl.pallas_call(
        kernel,
        out_shape=[
            jax.ShapeDtypeStruct((lay.slots, rows, width), jnp.float32),
            jax.ShapeDtypeStruct((lay.places, rows, width), jnp.float32),
        ],
        in_specs=smem(4) + vmem(2 * lay.modes),
        out_specs=vmem(2),
        scratch_shapes=[
            pltpu.VMEM((lay.places, 4, rows, width), jnp.float32),
            pltpu.VMEM((lay.places, rows, width), jnp.float32),
            pltpu.VMEM(((lay.terms - 1) * ACTIVE, rows, width), jnp.float32),
        ],
        compiler_params=pltpu.CompilerParams(vmem_limit_bytes=VMEM_LIMIT),
        name=name,
    )(j, *lists, *pieces, *others)


def outer(centre, partial, halos, lists, j, name, lay):
    rows, width = lay.rows, lay.width

    def kernel(j_ref, source_ref, take_ref, factor_ref, centre_ref, part_ref, *refs):
        halo_refs, refs = refs[: len(halos)], refs[len(halos) :]
        out_refs, (far_ref, product_ref) = refs[: lay.modes], refs[lay.modes :]
        mode = lax.rem(j_ref[0], lay.modes)
        block = 0
        for halo_ref in halo_refs:
            for n in range(halo_ref.shape[0]):

                def spread_slot(i, carry, halo_ref=halo_ref, n=n, block=block):
                    far_ref[block * lay.quota + i] = halo_ref[n, pl.ds(i * rows, rows), :]
                    return carry

                lax.fori_loop(0, lay.quota, spread_slot, 0, unroll=UNROLL)
                for i in range(lay.quota, lay.fields):
                    far_ref[lay.place(block, i)] = halo_ref[n, i * rows : (i + 1) * rows, :]
                block += 1

        def operator_of(term):
            at = lay.term_place(term, mode)
            far = far_ref[at]
            half, whole = 0.5 * far, 0.5 * (centre_ref[at] + far)
            return lambda t: half * centre_ref[t] - whole * far_ref[t]

        for term in range(1, lay.terms):
            operator = operator_of(term)

            def apply(n, carry, operator=operator, term=term):
                e = (term - 1) * ACTIVE + n
                product_ref[e] = operator(source_ref[e])
                return carry

            lax.fori_loop(0, ACTIVE, apply, 0, unroll=UNROLL)

        operator = operator_of(0)
        for block in range(lay.modes):

            def collect(i, carry, out_ref=out_refs[block], block=block):
                s = block * lay.quota + i
                total = part_ref[s] + operator(s)
                out_ref[i] = gather_products(s, take_ref, factor_ref, product_ref, total)
                return carry

            lax.fori_loop(0, lay.quota, collect, 0, unroll=UNROLL)

    return pl.pallas_call(
        kernel,
        out_shape=[jax.ShapeDtypeStruct((lay.quota, rows, width), jnp.float32)] * lay.modes,
        in_specs=smem(4) + vmem(2 + len(halos)),
        out_specs=vmem(lay.modes),
        scratch_shapes=[
            pltpu.VMEM((lay.places, rows, width), jnp.float32),
            pltpu.VMEM(((lay.terms - 1) * ACTIVE, rows, width), jnp.float32),
        ],
        compiler_params=pltpu.CompilerParams(vmem_limit_bytes=VMEM_LIMIT),
        name=name,
    )(j, *lists, centre, partial, *halos)


def after(value, *done):
    return lax.optimization_barrier((value, *done))[0]


def on_device(chaos_field, mean_field, kl_fields, pattern, coupling, slot_mode):
    spaces, modes = lax.axis_size("space"), lax.axis_size("mode")
    quota, _, height, width = chaos_field.shape
    terms = kl_fields.shape[0] + 1
    lay = Layout(quota, terms, modes, height, width)
    axes = ("space", "mode")
    devices = spaces * modes
    space = lax.axis_index("space").astype(jnp.int32)
    mode = lax.axis_index("mode").astype(jnp.int32)
    j = (lax.rem(space, PLANES) * modes + mode).reshape(1)

    def swap(piece, r):
        if r == 0:
            return piece
        return lax.ppermute(piece, axes, [(d, d ^ r) for d in range(devices)])

    def shift(pieces, crossing):
        pairs = []
        for d in range(devices):
            upper = (d // modes) % PLANES == (0 if crossing else 1)
            other = d + lay.group if upper else d - lay.group
            if 0 <= other < devices:
                pairs.append((d, other))
        main = jnp.stack([piece[: lay.main] for piece in pieces])
        return lax.ppermute(main, axes, pairs)

    field, kl = chaos_field[:, 0], kl_fields[:, 0]
    sent = [None] * lay.group
    sent[modes:] = pack(field, mean_field, kl, j, True, lay)
    sent[:modes] = pack(field, mean_field, kl, after(j, *sent[modes:]), False, lay)
    pieces = sent[:1] + [None] * (lay.group - 1)
    half = modes + modes // 2
    early = [r for r in range(modes, half)] + [r for r in range(1, modes)]
    for r in early:
        pieces[r] = swap(sent[r], r)
    for r in range(half, lay.group):
        pieces[r] = swap(after(sent[r], pieces[r - half + 1]), r)
    number = jnp.arange(modes, dtype=jnp.int32)
    mine = jnp.bitwise_xor(number, mode)[:, None, None] == number[None, :, None]
    slot_mode = jnp.sum(jnp.where(mine, slot_mode.reshape(1, modes, quota), 0), 1).reshape(-1)
    lists = coupling_lists(pattern, coupling, slot_mode)
    pieces[modes] = after(pieces[modes], *lists)
    far_own = shift(pieces[:modes], False)
    far_first = shift(pieces[modes:half], True)
    far_second = shift(pieces[half:], True)

    part, centre = inner(pieces[modes:], pieces[:modes], lists, j, "inner_crossing", lay)
    own_part, own_centre = inner(pieces[:modes], pieces[modes:], lists, j, "inner_own", lay)
    crossing = outer(centre, part, [far_own], lists, j, "outer_crossing", lay)
    own_part = after(own_part, *crossing)
    own = outer(own_centre, own_part, [far_first, far_second], lists, j, "outer_own", lay)
    back = {modes + n: swap(piece, modes + n) for n, piece in enumerate(crossing)}
    back.update({n: swap(piece, n) for n, piece in enumerate(own)})
    return unpack(back, j, (quota, height, width), lay).reshape(chaos_field.shape)


def solution(mesh):
    in_specs = (
        P("mode", "space", None, None),
        P("space", None, None),
        P(None, "space", None, None),
        P(),
        P(),
        P(),
    )
    out_specs = P("mode", "space", None, None)
    return jax.shard_map(
        on_device, mesh=mesh, in_specs=in_specs, out_specs=out_specs, check_vma=False
    )
```

```python
import jax
import jax.numpy as jnp
from jax import lax
from jax.experimental import pallas as pl
from jax.experimental.pallas import tpu as pltpu
from jax.sharding import PartitionSpec as P

VMEM_LIMIT = 40 * 1024 * 1024
PACK_LIMIT = 60 * 1024 * 1024
PLANES = 2
ACTIVE = 49
MOST = 8
UNROLL = 7


class Layout:
    def __init__(self, quota, terms, modes, height, width):
        self.modes = modes
        self.group = PLANES * modes
        self.rows = height // self.group
        self.width = width
        self.terms = terms
        self.quota = quota
        self.slots = quota * modes
        self.share = -(-terms // modes)
        self.fields = quota + self.share
        self.main = self.fields * self.rows
        self.parts = self.fields + -(-2 * self.fields // self.rows)
        self.piece = self.parts * self.rows
        self.places = self.fields * modes

    def edge(self, i):
        return self.fields + 2 * i // self.rows, 2 * i % self.rows

    def place(self, block, i):
        if i < self.quota:
            return block * self.quota + i
        return self.slots + block * self.share + (i - self.quota)

    def term_place(self, term, mode):
        block = jnp.bitwise_xor(term // self.share, mode)
        return self.slots + block * self.share + term % self.share


def vmem(count):
    return [pl.BlockSpec(memory_space=pltpu.VMEM)] * count


def smem(count):
    return [pl.BlockSpec(memory_space=pltpu.SMEM)] * count


def pack(field, mean, kl, j, crossing, lay):
    kl_terms = kl.shape[0]
    rows, width, modes, quota = lay.rows, lay.width, lay.modes, lay.quota
    half = modes * rows
    tile = 8

    def kernel(j_ref, field_ref, mean_ref, kl_ref, *refs):
        out_refs, (stage_ref, past_ref, in_sems, out_sems) = refs[:modes], refs[modes:]
        plane = j_ref[0] // modes
        mode = j_ref[0] - plane * modes
        side = 1 - plane if crossing else plane
        start = side * half
        beside = pl.multiple_of(half - side * tile, tile)

        def load(n, begin=True):
            if n < modes:
                at, target = pl.ds(pl.multiple_of(start + n * rows, tile), rows), stage_ref.at[n]
            else:
                at, target = pl.ds(beside, tile), past_ref
            copies = [
                pltpu.make_async_copy(
                    field_ref.at[:, at, :], target.at[pl.ds(0, quota)], in_sems.at[n, 0]
                )
            ]
            if begin:
                copies[0].start()
            for i in range(lay.share):
                term = mode * lay.share + i
                into, sem = target.at[quota + i], in_sems.at[n, 1 + i]
                if not begin:
                    copies.append(pltpu.make_async_copy(mean_ref.at[0, at, :], into, sem))
                    continue

                @pl.when(term == 0)
                def _():
                    pltpu.make_async_copy(mean_ref.at[0, at, :], into, sem).start()

                @pl.when(term > 0)
                def _():
                    source = kl_ref.at[jnp.clip(term - 1, 0, kl_terms - 1), at, :]
                    pltpu.make_async_copy(source, into, sem).start()

            return copies

        for n in range(modes + 1):
            load(n)
        for n in range(modes + 1):
            for made in load(n, begin=False):
                made.wait()
        low_there = jnp.where(side == 0, 0.0, 1.0)
        high_there = jnp.where(side == PLANES - 1, 0.0, 1.0)
        for n in range(modes):
            for i in range(lay.fields):
                if n > 0:
                    low = stage_ref[n - 1, i, rows - 1 :]
                else:
                    low = past_ref[i, tile - 1 :] * low_there
                if n < modes - 1:
                    high = stage_ref[n + 1, i, :1]
                else:
                    high = past_ref[i, :1] * high_there
                part, line = lay.edge(i)
                stage_ref[n, part, line : line + 1] = low
                stage_ref[n, part, line + 1 : line + 2] = high
            part, line = lay.edge(lay.fields)
            if part < lay.parts:
                stage_ref[n, part, line:] = jnp.zeros((rows - line, width), jnp.float32)
        copies = []
        for n, out_ref in enumerate(out_refs):
            source = stage_ref.at[jnp.bitwise_xor(mode, n)]
            made = pltpu.make_async_copy(source, out_ref, out_sems.at[n])
            made.start()
            copies.append(made)
        for made in copies:
            made.wait()

    shape = (lay.parts, rows, width)
    sent = pl.pallas_call(
        kernel,
        out_shape=[jax.ShapeDtypeStruct(shape, jnp.float32)] * modes,
        in_specs=smem(1) + [pl.BlockSpec(memory_space=pltpu.HBM)] * 3,
        out_specs=[pl.BlockSpec(memory_space=pltpu.HBM)] * modes,
        scratch_shapes=[
            pltpu.VMEM((modes, *shape), jnp.float32),
            pltpu.VMEM((lay.fields, tile, width), jnp.float32),
            pltpu.SemaphoreType.DMA((modes + 1, 1 + lay.share)),
            pltpu.SemaphoreType.DMA((modes,)),
        ],
        compiler_params=pltpu.CompilerParams(vmem_limit_bytes=PACK_LIMIT),
        name="pack_crossing" if crossing else "pack_own",
    )(j, field, mean, kl)
    return [piece.reshape(lay.piece, width) for piece in sent]


def unpack(pieces, j, shape, lay):
    rows = lay.rows

    def kernel(j_ref, *refs):
        piece_refs, out_ref, sems = refs[:-2], refs[-2], refs[-1]
        copies = []
        for r, piece_ref in zip(pieces, piece_refs):
            start = pl.multiple_of(jnp.bitwise_xor(j_ref[0], r) * rows, 8)
            made = pltpu.make_async_copy(
                piece_ref, out_ref.at[:, pl.ds(start, rows), :], sems.at[r]
            )
            made.start()
            copies.append(made)
        for made in copies:
            made.wait()

    return pl.pallas_call(
        kernel,
        out_shape=jax.ShapeDtypeStruct(shape, jnp.float32),
        in_specs=smem(1) + vmem(lay.group),
        out_specs=pl.BlockSpec(memory_space=pltpu.HBM),
        scratch_shapes=[pltpu.SemaphoreType.DMA((lay.group,))],
        compiler_params=pltpu.CompilerParams(vmem_limit_bytes=VMEM_LIMIT),
        name="unpack",
    )(j, *pieces.values())


def coupling_lists(pattern, coupling, slot_mode):
    masked = (coupling * pattern.astype(jnp.float32))[1:]
    terms, modes = masked.shape[0], masked.shape[1]
    number = jnp.arange(modes, dtype=jnp.int32)
    one_hot = (slot_mode[:, None] == number[None, :]).astype(jnp.float32)
    coupled = jnp.einsum(
        "sa,kab,tb->kst", one_hot, masked, one_hot, precision=lax.Precision.HIGHEST
    )
    there = coupled != 0.0
    column = number[None, None, :]
    first = jnp.min(jnp.where(there, column, modes), 2)
    last = jnp.max(jnp.where(there, column, -1), 2)
    active = first < modes
    earlier = column < number[None, :, None]
    rank = jnp.sum(jnp.where(active[:, None, :] & earlier, 1, 0), 2)
    place = jnp.arange(ACTIVE, dtype=jnp.int32)[None, :, None]
    chosen = active[:, None, :] & (rank[:, None, :] == place)
    sources = jnp.sum(jnp.where(chosen, column, 0), 2)

    base = ACTIVE * jnp.arange(terms, dtype=jnp.int32)[:, None]
    products, factors, valid = [], [], []
    for chosen_t, is_valid in ((first, active), (last, last > first)):
        before = active[:, None, :] & (column < chosen_t[:, :, None])
        products.append(base + jnp.sum(jnp.where(before, 1, 0), 2))
        factors.append(jnp.sum(jnp.where(column == chosen_t[:, :, None], coupled, 0.0), 2))
        valid.append(is_valid)
    products = jnp.concatenate(products, 0)
    factors = jnp.concatenate(factors, 0)
    valid = jnp.concatenate(valid, 0)
    index = jnp.arange(2 * terms, dtype=jnp.int32)
    order = index[None, :] < index[:, None]
    rank = jnp.sum(jnp.where(valid[None] & order[:, :, None], 1, 0), 1)
    place = jnp.arange(MOST, dtype=jnp.int32)[:, None, None]
    chosen = valid[None] & (rank[None] == place)
    take = jnp.sum(jnp.where(chosen, products[None], 0), 1)
    factor = jnp.sum(jnp.where(chosen, factors[None], 0.0), 1)
    return sources.reshape(-1), take.T.reshape(-1), factor.T.reshape(-1)


def gather_products(s, take_ref, factor_ref, product_ref, total):
    for n in range(MOST):
        e = s * MOST + n
        total = total + factor_ref[e] * product_ref[take_ref[e]]
    return total


def stencil(pieces, others, halos, lists, j, name, lay):
    rows, width = lay.rows, lay.width
    full = (rows, width)

    def kernel(j_ref, source_ref, take_ref, factor_ref, *refs):
        piece_refs, refs = refs[: lay.modes], refs[lay.modes :]
        other_refs, refs = refs[: lay.modes], refs[lay.modes :]
        halo_refs, refs = refs[: len(halos)], refs[len(halos) :]
        out_refs, (near_ref, product_ref) = refs[: lay.modes], refs[lay.modes :]
        lane = lax.broadcasted_iota(jnp.int32, full, 1)
        line = lax.broadcasted_iota(jnp.int32, full, 0)
        mode = lax.rem(j_ref[0], lay.modes)
        halo_parts = [(ref, n) for ref in halo_refs for n in range(ref.shape[0])]

        for block in range(lay.modes):

            def spread(i, at, block=block):
                piece_ref = piece_refs[block]
                halo_ref, n = halo_parts[block]
                here = piece_ref[pl.ds(i * rows, rows), :]
                low = piece_ref[pl.ds(lay.main + 2 * i, 1), :]
                high = piece_ref[pl.ds(lay.main + 2 * i + 1, 1), :]
                near_ref[at, 0] = here
                near_ref[at, 1] = pltpu.roll(here, width - 1, 1)
                near_ref[at, 2] = pltpu.roll(here, 1, 1)
                near_ref[at, 3] = jnp.where(line == rows - 1, high, pltpu.roll(here, rows - 1, 0))
                near_ref[at, 4] = jnp.where(line == 0, low, pltpu.roll(here, 1, 0))
                near_ref[at, 5] = other_refs[block][pl.ds(i * rows, rows), :]
                near_ref[at, 6] = halo_ref[n, pl.ds(i * rows, rows), :]

            def spread_slot(i, carry, spread=spread, block=block):
                spread(i, block * lay.quota + i)
                return carry

            lax.fori_loop(0, lay.quota, spread_slot, 0, unroll=UNROLL)
            for i in range(lay.quota, lay.fields):
                spread(i, lay.place(block, i))

        def operator_of(term):
            at = lay.term_place(term, mode)
            here, right, left, *rest = [near_ref[at, n] for n in range(7)]
            right = jnp.where(lane == width - 1, 0.0, right)
            left = jnp.where(lane == 0, 0.0, left)
            faces = [0.5 * (here + n) for n in (right, left, *rest)]
            diagonal = faces[0] + faces[1] + faces[2] + faces[3] + faces[4] + faces[5]
            faces[0] = jnp.where(lane == width - 1, 0.0, faces[0])
            faces[1] = jnp.where(lane == 0, 0.0, faces[1])

            def operator(t):
                total = diagonal * near_ref[t, 0]
                for n, face in enumerate(faces):
                    total = total - face * near_ref[t, n + 1]
                return total

            return operator

        for term in range(1, lay.terms):
            operator = operator_of(term)

            def apply(n, carry, operator=operator, term=term):
                e = (term - 1) * ACTIVE + n
                product_ref[e] = operator(source_ref[e])
                return carry

            lax.fori_loop(0, ACTIVE, apply, 0, unroll=UNROLL)

        operator = operator_of(0)
        for block in range(lay.modes):

            def collect(i, carry, out_ref=out_refs[block], block=block):
                s = block * lay.quota + i
                out_ref[i] = gather_products(s, take_ref, factor_ref, product_ref, operator(s))
                return carry

            lax.fori_loop(0, lay.quota, collect, 0, unroll=UNROLL)

    return pl.pallas_call(
        kernel,
        out_shape=[jax.ShapeDtypeStruct((lay.quota, rows, width), jnp.float32)] * lay.modes,
        in_specs=smem(4) + vmem(2 * lay.modes + len(halos)),
        out_specs=vmem(lay.modes),
        scratch_shapes=[
            pltpu.VMEM((lay.places, 7, rows, width), jnp.float32),
            pltpu.VMEM(((lay.terms - 1) * ACTIVE, rows, width), jnp.float32),
        ],
        compiler_params=pltpu.CompilerParams(vmem_limit_bytes=VMEM_LIMIT),
        name=name,
    )(j, *lists, *pieces, *others, *halos)


def after(value, *done):
    return lax.optimization_barrier((value, *done))[0]


def on_device(chaos_field, mean_field, kl_fields, pattern, coupling, slot_mode):
    spaces, modes = lax.axis_size("space"), lax.axis_size("mode")
    quota, _, height, width = chaos_field.shape
    terms = kl_fields.shape[0] + 1
    lay = Layout(quota, terms, modes, height, width)
    axes = ("space", "mode")
    devices = spaces * modes
    space = lax.axis_index("space").astype(jnp.int32)
    mode = lax.axis_index("mode").astype(jnp.int32)
    j = (lax.rem(space, PLANES) * modes + mode).reshape(1)

    def swap(piece, r):
        if r == 0:
            return piece
        return lax.ppermute(piece, axes, [(d, d ^ r) for d in range(devices)])

    def shift(pieces, crossing):
        pairs = []
        for d in range(devices):
            upper = (d // modes) % PLANES == (0 if crossing else 1)
            other = d + lay.group if upper else d - lay.group
            if 0 <= other < devices:
                pairs.append((d, other))
        main = jnp.stack([piece[: lay.main] for piece in pieces])
        return lax.ppermute(main, axes, pairs)

    field, kl = chaos_field[:, 0], kl_fields[:, 0]
    sent = [None] * lay.group
    sent[:modes] = pack(field, mean_field, kl, j, False, lay)
    sent[modes:] = pack(field, mean_field, kl, after(j, *sent[:modes]), True, lay)
    half = modes // 2
    pieces = sent[:1] + [None] * (lay.group - 1)
    for r in [*range(half, modes), *range(1, half), *range(modes, modes + half)]:
        pieces[r] = swap(sent[r], r)
    for r in range(modes + half, lay.group):
        pieces[r] = swap(after(sent[r], *pieces[half:modes]), r)
    number = jnp.arange(modes, dtype=jnp.int32)
    mine = jnp.bitwise_xor(number, mode)[:, None, None] == number[None, :, None]
    slot_mode = jnp.sum(jnp.where(mine, slot_mode.reshape(1, modes, quota), 0), 1).reshape(-1)
    lists = coupling_lists(pattern, coupling, slot_mode)
    pieces[half] = after(pieces[half], *lists)
    own_halo = shift(pieces[:modes], False)
    halos = [shift(pieces[r : r + half], True) for r in (modes, modes + half)]

    own, crossing = pieces[:modes], pieces[modes:]
    crossing_out = stencil(crossing, own, [own_halo], lists, j, "stencil_crossing", lay)
    own_j = after(j, *crossing_out)
    own_out = stencil(own, crossing, halos, lists, own_j, "stencil_own", lay)
    back = {}
    for n in [*range(half, modes), *range(half)]:
        back[modes + n] = swap(crossing_out[n], modes + n)
    for n in [*range(half, modes), *range(half)]:
        back[n] = swap(own_out[n], n)
    return unpack(back, j, (quota, height, width), lay).reshape(chaos_field.shape)


def solution(mesh):
    in_specs = (
        P("mode", "space", None, None),
        P("space", None, None),
        P(None, "space", None, None),
        P(),
        P(),
        P(),
    )
    out_specs = P("mode", "space", None, None)
    return jax.shard_map(
        on_device, mesh=mesh, in_specs=in_specs, out_specs=out_specs, check_vma=False
    )
```

```python
import jax
import jax.numpy as jnp
from jax import lax
from jax.experimental import pallas as pl
from jax.experimental.pallas import tpu as pltpu
from jax.sharding import PartitionSpec as P

VMEM_LIMIT = 40 * 1024 * 1024
PLANES = 2
ACTIVE = 49
MOST = 8
GROUP = 7


class Layout:
    def __init__(self, quota, terms, modes, height, width):
        self.modes = modes
        self.group = PLANES * modes
        self.rows = height // self.group
        self.width = width
        self.terms = terms
        self.quota = quota
        self.slots = quota * modes
        self.share = -(-terms // modes)
        self.fields = quota + self.share
        self.main = self.fields * self.rows
        self.parts = self.fields + -(-2 * self.fields // self.rows)
        self.piece = self.parts * self.rows
        self.places = self.fields * modes

    def edge(self, i):
        return self.fields + 2 * i // self.rows, 2 * i % self.rows

    def place(self, block, i):
        if i < self.quota:
            return block * self.quota + i
        return self.slots + block * self.share + (i - self.quota)

    def term_place(self, term, mode):
        block = jnp.bitwise_xor(term // self.share, mode)
        return self.slots + block * self.share + term % self.share


def vmem(count):
    return [pl.BlockSpec(memory_space=pltpu.VMEM)] * count


def smem(count):
    return [pl.BlockSpec(memory_space=pltpu.SMEM)] * count


def pack(field, mean, kl, j, crossing, lay):
    kl_terms = kl.shape[0]
    rows, width, modes, quota = lay.rows, lay.width, lay.modes, lay.quota
    half = modes * rows
    tile = 8

    def kernel(j_ref, field_ref, mean_ref, kl_ref, *refs):
        out_refs, (stage_ref, past_ref, in_sems) = refs[:modes], refs[modes:]
        plane = j_ref[0] // modes
        mode = j_ref[0] - plane * modes
        side = 1 - plane if crossing else plane
        start = side * half
        beside = pl.multiple_of(half - side * tile, tile)

        def load(n, begin=True):
            if n < modes:
                at, target = pl.ds(pl.multiple_of(start + n * rows, tile), rows), stage_ref.at[n]
            else:
                at, target = pl.ds(beside, tile), past_ref
            copies = [
                pltpu.make_async_copy(
                    field_ref.at[:, at, :], target.at[pl.ds(0, quota)], in_sems.at[n, 0]
                )
            ]
            if begin:
                copies[0].start()
            for i in range(lay.share):
                term = mode * lay.share + i
                into, sem = target.at[quota + i], in_sems.at[n, 1 + i]
                if not begin:
                    copies.append(pltpu.make_async_copy(mean_ref.at[0, at, :], into, sem))
                    continue

                @pl.when(term == 0)
                def _():
                    pltpu.make_async_copy(mean_ref.at[0, at, :], into, sem).start()

                @pl.when(term > 0)
                def _():
                    source = kl_ref.at[jnp.clip(term - 1, 0, kl_terms - 1), at, :]
                    pltpu.make_async_copy(source, into, sem).start()

            return copies

        for n in range(modes + 1):
            load(n)
        for n in range(modes + 1):
            for made in load(n, begin=False):
                made.wait()
        low_there = jnp.where(side == 0, 0.0, 1.0)
        high_there = jnp.where(side == PLANES - 1, 0.0, 1.0)
        for n in range(modes):
            for i in range(lay.fields):
                if n > 0:
                    low = stage_ref[n - 1, i, rows - 1 :]
                else:
                    low = past_ref[i, tile - 1 :] * low_there
                if n < modes - 1:
                    high = stage_ref[n + 1, i, :1]
                else:
                    high = past_ref[i, :1] * high_there
                part, line = lay.edge(i)
                stage_ref[n, part, line : line + 1] = low
                stage_ref[n, part, line + 1 : line + 2] = high
            part, line = lay.edge(lay.fields)
            if part < lay.parts:
                stage_ref[n, part, line:] = jnp.zeros((rows - line, width), jnp.float32)
        for n, out_ref in enumerate(out_refs):
            to = jnp.bitwise_xor(mode, n)
            for part in range(lay.parts):
                out_ref[part] = stage_ref[to, part]

    shape = (lay.parts, rows, width)
    sent = pl.pallas_call(
        kernel,
        out_shape=[pltpu.VMEM(shape, jnp.float32)] * modes,
        in_specs=smem(1) + [pl.BlockSpec(memory_space=pltpu.HBM)] * 3,
        out_specs=vmem(modes),
        scratch_shapes=[
            pltpu.VMEM((modes, *shape), jnp.float32),
            pltpu.VMEM((lay.fields, tile, width), jnp.float32),
            pltpu.SemaphoreType.DMA((modes + 1, 1 + lay.share)),
        ],
        compiler_params=pltpu.CompilerParams(vmem_limit_bytes=VMEM_LIMIT),
        name="pack_crossing" if crossing else "pack_own",
    )(j, *[pltpu.with_memory_space_constraint(x, pltpu.HBM) for x in (field, mean, kl)])
    return [piece.reshape(lay.piece, width) for piece in sent]


def unpack(pieces, j, shape, lay):
    rows = lay.rows

    def kernel(j_ref, *refs):
        piece_refs, out_ref, sems = refs[:-2], refs[-2], refs[-1]
        copies = []
        for r, piece_ref in zip(pieces, piece_refs):
            start = pl.multiple_of(jnp.bitwise_xor(j_ref[0], r) * rows, 8)
            made = pltpu.make_async_copy(
                piece_ref, out_ref.at[:, pl.ds(start, rows), :], sems.at[r]
            )
            made.start()
            copies.append(made)
        for made in copies:
            made.wait()

    return pl.pallas_call(
        kernel,
        out_shape=jax.ShapeDtypeStruct(shape, jnp.float32),
        in_specs=smem(1) + vmem(lay.group),
        out_specs=pl.BlockSpec(memory_space=pltpu.HBM),
        scratch_shapes=[pltpu.SemaphoreType.DMA((lay.group,))],
        compiler_params=pltpu.CompilerParams(vmem_limit_bytes=VMEM_LIMIT),
        name="unpack",
    )(j, *pieces.values())


def coupling_lists(pattern, coupling, slot_mode):
    masked = (coupling * pattern.astype(jnp.float32))[1:]
    terms, modes = masked.shape[0], masked.shape[1]
    number = jnp.arange(modes, dtype=jnp.int32)
    one_hot = (slot_mode[:, None] == number[None, :]).astype(jnp.float32)
    coupled = jnp.einsum(
        "sa,kab,tb->kst", one_hot, masked, one_hot, precision=lax.Precision.HIGHEST
    )
    there = coupled != 0.0
    column = number[None, None, :]
    first = jnp.min(jnp.where(there, column, modes), 2)
    last = jnp.max(jnp.where(there, column, -1), 2)
    active = first < modes
    earlier = column < number[None, :, None]
    rank = jnp.sum(jnp.where(active[:, None, :] & earlier, 1, 0), 2)
    place = jnp.arange(ACTIVE, dtype=jnp.int32)[None, :, None]
    chosen = active[:, None, :] & (rank[:, None, :] == place)
    sources = jnp.sum(jnp.where(chosen, column, 0), 2)

    base = ACTIVE * jnp.arange(terms, dtype=jnp.int32)[:, None]
    products, factors, valid = [], [], []
    for chosen_t, is_valid in ((first, active), (last, last > first)):
        before = active[:, None, :] & (column < chosen_t[:, :, None])
        products.append(base + jnp.sum(jnp.where(before, 1, 0), 2))
        factors.append(jnp.sum(jnp.where(column == chosen_t[:, :, None], coupled, 0.0), 2))
        valid.append(is_valid)
    products = jnp.concatenate(products, 0)
    factors = jnp.concatenate(factors, 0)
    valid = jnp.concatenate(valid, 0)
    index = jnp.arange(2 * terms, dtype=jnp.int32)
    order = index[None, :] < index[:, None]
    rank = jnp.sum(jnp.where(valid[None] & order[:, :, None], 1, 0), 1)
    place = jnp.arange(MOST, dtype=jnp.int32)[:, None, None]
    chosen = valid[None] & (rank[None] == place)
    take = jnp.sum(jnp.where(chosen, products[None], 0), 1)
    factor = jnp.sum(jnp.where(chosen, factors[None], 0.0), 1)
    return sources.reshape(-1), take.T.reshape(-1), factor.T.reshape(-1)


def gather_products(s, take_ref, factor_ref, product_ref, total):
    for n in range(MOST):
        e = s * MOST + n
        total = total + factor_ref[e] * product_ref[take_ref[e]]
    return total


def stencil(pieces, others, halos, lists, j, name, lay):
    rows, width = lay.rows, lay.width
    full = (rows, width)

    def kernel(j_ref, source_ref, take_ref, factor_ref, *refs):
        piece_refs, refs = refs[: lay.modes], refs[lay.modes :]
        other_refs, refs = refs[: lay.modes], refs[lay.modes :]
        halo_refs, refs = refs[: len(halos)], refs[len(halos) :]
        out_refs, (near_ref, product_ref) = refs[: lay.modes], refs[lay.modes :]
        lane = lax.broadcasted_iota(jnp.int32, full, 1)
        line = lax.broadcasted_iota(jnp.int32, full, 0)
        mode = lax.rem(j_ref[0], lay.modes)
        halo_parts = [(ref, n) for ref in halo_refs for n in range(ref.shape[0])]

        for block in range(lay.modes):

            def spread(i, block=block):
                piece_ref = piece_refs[block]
                halo_ref, n = halo_parts[block]
                here = piece_ref[pl.ds(i * rows, rows), :]
                low = piece_ref[pl.ds(lay.main + 2 * i, 1), :]
                high = piece_ref[pl.ds(lay.main + 2 * i + 1, 1), :]
                return (
                    here,
                    pltpu.roll(here, width - 1, 1),
                    pltpu.roll(here, 1, 1),
                    jnp.where(line == rows - 1, high, pltpu.roll(here, rows - 1, 0)),
                    jnp.where(line == 0, low, pltpu.roll(here, 1, 0)),
                    other_refs[block][pl.ds(i * rows, rows), :],
                    halo_ref[n, pl.ds(i * rows, rows), :],
                )

            def keep(at, values):
                for n, value in enumerate(values):
                    near_ref[at, n] = value

            def keep_slot(i, values, block=block):
                keep(block * lay.quota + i, values)

            grouped(0, lay.quota, spread, keep_slot)
            for i in range(lay.quota, lay.fields):
                keep(lay.place(block, i), spread(i))

        def operator_of(term):
            at = lay.term_place(term, mode)
            here, right, left, *rest = [near_ref[at, n] for n in range(7)]
            right = jnp.where(lane == width - 1, 0.0, right)
            left = jnp.where(lane == 0, 0.0, left)
            faces = [0.5 * (here + n) for n in (right, left, *rest)]
            diagonal = faces[0] + faces[1] + faces[2] + faces[3] + faces[4] + faces[5]
            faces[0] = jnp.where(lane == width - 1, 0.0, faces[0])
            faces[1] = jnp.where(lane == 0, 0.0, faces[1])

            def operator(t):
                total = diagonal * near_ref[t, 0]
                for n, face in enumerate(faces):
                    total = total - face * near_ref[t, n + 1]
                return total

            return operator

        def keep_product(e, value):
            product_ref[e] = value

        for term in range(1, lay.terms):
            operator = operator_of(term)
            grouped(
                (term - 1) * ACTIVE,
                ACTIVE,
                lambda e, operator=operator: operator(source_ref[e]),
                keep_product,
            )

        operator = operator_of(0)
        for block in range(lay.modes):

            def collect(i, block=block):
                s = block * lay.quota + i
                return gather_products(s, take_ref, factor_ref, product_ref, operator(s))

            def keep_out(i, value, out_ref=out_refs[block]):
                out_ref[i] = value

            grouped(0, lay.quota, collect, keep_out)

    return pl.pallas_call(
        kernel,
        out_shape=[jax.ShapeDtypeStruct((lay.quota, rows, width), jnp.float32)] * lay.modes,
        in_specs=smem(4) + vmem(2 * lay.modes + len(halos)),
        out_specs=vmem(lay.modes),
        scratch_shapes=[
            pltpu.VMEM((lay.places, 7, rows, width), jnp.float32),
            pltpu.VMEM(((lay.terms - 1) * ACTIVE, rows, width), jnp.float32),
        ],
        compiler_params=pltpu.CompilerParams(vmem_limit_bytes=VMEM_LIMIT),
        name=name,
    )(j, *lists, *pieces, *others, *halos)


def grouped(first, count, compute, store):
    size = max(n for n in range(1, GROUP + 1) if count % n == 0)

    def step(g, carry):
        numbers = [first + g * size + n for n in range(size)]
        values = [compute(n) for n in numbers]
        for n, value in zip(numbers, values):
            store(n, value)
        return carry

    lax.fori_loop(0, count // size, step, 0)


def after(value, *done):
    return lax.optimization_barrier((value, *done))[0]


def on_device(chaos_field, mean_field, kl_fields, pattern, coupling, slot_mode):
    spaces, modes = lax.axis_size("space"), lax.axis_size("mode")
    quota, _, height, width = chaos_field.shape
    terms = kl_fields.shape[0] + 1
    lay = Layout(quota, terms, modes, height, width)
    axes = ("space", "mode")
    devices = spaces * modes
    space = lax.axis_index("space").astype(jnp.int32)
    mode = lax.axis_index("mode").astype(jnp.int32)
    j = (lax.rem(space, PLANES) * modes + mode).reshape(1)

    def swap(piece, r):
        if r == 0:
            return piece
        return lax.ppermute(piece, axes, [(d, d ^ r) for d in range(devices)])

    def shift(pieces, crossing):
        pairs = []
        for d in range(devices):
            upper = (d // modes) % PLANES == (0 if crossing else 1)
            other = d + lay.group if upper else d - lay.group
            if 0 <= other < devices:
                pairs.append((d, other))
        main = jnp.stack([piece[: lay.main] for piece in pieces])
        return lax.ppermute(main, axes, pairs)

    field, kl = chaos_field[:, 0], kl_fields[:, 0]
    sent = [None] * lay.group
    sent[:modes] = pack(field, mean_field, kl, j, False, lay)
    sent[modes:] = pack(field, mean_field, kl, after(j, *sent[:modes]), True, lay)
    half = modes // 2
    pieces = sent[:1] + [None] * (lay.group - 1)
    for r in [*range(half, modes), *range(1, half), *range(modes, modes + half)]:
        pieces[r] = swap(sent[r], r)
    for r in range(modes + half, lay.group):
        pieces[r] = swap(after(sent[r], *pieces[half:modes]), r)
    number = jnp.arange(modes, dtype=jnp.int32)
    mine = jnp.bitwise_xor(number, mode)[:, None, None] == number[None, :, None]
    slot_mode = jnp.sum(jnp.where(mine, slot_mode.reshape(1, modes, quota), 0), 1).reshape(-1)
    lists = coupling_lists(pattern, coupling, slot_mode)
    pieces[half] = after(pieces[half], *lists)
    own_halo = shift(pieces[:modes], False)
    halos = [shift(pieces[r : r + half], True) for r in (modes, modes + half)]

    own, crossing = pieces[:modes], pieces[modes:]
    crossing_out = stencil(crossing, own, [own_halo], lists, j, "stencil_crossing", lay)
    own_j = after(j, *crossing_out)
    own_out = stencil(own, crossing, halos, lists, own_j, "stencil_own", lay)
    out = [*own_out, *crossing_out]
    for r in range(modes, modes + half):
        out[r] = after(out[r], *own_out)
    first = [*range(modes + half, lay.group)]
    rest = [r + n for n in range(half) for r in (half, modes)] + [*range(half)]
    back = {r: swap(out[r], r) for r in first + rest}
    return unpack(back, j, (quota, height, width), lay).reshape(chaos_field.shape)


def solution(mesh):
    in_specs = (
        P("mode", "space", None, None),
        P("space", None, None),
        P(None, "space", None, None),
        P(),
        P(),
        P(),
    )
    out_specs = P("mode", "space", None, None)
    return jax.shard_map(
        on_device, mesh=mesh, in_specs=in_specs, out_specs=out_specs, check_vma=False
    )
```

```python
import jax
import jax.numpy as jnp
from jax import lax
from jax.experimental import pallas as pl
from jax.experimental.pallas import tpu as pltpu
from jax.sharding import PartitionSpec as P

VMEM_LIMIT = 40 * 1024 * 1024
PLANES = 2
ACTIVE = 49
MOST = 8
GROUP = 7


class Layout:
    def __init__(self, quota, terms, modes, height, width):
        self.modes = modes
        self.group = PLANES * modes
        self.rows = height // self.group
        self.width = width
        self.terms = terms
        self.quota = quota
        self.slots = quota * modes
        self.share = -(-terms // modes)
        self.fields = quota + self.share
        self.main = self.fields * self.rows
        self.parts = self.fields + -(-2 * self.fields // self.rows)
        self.piece = self.parts * self.rows
        self.places = self.fields * modes

    def edge(self, i):
        return self.fields + 2 * i // self.rows, 2 * i % self.rows

    def place(self, block, i):
        if i < self.quota:
            return block * self.quota + i
        return self.slots + block * self.share + (i - self.quota)

    def term_place(self, term, mode):
        block = jnp.bitwise_xor(term // self.share, mode)
        return self.slots + block * self.share + term % self.share


def vmem(count):
    return [pl.BlockSpec(memory_space=pltpu.VMEM)] * count


def smem(count):
    return [pl.BlockSpec(memory_space=pltpu.SMEM)] * count


def pack(field, mean, kl, j, lay):
    kl_terms = kl.shape[0]
    rows, width, quota = lay.rows, lay.width, lay.quota

    def kernel(j_ref, field_ref, mean_ref, kl_ref, *refs):
        out_refs, (stage_ref, sems) = refs[: lay.group], refs[lay.group :]
        mode = lax.rem(j_ref[0], lay.modes)

        def load(n, begin=True):
            at, target = pl.ds(n * rows, rows), stage_ref.at[n]
            copies = [
                pltpu.make_async_copy(
                    field_ref.at[:, at, :], target.at[pl.ds(0, quota)], sems.at[n, 0]
                )
            ]
            if begin:
                copies[0].start()
            for i in range(lay.share):
                term = mode * lay.share + i
                into, sem = target.at[quota + i], sems.at[n, 1 + i]
                if not begin:
                    copies.append(pltpu.make_async_copy(mean_ref.at[0, at, :], into, sem))
                    continue

                @pl.when(term == 0)
                def _():
                    pltpu.make_async_copy(mean_ref.at[0, at, :], into, sem).start()

                @pl.when(term > 0)
                def _():
                    source = kl_ref.at[jnp.clip(term - 1, 0, kl_terms - 1), at, :]
                    pltpu.make_async_copy(source, into, sem).start()

            return copies

        for n in range(lay.group):
            load(n)
        for n in range(lay.group):
            for made in load(n, begin=False):
                made.wait()
        none = jnp.zeros((1, width), jnp.float32)
        for n in range(lay.group):
            for i in range(lay.fields):
                part, line = lay.edge(i)
                low = stage_ref[n - 1, i, rows - 1 :] if n > 0 else none
                high = stage_ref[n + 1, i, :1] if n < lay.group - 1 else none
                stage_ref[n, part, line : line + 1] = low
                stage_ref[n, part, line + 1 : line + 2] = high
            part, line = lay.edge(lay.fields)
            if part < lay.parts:
                stage_ref[n, part, line:] = jnp.zeros((rows - line, width), jnp.float32)
        for r, out_ref in enumerate(out_refs):
            to = jnp.bitwise_xor(j_ref[0], r)
            for part in range(lay.parts):
                out_ref[part] = stage_ref[to, part]

    shape = (lay.parts, rows, width)
    sent = pl.pallas_call(
        kernel,
        out_shape=[pltpu.VMEM(shape, jnp.float32)] * lay.group,
        in_specs=smem(1) + [pl.BlockSpec(memory_space=pltpu.HBM)] * 3,
        out_specs=vmem(lay.group),
        scratch_shapes=[
            pltpu.VMEM((lay.group, *shape), jnp.float32),
            pltpu.SemaphoreType.DMA((lay.group, 1 + lay.share)),
        ],
        compiler_params=pltpu.CompilerParams(vmem_limit_bytes=VMEM_LIMIT),
        name="pack",
    )(j, *[pltpu.with_memory_space_constraint(x, pltpu.HBM) for x in (field, mean, kl)])
    return [piece.reshape(lay.piece, width) for piece in sent]


def unpack(pieces, j, shape, lay):
    rows = lay.rows

    def kernel(j_ref, *refs):
        piece_refs, out_ref, sems = refs[:-2], refs[-2], refs[-1]
        copies = []
        for r, piece_ref in zip(pieces, piece_refs):
            start = pl.multiple_of(jnp.bitwise_xor(j_ref[0], r) * rows, 8)
            made = pltpu.make_async_copy(
                piece_ref, out_ref.at[:, pl.ds(start, rows), :], sems.at[r]
            )
            made.start()
            copies.append(made)
        for made in copies:
            made.wait()

    return pl.pallas_call(
        kernel,
        out_shape=jax.ShapeDtypeStruct(shape, jnp.float32),
        in_specs=smem(1) + vmem(lay.group),
        out_specs=pl.BlockSpec(memory_space=pltpu.HBM),
        scratch_shapes=[pltpu.SemaphoreType.DMA((lay.group,))],
        compiler_params=pltpu.CompilerParams(vmem_limit_bytes=VMEM_LIMIT),
        name="unpack",
    )(j, *pieces.values())


def coupling_lists(pattern, coupling, slot_mode):
    masked = (coupling * pattern.astype(jnp.float32))[1:]
    terms, modes = masked.shape[0], masked.shape[1]
    number = jnp.arange(modes, dtype=jnp.int32)
    one_hot = (slot_mode[:, None] == number[None, :]).astype(jnp.float32)
    coupled = jnp.einsum(
        "sa,kab,tb->kst", one_hot, masked, one_hot, precision=lax.Precision.HIGHEST
    )
    there = coupled != 0.0
    column = number[None, None, :]
    first = jnp.min(jnp.where(there, column, modes), 2)
    last = jnp.max(jnp.where(there, column, -1), 2)
    active = first < modes
    earlier = column < number[None, :, None]
    rank = jnp.sum(jnp.where(active[:, None, :] & earlier, 1, 0), 2)
    place = jnp.arange(ACTIVE, dtype=jnp.int32)[None, :, None]
    chosen = active[:, None, :] & (rank[:, None, :] == place)
    sources = jnp.sum(jnp.where(chosen, column, 0), 2)

    base = ACTIVE * jnp.arange(terms, dtype=jnp.int32)[:, None]
    products, factors, valid = [], [], []
    for chosen_t, is_valid in ((first, active), (last, last > first)):
        before = active[:, None, :] & (column < chosen_t[:, :, None])
        products.append(base + jnp.sum(jnp.where(before, 1, 0), 2))
        factors.append(jnp.sum(jnp.where(column == chosen_t[:, :, None], coupled, 0.0), 2))
        valid.append(is_valid)
    products = jnp.concatenate(products, 0)
    factors = jnp.concatenate(factors, 0)
    valid = jnp.concatenate(valid, 0)
    index = jnp.arange(2 * terms, dtype=jnp.int32)
    order = index[None, :] < index[:, None]
    rank = jnp.sum(jnp.where(valid[None] & order[:, :, None], 1, 0), 1)
    place = jnp.arange(MOST, dtype=jnp.int32)[:, None, None]
    chosen = valid[None] & (rank[None] == place)
    take = jnp.sum(jnp.where(chosen, products[None], 0), 1)
    factor = jnp.sum(jnp.where(chosen, factors[None], 0.0), 1)
    return sources.reshape(-1), take.T.reshape(-1), factor.T.reshape(-1)


def gather_products(s, take_ref, factor_ref, product_ref, total):
    for n in range(MOST):
        e = s * MOST + n
        total = total + factor_ref[e] * product_ref[take_ref[e]]
    return total


def stencil(pieces, others, halos, lists, j, name, lay):
    rows, width = lay.rows, lay.width
    full = (rows, width)

    def kernel(j_ref, source_ref, take_ref, factor_ref, *refs):
        piece_refs, refs = refs[: lay.modes], refs[lay.modes :]
        other_refs, refs = refs[: lay.modes], refs[lay.modes :]
        halo_refs, refs = refs[: len(halos)], refs[len(halos) :]
        out_refs, (near_ref, product_ref) = refs[: lay.modes], refs[lay.modes :]
        lane = lax.broadcasted_iota(jnp.int32, full, 1)
        line = lax.broadcasted_iota(jnp.int32, full, 0)
        mode = lax.rem(j_ref[0], lay.modes)
        halo_parts = [(ref, n) for ref in halo_refs for n in range(ref.shape[0])]

        for block in range(lay.modes):

            def spread(i, block=block):
                piece_ref = piece_refs[block]
                halo_ref, n = halo_parts[block]
                here = piece_ref[pl.ds(i * rows, rows), :]
                low = piece_ref[pl.ds(lay.main + 2 * i, 1), :]
                high = piece_ref[pl.ds(lay.main + 2 * i + 1, 1), :]
                return (
                    here,
                    pltpu.roll(here, width - 1, 1),
                    pltpu.roll(here, 1, 1),
                    jnp.where(line == rows - 1, high, pltpu.roll(here, rows - 1, 0)),
                    jnp.where(line == 0, low, pltpu.roll(here, 1, 0)),
                    other_refs[block][pl.ds(i * rows, rows), :],
                    halo_ref[n, pl.ds(i * rows, rows), :],
                )

            def keep(at, values):
                for n, value in enumerate(values):
                    near_ref[at, n] = value

            def keep_slot(i, values, block=block):
                keep(block * lay.quota + i, values)

            grouped(0, lay.quota, spread, keep_slot)
            for i in range(lay.quota, lay.fields):
                keep(lay.place(block, i), spread(i))

        def operator_of(term):
            at = lay.term_place(term, mode)
            here, right, left, *rest = [near_ref[at, n] for n in range(7)]
            right = jnp.where(lane == width - 1, 0.0, right)
            left = jnp.where(lane == 0, 0.0, left)
            faces = [0.5 * (here + n) for n in (right, left, *rest)]
            diagonal = faces[0] + faces[1] + faces[2] + faces[3] + faces[4] + faces[5]
            faces[0] = jnp.where(lane == width - 1, 0.0, faces[0])
            faces[1] = jnp.where(lane == 0, 0.0, faces[1])

            def operator(t):
                total = diagonal * near_ref[t, 0]
                for n, face in enumerate(faces):
                    total = total - face * near_ref[t, n + 1]
                return total

            return operator

        def keep_product(e, value):
            product_ref[e] = value

        for term in range(1, lay.terms):
            operator = operator_of(term)
            grouped(
                (term - 1) * ACTIVE,
                ACTIVE,
                lambda e, operator=operator: operator(source_ref[e]),
                keep_product,
            )

        operator = operator_of(0)
        for block in range(lay.modes):

            def collect(i, block=block):
                s = block * lay.quota + i
                return gather_products(s, take_ref, factor_ref, product_ref, operator(s))

            def keep_out(i, value, out_ref=out_refs[block]):
                out_ref[i] = value

            grouped(0, lay.quota, collect, keep_out)

    return pl.pallas_call(
        kernel,
        out_shape=[jax.ShapeDtypeStruct((lay.quota, rows, width), jnp.float32)] * lay.modes,
        in_specs=smem(4) + vmem(2 * lay.modes + len(halos)),
        out_specs=vmem(lay.modes),
        scratch_shapes=[
            pltpu.VMEM((lay.places, 7, rows, width), jnp.float32),
            pltpu.VMEM(((lay.terms - 1) * ACTIVE, rows, width), jnp.float32),
        ],
        compiler_params=pltpu.CompilerParams(vmem_limit_bytes=VMEM_LIMIT),
        name=name,
    )(j, *lists, *pieces, *others, *halos)


def grouped(first, count, compute, store):
    size = max(n for n in range(1, GROUP + 1) if count % n == 0)

    def step(g, carry):
        numbers = [first + g * size + n for n in range(size)]
        values = [compute(n) for n in numbers]
        for n, value in zip(numbers, values):
            store(n, value)
        return carry

    lax.fori_loop(0, count // size, step, 0)


def after(value, *done):
    return lax.optimization_barrier((value, *done))[0]


def on_device(chaos_field, mean_field, kl_fields, pattern, coupling, slot_mode):
    spaces, modes = lax.axis_size("space"), lax.axis_size("mode")
    quota, _, height, width = chaos_field.shape
    terms = kl_fields.shape[0] + 1
    lay = Layout(quota, terms, modes, height, width)
    axes = ("space", "mode")
    devices = spaces * modes
    space = lax.axis_index("space").astype(jnp.int32)
    mode = lax.axis_index("mode").astype(jnp.int32)
    j = (lax.rem(space, PLANES) * modes + mode).reshape(1)

    def swap(piece, r):
        if r == 0:
            return piece
        return lax.ppermute(piece, axes, [(d, d ^ r) for d in range(devices)])

    def shift(pieces, crossing):
        pairs = []
        for d in range(devices):
            upper = (d // modes) % PLANES == (0 if crossing else 1)
            other = d + lay.group if upper else d - lay.group
            if 0 <= other < devices:
                pairs.append((d, other))
        main = jnp.stack([piece[: lay.main] for piece in pieces])
        return lax.ppermute(main, axes, pairs)

    field, kl = chaos_field[:, 0], kl_fields[:, 0]
    sent = pack(field, mean_field, kl, j, lay)
    half = modes // 2
    pieces = sent[:1] + [None] * (lay.group - 1)
    for r in [modes, half, *range(1, half), *range(half + 1, modes)]:
        pieces[r] = swap(sent[r], r)
    for r in range(modes + 1, modes + half):
        pieces[r] = swap(after(sent[r], *pieces[1:half]), r)
    halos = [shift(pieces[:1], False)]
    for r in range(modes + half, lay.group):
        pieces[r] = swap(after(sent[r], *pieces[half : modes + half], halos[0]), r)
    number = jnp.arange(modes, dtype=jnp.int32)
    mine = jnp.bitwise_xor(number, mode)[:, None, None] == number[None, :, None]
    slot_mode = jnp.sum(jnp.where(mine, slot_mode.reshape(1, modes, quota), 0), 1).reshape(-1)
    lists = coupling_lists(pattern, coupling, after(slot_mode, pieces[modes + 1]))
    pieces[modes + half] = after(pieces[modes + half], *lists)
    halos.append(shift(pieces[1:modes], False))
    halos.append(shift(pieces[modes : modes + half], True))
    halos.append(shift(pieces[modes + half :], True))

    own, crossing = pieces[:modes], pieces[modes:]
    crossing_out = stencil(crossing, own, halos[:2], lists, j, "stencil_crossing", lay)
    own_j = after(j, *crossing_out)
    own_out = stencil(own, crossing, halos[2:], lists, own_j, "stencil_own", lay)
    out = [*own_out, *crossing_out]
    for r in range(modes, modes + half):
        out[r] = after(out[r], *own_out)
    first = [*range(modes + half, lay.group)]
    rest = [r + n for n in range(half) for r in (half, modes)] + [*range(half)]
    back = {r: swap(out[r], r) for r in first + rest}
    return unpack(back, j, (quota, height, width), lay).reshape(chaos_field.shape)


def solution(mesh):
    in_specs = (
        P("mode", "space", None, None),
        P("space", None, None),
        P(None, "space", None, None),
        P(),
        P(),
        P(),
    )
    out_specs = P("mode", "space", None, None)
    return jax.shard_map(
        on_device, mesh=mesh, in_specs=in_specs, out_specs=out_specs, check_vma=False
    )
```

```python
import jax
import jax.numpy as jnp
from jax import lax
from jax.experimental import pallas as pl
from jax.experimental.pallas import tpu as pltpu
from jax.sharding import PartitionSpec as P

VMEM_LIMIT = 40 * 1024 * 1024
PLANES = 2
ACTIVE = 49
MOST = 8
GROUP = 7


class Layout:
    def __init__(self, quota, terms, modes, height, width):
        self.modes = modes
        self.group = PLANES * modes
        self.rows = height // self.group
        self.width = width
        self.terms = terms
        self.quota = quota
        self.slots = quota * modes
        self.share = -(-terms // modes)
        self.fields = quota + self.share
        self.main = self.fields * self.rows
        self.parts = self.fields + -(-2 * self.fields // self.rows)
        self.piece = self.parts * self.rows
        self.places = self.fields * modes

    def edge(self, i):
        return self.fields + 2 * i // self.rows, 2 * i % self.rows

    def place(self, block, i):
        if i < self.quota:
            return block * self.quota + i
        return self.slots + block * self.share + (i - self.quota)

    def term_place(self, term, mode):
        block = jnp.bitwise_xor(term // self.share, mode)
        return self.slots + block * self.share + term % self.share


def vmem(count):
    return [pl.BlockSpec(memory_space=pltpu.VMEM)] * count


def smem(count):
    return [pl.BlockSpec(memory_space=pltpu.SMEM)] * count


def pack(field, mean, kl, j, lay):
    kl_terms = kl.shape[0]
    rows, width, quota = lay.rows, lay.width, lay.quota

    def kernel(j_ref, field_ref, mean_ref, kl_ref, *refs):
        out_refs, (stage_ref, sems) = refs[: lay.group], refs[lay.group :]
        mode = lax.rem(j_ref[0], lay.modes)

        def load(n, begin=True):
            at, target = pl.ds(n * rows, rows), stage_ref.at[n]
            copies = [
                pltpu.make_async_copy(
                    field_ref.at[:, at, :], target.at[pl.ds(0, quota)], sems.at[n, 0]
                )
            ]
            if begin:
                copies[0].start()
            for i in range(lay.share):
                term = mode * lay.share + i
                into, sem = target.at[quota + i], sems.at[n, 1 + i]
                if not begin:
                    copies.append(pltpu.make_async_copy(mean_ref.at[0, at, :], into, sem))
                    continue

                @pl.when(term == 0)
                def _():
                    pltpu.make_async_copy(mean_ref.at[0, at, :], into, sem).start()

                @pl.when(term > 0)
                def _():
                    source = kl_ref.at[jnp.clip(term - 1, 0, kl_terms - 1), at, :]
                    pltpu.make_async_copy(source, into, sem).start()

            return copies

        for n in range(lay.group):
            load(n)
        for n in range(lay.group):
            for made in load(n, begin=False):
                made.wait()
        none = jnp.zeros((1, width), jnp.float32)
        for n in range(lay.group):
            for i in range(lay.fields):
                part, line = lay.edge(i)
                low = stage_ref[n - 1, i, rows - 1 :] if n > 0 else none
                high = stage_ref[n + 1, i, :1] if n < lay.group - 1 else none
                stage_ref[n, part, line : line + 1] = low
                stage_ref[n, part, line + 1 : line + 2] = high
            part, line = lay.edge(lay.fields)
            if part < lay.parts:
                stage_ref[n, part, line:] = jnp.zeros((rows - line, width), jnp.float32)
        for r, out_ref in enumerate(out_refs):
            to = jnp.bitwise_xor(j_ref[0], r)
            for part in range(lay.parts):
                out_ref[part] = stage_ref[to, part]

    shape = (lay.parts, rows, width)
    sent = pl.pallas_call(
        kernel,
        out_shape=[pltpu.VMEM(shape, jnp.float32)] * lay.group,
        in_specs=smem(1) + [pl.BlockSpec(memory_space=pltpu.HBM)] * 3,
        out_specs=vmem(lay.group),
        scratch_shapes=[
            pltpu.VMEM((lay.group, *shape), jnp.float32),
            pltpu.SemaphoreType.DMA((lay.group, 1 + lay.share)),
        ],
        compiler_params=pltpu.CompilerParams(vmem_limit_bytes=VMEM_LIMIT),
        name="pack",
    )(j, *[pltpu.with_memory_space_constraint(x, pltpu.HBM) for x in (field, mean, kl)])
    return [piece.reshape(lay.piece, width) for piece in sent]


def unpack(pieces, j, shape, lay):
    rows = lay.rows

    def kernel(j_ref, *refs):
        piece_refs, out_ref, sems = refs[:-2], refs[-2], refs[-1]
        copies = []
        for r, piece_ref in zip(pieces, piece_refs):
            start = pl.multiple_of(jnp.bitwise_xor(j_ref[0], r) * rows, 8)
            made = pltpu.make_async_copy(
                piece_ref, out_ref.at[:, pl.ds(start, rows), :], sems.at[r]
            )
            made.start()
            copies.append(made)
        for made in copies:
            made.wait()

    return pl.pallas_call(
        kernel,
        out_shape=jax.ShapeDtypeStruct(shape, jnp.float32),
        in_specs=smem(1) + vmem(lay.group),
        out_specs=pl.BlockSpec(memory_space=pltpu.HBM),
        scratch_shapes=[pltpu.SemaphoreType.DMA((lay.group,))],
        compiler_params=pltpu.CompilerParams(vmem_limit_bytes=VMEM_LIMIT),
        name="unpack",
    )(j, *pieces.values())


def coupling_lists(pattern, coupling, slot_mode):
    masked = (coupling * pattern.astype(jnp.float32))[1:]
    terms, modes = masked.shape[0], masked.shape[1]
    number = jnp.arange(modes, dtype=jnp.int32)
    one_hot = (slot_mode[:, None] == number[None, :]).astype(jnp.float32)
    coupled = jnp.einsum(
        "sa,kab,tb->kst", one_hot, masked, one_hot, precision=lax.Precision.HIGHEST
    )
    there = coupled != 0.0
    column = number[None, None, :]
    first = jnp.min(jnp.where(there, column, modes), 2)
    last = jnp.max(jnp.where(there, column, -1), 2)
    active = first < modes
    earlier = column < number[None, :, None]
    rank = jnp.sum(jnp.where(active[:, None, :] & earlier, 1, 0), 2)
    place = jnp.arange(ACTIVE, dtype=jnp.int32)[None, :, None]
    chosen = active[:, None, :] & (rank[:, None, :] == place)
    sources = jnp.sum(jnp.where(chosen, column, 0), 2)

    base = ACTIVE * jnp.arange(terms, dtype=jnp.int32)[:, None]
    products, factors, valid = [], [], []
    for chosen_t, is_valid in ((first, active), (last, last > first)):
        before = active[:, None, :] & (column < chosen_t[:, :, None])
        products.append(base + jnp.sum(jnp.where(before, 1, 0), 2))
        factors.append(jnp.sum(jnp.where(column == chosen_t[:, :, None], coupled, 0.0), 2))
        valid.append(is_valid)
    products = jnp.concatenate(products, 0)
    factors = jnp.concatenate(factors, 0)
    valid = jnp.concatenate(valid, 0)
    index = jnp.arange(2 * terms, dtype=jnp.int32)
    order = index[None, :] < index[:, None]
    rank = jnp.sum(jnp.where(valid[None] & order[:, :, None], 1, 0), 1)
    place = jnp.arange(MOST, dtype=jnp.int32)[:, None, None]
    chosen = valid[None] & (rank[None] == place)
    take = jnp.sum(jnp.where(chosen, products[None], 0), 1)
    factor = jnp.sum(jnp.where(chosen, factors[None], 0.0), 1)
    return sources.reshape(-1), take.T.reshape(-1), factor.T.reshape(-1)


def gather_products(s, take_ref, factor_ref, product_ref, total):
    for n in range(MOST):
        e = s * MOST + n
        total = total + factor_ref[e] * product_ref[take_ref[e]]
    return total


def stencil(pieces, others, halos, lists, j, name, lay):
    rows, width = lay.rows, lay.width
    full = (rows, width)

    def kernel(j_ref, source_ref, take_ref, factor_ref, *refs):
        piece_refs, refs = refs[: lay.modes], refs[lay.modes :]
        other_refs, refs = refs[: lay.modes], refs[lay.modes :]
        halo_refs, refs = refs[: len(halos)], refs[len(halos) :]
        out_refs, (near_ref, product_ref) = refs[: lay.modes], refs[lay.modes :]
        lane = lax.broadcasted_iota(jnp.int32, full, 1)
        line = lax.broadcasted_iota(jnp.int32, full, 0)
        mode = lax.rem(j_ref[0], lay.modes)
        halo_parts = [(ref, n) for ref in halo_refs for n in range(ref.shape[0])]

        for block in range(lay.modes):

            def spread(i, block=block):
                piece_ref = piece_refs[block]
                halo_ref, n = halo_parts[block]
                here = piece_ref[pl.ds(i * rows, rows), :]
                low = piece_ref[pl.ds(lay.main + 2 * i, 1), :]
                high = piece_ref[pl.ds(lay.main + 2 * i + 1, 1), :]
                return (
                    here,
                    pltpu.roll(here, width - 1, 1),
                    pltpu.roll(here, 1, 1),
                    jnp.where(line == rows - 1, high, pltpu.roll(here, rows - 1, 0)),
                    jnp.where(line == 0, low, pltpu.roll(here, 1, 0)),
                    other_refs[block][pl.ds(i * rows, rows), :],
                    halo_ref[n, pl.ds(i * rows, rows), :],
                )

            def keep(at, values):
                for n, value in enumerate(values):
                    near_ref[at, n] = value

            def keep_slot(i, values, block=block):
                keep(block * lay.quota + i, values)

            grouped(0, lay.quota, spread, keep_slot)
            for i in range(lay.quota, lay.fields):
                keep(lay.place(block, i), spread(i))

        def operator_of(term):
            at = lay.term_place(term, mode)
            here, right, left, *rest = [near_ref[at, n] for n in range(7)]
            right = jnp.where(lane == width - 1, 0.0, right)
            left = jnp.where(lane == 0, 0.0, left)
            faces = [0.5 * (here + n) for n in (right, left, *rest)]
            diagonal = faces[0] + faces[1] + faces[2] + faces[3] + faces[4] + faces[5]
            faces[0] = jnp.where(lane == width - 1, 0.0, faces[0])
            faces[1] = jnp.where(lane == 0, 0.0, faces[1])

            def operator(t):
                total = diagonal * near_ref[t, 0]
                for n, face in enumerate(faces):
                    total = total - face * near_ref[t, n + 1]
                return total

            return operator

        def keep_product(e, value):
            product_ref[e] = value

        for term in range(1, lay.terms):
            operator = operator_of(term)
            grouped(
                (term - 1) * ACTIVE,
                ACTIVE,
                lambda e, operator=operator: operator(source_ref[e]),
                keep_product,
            )

        operator = operator_of(0)
        for block in range(lay.modes):

            def collect(i, block=block):
                s = block * lay.quota + i
                return gather_products(s, take_ref, factor_ref, product_ref, operator(s))

            def keep_out(i, value, out_ref=out_refs[block]):
                out_ref[i] = value

            grouped(0, lay.quota, collect, keep_out)

    return pl.pallas_call(
        kernel,
        out_shape=[jax.ShapeDtypeStruct((lay.quota, rows, width), jnp.float32)] * lay.modes,
        in_specs=smem(4) + vmem(2 * lay.modes + len(halos)),
        out_specs=vmem(lay.modes),
        scratch_shapes=[
            pltpu.VMEM((lay.places, 7, rows, width), jnp.float32),
            pltpu.VMEM(((lay.terms - 1) * ACTIVE, rows, width), jnp.float32),
        ],
        compiler_params=pltpu.CompilerParams(vmem_limit_bytes=VMEM_LIMIT),
        name=name,
    )(j, *lists, *pieces, *others, *halos)


def grouped(first, count, compute, store):
    size = max(n for n in range(1, GROUP + 1) if count % n == 0)

    def step(g, carry):
        numbers = [first + g * size + n for n in range(size)]
        values = [compute(n) for n in numbers]
        for n, value in zip(numbers, values):
            store(n, value)
        return carry

    lax.fori_loop(0, count // size, step, 0)


def after(value, *done):
    return lax.optimization_barrier((value, *done))[0]


def on_device(chaos_field, mean_field, kl_fields, pattern, coupling, slot_mode):
    spaces, modes = lax.axis_size("space"), lax.axis_size("mode")
    quota, _, height, width = chaos_field.shape
    terms = kl_fields.shape[0] + 1
    lay = Layout(quota, terms, modes, height, width)
    axes = ("space", "mode")
    devices = spaces * modes
    space = lax.axis_index("space").astype(jnp.int32)
    mode = lax.axis_index("mode").astype(jnp.int32)
    j = (lax.rem(space, PLANES) * modes + mode).reshape(1)

    def swap(piece, r):
        if r == 0:
            return piece
        return lax.ppermute(piece, axes, [(d, d ^ r) for d in range(devices)])

    def shift(pieces, crossing):
        pairs = []
        for d in range(devices):
            upper = (d // modes) % PLANES == (0 if crossing else 1)
            other = d + lay.group if upper else d - lay.group
            if 0 <= other < devices:
                pairs.append((d, other))
        main = jnp.stack([piece[: lay.main] for piece in pieces])
        return lax.ppermute(main, axes, pairs)

    field, kl = chaos_field[:, 0], kl_fields[:, 0]
    sent = pack(field, mean_field, kl, j, lay)
    half = modes // 2
    pieces = sent[:1] + [None] * (lay.group - 1)
    for r in [half, modes, *range(half + 1, modes), *range(modes + 1, modes + half), *range(1, half)]:
        pieces[r] = swap(sent[r], r)
    halos = [shift(pieces[:1], False)]
    for r in range(modes + half, lay.group):
        pieces[r] = swap(after(sent[r], *pieces[half:modes], halos[0]), r)
    number = jnp.arange(modes, dtype=jnp.int32)
    mine = jnp.bitwise_xor(number, mode)[:, None, None] == number[None, :, None]
    slot_mode = jnp.sum(jnp.where(mine, slot_mode.reshape(1, modes, quota), 0), 1).reshape(-1)
    lists = coupling_lists(pattern, coupling, after(slot_mode, pieces[modes]))
    pieces[modes + half] = after(pieces[modes + half], *lists)
    halos.append(shift(pieces[1:modes], False))
    halos += [shift(pieces[r : r + half], True) for r in (modes, modes + half)]

    own, crossing = pieces[:modes], pieces[modes:]
    crossing_out = stencil(crossing, own, halos[:2], lists, j, "stencil_crossing", lay)
    own_j = after(j, *crossing_out)
    own_out = stencil(own, crossing, halos[2:], lists, own_j, "stencil_own", lay)
    out = [*own_out, *crossing_out]
    for r in range(modes, modes + half):
        out[r] = after(out[r], *own_out)
    first = [*range(modes + half, lay.group)]
    rest = [r + n for n in range(half) for r in (half, modes)] + [*range(half)]
    back = {r: swap(out[r], r) for r in first + rest}
    return unpack(back, j, (quota, height, width), lay).reshape(chaos_field.shape)


def solution(mesh):
    in_specs = (
        P("mode", "space", None, None),
        P("space", None, None),
        P(None, "space", None, None),
        P(),
        P(),
        P(),
    )
    out_specs = P("mode", "space", None, None)
    return jax.shard_map(
        on_device, mesh=mesh, in_specs=in_specs, out_specs=out_specs, check_vma=False
    )
```

```python
import jax
import jax.numpy as jnp
from jax import lax
from jax.experimental import pallas as pl
from jax.experimental.pallas import tpu as pltpu
from jax.sharding import PartitionSpec as P

VMEM_LIMIT = 40 * 1024 * 1024
PLANES = 2
CORES = 2
ACTIVE = 49
MOST = 8
GROUP = 7


class Layout:
    def __init__(self, quota, terms, modes, height, width):
        self.modes = modes
        self.group = PLANES * modes
        self.rows = height // self.group
        self.width = width
        self.terms = terms
        self.quota = quota
        self.slots = quota * modes
        self.share = -(-terms // modes)
        self.fields = quota + self.share
        self.main = self.fields * self.rows
        self.parts = self.fields + -(-2 * self.fields // self.rows)
        self.piece = self.parts * self.rows
        self.places = self.fields * modes

    def edge(self, i):
        return self.fields + 2 * i // self.rows, 2 * i % self.rows

    def place(self, block, i):
        if i < self.quota:
            return block * self.quota + i
        return self.slots + block * self.share + (i - self.quota)

    def term_place(self, term, mode):
        block = jnp.bitwise_xor(term // self.share, mode)
        return self.slots + block * self.share + term % self.share


def vmem(count):
    return [pl.BlockSpec(memory_space=pltpu.VMEM)] * count


def smem(count):
    return [pl.BlockSpec(memory_space=pltpu.SMEM)] * count


def pack(field, mean, kl, j, lay):
    kl_terms = kl.shape[0]
    rows, width, quota = lay.rows, lay.width, lay.quota

    def kernel(j_ref, field_ref, mean_ref, kl_ref, *refs):
        out_refs, (halo_ref, stage_ref, sems) = refs[: lay.group], refs[lay.group :]
        mode = lax.rem(j_ref[0], lay.modes)

        def load(n, begin=True):
            at, target = pl.ds(n * rows, rows), stage_ref.at[n]
            copies = [
                pltpu.make_async_copy(
                    field_ref.at[:, at, :], target.at[pl.ds(0, quota)], sems.at[n, 0]
                )
            ]
            if begin:
                copies[0].start()
            for i in range(lay.share):
                term = mode * lay.share + i
                into, sem = target.at[quota + i], sems.at[n, 1 + i]
                if not begin:
                    copies.append(pltpu.make_async_copy(mean_ref.at[0, at, :], into, sem))
                    continue

                @pl.when(term == 0)
                def _():
                    pltpu.make_async_copy(mean_ref.at[0, at, :], into, sem).start()

                @pl.when(term > 0)
                def _():
                    source = kl_ref.at[jnp.clip(term - 1, 0, kl_terms - 1), at, :]
                    pltpu.make_async_copy(source, into, sem).start()

            return copies

        for n in range(lay.group):
            load(n)
        for n in range(lay.group):
            for made in load(n, begin=False):
                made.wait()
        none = jnp.zeros((1, width), jnp.float32)
        for n in range(lay.group):
            for i in range(lay.fields):
                part, line = lay.edge(i)
                low = stage_ref[n - 1, i, rows - 1 :] if n > 0 else none
                high = stage_ref[n + 1, i, :1] if n < lay.group - 1 else none
                stage_ref[n, part, line : line + 1] = low
                stage_ref[n, part, line + 1 : line + 2] = high
            part, line = lay.edge(lay.fields)
            if part < lay.parts:
                stage_ref[n, part, line:] = jnp.zeros((rows - line, width), jnp.float32)
        for r, out_ref in enumerate(out_refs):
            to = jnp.bitwise_xor(j_ref[0], r)
            for part in range(lay.parts):
                out_ref[part] = stage_ref[to, part]
                if r < CORES and part < lay.fields:
                    halo_ref[r, part] = stage_ref[to, part]

    shape = (lay.parts, rows, width)
    *sent, halo = pl.pallas_call(
        kernel,
        out_shape=[pltpu.VMEM(shape, jnp.float32)] * lay.group
        + [pltpu.VMEM((CORES, lay.fields, rows, width), jnp.float32)],
        in_specs=smem(1) + [pl.BlockSpec(memory_space=pltpu.HBM)] * 3,
        out_specs=vmem(lay.group + 1),
        scratch_shapes=[
            pltpu.VMEM((lay.group, *shape), jnp.float32),
            pltpu.SemaphoreType.DMA((lay.group, 1 + lay.share)),
        ],
        compiler_params=pltpu.CompilerParams(vmem_limit_bytes=VMEM_LIMIT),
        name="pack",
    )(j, *[pltpu.with_memory_space_constraint(x, pltpu.HBM) for x in (field, mean, kl)])
    sent = [piece.reshape(lay.piece, width) for piece in sent]
    return sent, halo.reshape(CORES, lay.main, width)


def unpack(pieces, j, shape, lay):
    rows = lay.rows

    def kernel(j_ref, *refs):
        piece_refs, out_ref, sems = refs[:-2], refs[-2], refs[-1]
        copies = []
        for r, piece_ref in zip(pieces, piece_refs):
            start = pl.multiple_of(jnp.bitwise_xor(j_ref[0], r) * rows, 8)
            made = pltpu.make_async_copy(
                piece_ref, out_ref.at[:, pl.ds(start, rows), :], sems.at[r]
            )
            made.start()
            copies.append(made)
        for made in copies:
            made.wait()

    return pl.pallas_call(
        kernel,
        out_shape=jax.ShapeDtypeStruct(shape, jnp.float32),
        in_specs=smem(1) + vmem(lay.group),
        out_specs=pl.BlockSpec(memory_space=pltpu.HBM),
        scratch_shapes=[pltpu.SemaphoreType.DMA((lay.group,))],
        compiler_params=pltpu.CompilerParams(vmem_limit_bytes=VMEM_LIMIT),
        name="unpack",
    )(j, *pieces.values())


def coupling_lists(pattern, coupling, slot_mode):
    masked = (coupling * pattern.astype(jnp.float32))[1:]
    terms, modes = masked.shape[0], masked.shape[1]
    number = jnp.arange(modes, dtype=jnp.int32)
    one_hot = (slot_mode[:, None] == number[None, :]).astype(jnp.float32)
    coupled = jnp.einsum(
        "sa,kab,tb->kst", one_hot, masked, one_hot, precision=lax.Precision.HIGHEST
    )
    there = coupled != 0.0
    column = number[None, None, :]
    first = jnp.min(jnp.where(there, column, modes), 2)
    last = jnp.max(jnp.where(there, column, -1), 2)
    active = first < modes
    earlier = column < number[None, :, None]
    rank = jnp.sum(jnp.where(active[:, None, :] & earlier, 1, 0), 2)
    place = jnp.arange(ACTIVE, dtype=jnp.int32)[None, :, None]
    chosen = active[:, None, :] & (rank[:, None, :] == place)
    sources = jnp.sum(jnp.where(chosen, column, 0), 2)

    base = ACTIVE * jnp.arange(terms, dtype=jnp.int32)[:, None]
    products, factors, valid = [], [], []
    for chosen_t, is_valid in ((first, active), (last, last > first)):
        before = active[:, None, :] & (column < chosen_t[:, :, None])
        products.append(base + jnp.sum(jnp.where(before, 1, 0), 2))
        factors.append(jnp.sum(jnp.where(column == chosen_t[:, :, None], coupled, 0.0), 2))
        valid.append(is_valid)
    products = jnp.concatenate(products, 0)
    factors = jnp.concatenate(factors, 0)
    valid = jnp.concatenate(valid, 0)
    index = jnp.arange(2 * terms, dtype=jnp.int32)
    order = index[None, :] < index[:, None]
    rank = jnp.sum(jnp.where(valid[None] & order[:, :, None], 1, 0), 1)
    place = jnp.arange(MOST, dtype=jnp.int32)[:, None, None]
    chosen = valid[None] & (rank[None] == place)
    take = jnp.sum(jnp.where(chosen, products[None], 0), 1)
    factor = jnp.sum(jnp.where(chosen, factors[None], 0.0), 1)
    return sources.reshape(-1), take.T.reshape(-1), factor.T.reshape(-1)


def gather_products(s, take_ref, factor_ref, product_ref, total):
    for n in range(MOST):
        e = s * MOST + n
        total = total + factor_ref[e] * product_ref[take_ref[e]]
    return total


def stencil(pieces, others, halos, lists, j, name, lay):
    rows, width = lay.rows, lay.width
    full = (rows, width)

    def kernel(j_ref, source_ref, take_ref, factor_ref, *refs):
        piece_refs, refs = refs[: lay.modes], refs[lay.modes :]
        other_refs, refs = refs[: lay.modes], refs[lay.modes :]
        halo_refs, refs = refs[: len(halos)], refs[len(halos) :]
        out_refs, (near_ref, product_ref) = refs[: lay.modes], refs[lay.modes :]
        lane = lax.broadcasted_iota(jnp.int32, full, 1)
        line = lax.broadcasted_iota(jnp.int32, full, 0)
        mode = lax.rem(j_ref[0], lay.modes)
        halo_parts = [(ref, n) for ref in halo_refs for n in range(ref.shape[0])]

        for block in range(lay.modes):

            def spread(i, block=block):
                piece_ref = piece_refs[block]
                halo_ref, n = halo_parts[block]
                here = piece_ref[pl.ds(i * rows, rows), :]
                low = piece_ref[pl.ds(lay.main + 2 * i, 1), :]
                high = piece_ref[pl.ds(lay.main + 2 * i + 1, 1), :]
                return (
                    here,
                    pltpu.roll(here, width - 1, 1),
                    pltpu.roll(here, 1, 1),
                    jnp.where(line == rows - 1, high, pltpu.roll(here, rows - 1, 0)),
                    jnp.where(line == 0, low, pltpu.roll(here, 1, 0)),
                    other_refs[block][pl.ds(i * rows, rows), :],
                    halo_ref[n, pl.ds(i * rows, rows), :],
                )

            def keep(at, values):
                for n, value in enumerate(values):
                    near_ref[at, n] = value

            def keep_slot(i, values, block=block):
                keep(block * lay.quota + i, values)

            grouped(0, lay.quota, spread, keep_slot)
            for i in range(lay.quota, lay.fields):
                keep(lay.place(block, i), spread(i))

        def operator_of(term):
            at = lay.term_place(term, mode)
            here, right, left, *rest = [near_ref[at, n] for n in range(7)]
            right = jnp.where(lane == width - 1, 0.0, right)
            left = jnp.where(lane == 0, 0.0, left)
            faces = [0.5 * (here + n) for n in (right, left, *rest)]
            diagonal = faces[0] + faces[1] + faces[2] + faces[3] + faces[4] + faces[5]
            faces[0] = jnp.where(lane == width - 1, 0.0, faces[0])
            faces[1] = jnp.where(lane == 0, 0.0, faces[1])

            def operator(t):
                total = diagonal * near_ref[t, 0]
                for n, face in enumerate(faces):
                    total = total - face * near_ref[t, n + 1]
                return total

            return operator

        def keep_product(e, value):
            product_ref[e] = value

        for term in range(1, lay.terms):
            operator = operator_of(term)
            grouped(
                (term - 1) * ACTIVE,
                ACTIVE,
                lambda e, operator=operator: operator(source_ref[e]),
                keep_product,
            )

        operator = operator_of(0)
        for block in range(lay.modes):

            def collect(i, block=block):
                s = block * lay.quota + i
                return gather_products(s, take_ref, factor_ref, product_ref, operator(s))

            def keep_out(i, value, out_ref=out_refs[block]):
                out_ref[i] = value

            grouped(0, lay.quota, collect, keep_out)

    return pl.pallas_call(
        kernel,
        out_shape=[jax.ShapeDtypeStruct((lay.quota, rows, width), jnp.float32)] * lay.modes,
        in_specs=smem(4) + vmem(2 * lay.modes + len(halos)),
        out_specs=vmem(lay.modes),
        scratch_shapes=[
            pltpu.VMEM((lay.places, 7, rows, width), jnp.float32),
            pltpu.VMEM(((lay.terms - 1) * ACTIVE, rows, width), jnp.float32),
        ],
        compiler_params=pltpu.CompilerParams(vmem_limit_bytes=VMEM_LIMIT),
        name=name,
    )(j, *lists, *pieces, *others, *halos)


def grouped(first, count, compute, store):
    size = max(n for n in range(1, GROUP + 1) if count % n == 0)

    def step(g, carry):
        numbers = [first + g * size + n for n in range(size)]
        values = [compute(n) for n in numbers]
        for n, value in zip(numbers, values):
            store(n, value)
        return carry

    lax.fori_loop(0, count // size, step, 0)


def after(value, *done):
    return lax.optimization_barrier((value, *done))[0]


def on_device(chaos_field, mean_field, kl_fields, pattern, coupling, slot_mode):
    spaces, modes = lax.axis_size("space"), lax.axis_size("mode")
    quota, _, height, width = chaos_field.shape
    terms = kl_fields.shape[0] + 1
    lay = Layout(quota, terms, modes, height, width)
    axes = ("space", "mode")
    devices = spaces * modes
    space = lax.axis_index("space").astype(jnp.int32)
    mode = lax.axis_index("mode").astype(jnp.int32)
    j = (lax.rem(space, PLANES) * modes + mode).reshape(1)

    def swap(piece, r):
        if r == 0:
            return piece
        return lax.ppermute(piece, axes, [(d, d ^ r) for d in range(devices)])

    def shift(fields, crossing):
        pairs = []
        for d in range(devices):
            upper = (d // modes) % PLANES == (0 if crossing else 1)
            other = d + lay.group if upper else d - lay.group
            if 0 <= other < devices:
                pairs.append((d, other))
        return lax.ppermute(fields, axes, pairs)

    def mains(pieces):
        return jnp.stack([piece[: lay.main] for piece in pieces])

    field, kl = chaos_field[:, 0], kl_fields[:, 0]
    sent, chip_rows = pack(field, mean_field, kl, j, lay)
    half = modes // 2
    pieces = sent[:1] + [None] * (lay.group - 1)
    for r in [half, *range(half + 1, modes), *range(modes, modes + half), *range(1, half)]:
        pieces[r] = swap(sent[r], r)
    chip_halo = shift(chip_rows, False)
    first, last = modes + half, lay.group - 1
    pieces[first] = swap(after(sent[first], *pieces[half:first]), first)
    pieces[last] = swap(after(sent[last], *pieces[half:first]), last)
    number = jnp.arange(modes, dtype=jnp.int32)
    mine = jnp.bitwise_xor(number, mode)[:, None, None] == number[None, :, None]
    slot_mode = jnp.sum(jnp.where(mine, slot_mode.reshape(1, modes, quota), 0), 1).reshape(-1)
    lists = coupling_lists(pattern, coupling, after(slot_mode, chip_halo))
    pieces[first] = after(pieces[first], *lists)
    own_halos = [chip_halo[:1], swap(chip_halo[1:], 1), shift(mains(pieces[half:modes]), False)]
    crossing_halos = [shift(mains(pieces[r : r + half]), True) for r in (modes, first)]

    own, crossing = pieces[:modes], pieces[modes:]
    crossing_out = stencil(crossing, own, own_halos, lists, j, "stencil_crossing", lay)
    own_j = after(j, *crossing_out)
    own_out = stencil(own, crossing, crossing_halos, lists, own_j, "stencil_own", lay)
    out = [*own_out, *crossing_out]
    for r in range(modes, modes + half):
        out[r] = after(out[r], *own_out)
    first = [*range(modes + half, lay.group)]
    rest = [r + n for n in range(half) for r in (half, modes)] + [*range(half)]
    back = {r: swap(out[r], r) for r in first + rest}
    return unpack(back, j, (quota, height, width), lay).reshape(chaos_field.shape)


def solution(mesh):
    in_specs = (
        P("mode", "space", None, None),
        P("space", None, None),
        P(None, "space", None, None),
        P(),
        P(),
        P(),
    )
    out_specs = P("mode", "space", None, None)
    return jax.shard_map(
        on_device, mesh=mesh, in_specs=in_specs, out_specs=out_specs, check_vma=False
    )
```

```python
import jax
import jax.numpy as jnp
from jax import lax
from jax.experimental import pallas as pl
from jax.experimental.pallas import tpu as pltpu
from jax.sharding import PartitionSpec as P

VMEM_LIMIT = 40 * 1024 * 1024
PLANES = 2
CORES = 2
ACTIVE = 49
MOST = 8


class Layout:
    def __init__(self, quota, terms, modes, height, width):
        self.modes = modes
        self.group = PLANES * modes
        self.rows = height // self.group
        self.width = width
        self.terms = terms
        self.quota = quota
        self.slots = quota * modes
        self.share = -(-terms // modes)
        self.fields = quota + self.share
        self.main = self.fields * self.rows
        self.parts = self.fields + -(-2 * self.fields // self.rows)
        self.piece = self.parts * self.rows
        self.places = self.fields * modes

    def edge(self, i):
        return self.fields + 2 * i // self.rows, 2 * i % self.rows

    def place(self, block, i):
        if i < self.quota:
            return block * self.quota + i
        return self.slots + block * self.share + (i - self.quota)

    def term_place(self, term, mode):
        owner = lax.div(term, self.share)
        block = jnp.bitwise_xor(owner, mode)
        return self.slots + block * self.share + (term - owner * self.share)


def vmem(count):
    return [pl.BlockSpec(memory_space=pltpu.VMEM)] * count


def smem(count):
    return [pl.BlockSpec(memory_space=pltpu.SMEM)] * count


def pack(field, mean, kl, j, lay):
    kl_terms = kl.shape[0]
    rows, width, quota = lay.rows, lay.width, lay.quota

    def kernel(j_ref, field_ref, mean_ref, kl_ref, *refs):
        out_refs, (halo_ref, stage_ref, sems) = refs[: lay.group], refs[lay.group :]
        mode = lax.rem(j_ref[0], lay.modes)

        def load(n, begin=True):
            at, target = pl.ds(n * rows, rows), stage_ref.at[n]
            copies = [
                pltpu.make_async_copy(
                    field_ref.at[:, at, :], target.at[pl.ds(0, quota)], sems.at[n, 0]
                )
            ]
            if begin:
                copies[0].start()
            for i in range(lay.share):
                term = mode * lay.share + i
                into, sem = target.at[quota + i], sems.at[n, 1 + i]
                if not begin:
                    copies.append(pltpu.make_async_copy(mean_ref.at[0, at, :], into, sem))
                    continue

                @pl.when(term == 0)
                def _():
                    pltpu.make_async_copy(mean_ref.at[0, at, :], into, sem).start()

                @pl.when(term > 0)
                def _():
                    source = kl_ref.at[jnp.clip(term - 1, 0, kl_terms - 1), at, :]
                    pltpu.make_async_copy(source, into, sem).start()

            return copies

        for n in range(lay.group):
            load(n)
        for n in range(lay.group):
            for made in load(n, begin=False):
                made.wait()
        none = jnp.zeros((1, width), jnp.float32)
        for n in range(lay.group):
            for i in range(lay.fields):
                part, line = lay.edge(i)
                low = stage_ref[n - 1, i, rows - 1 :] if n > 0 else none
                high = stage_ref[n + 1, i, :1] if n < lay.group - 1 else none
                stage_ref[n, part, line : line + 1] = low
                stage_ref[n, part, line + 1 : line + 2] = high
            part, line = lay.edge(lay.fields)
            if part < lay.parts:
                stage_ref[n, part, line:] = jnp.zeros((rows - line, width), jnp.float32)
        for r, out_ref in enumerate(out_refs):
            to = jnp.bitwise_xor(j_ref[0], r)
            for part in range(lay.parts):
                out_ref[part] = stage_ref[to, part]
                if r < CORES and part < lay.fields:
                    halo_ref[r, part] = stage_ref[to, part]

    shape = (lay.parts, rows, width)
    *sent, halo = pl.pallas_call(
        kernel,
        out_shape=[pltpu.VMEM(shape, jnp.float32)] * lay.group
        + [pltpu.VMEM((CORES, lay.fields, rows, width), jnp.float32)],
        in_specs=smem(1) + [pl.BlockSpec(memory_space=pltpu.HBM)] * 3,
        out_specs=vmem(lay.group + 1),
        scratch_shapes=[
            pltpu.VMEM((lay.group, *shape), jnp.float32),
            pltpu.SemaphoreType.DMA((lay.group, 1 + lay.share)),
        ],
        compiler_params=pltpu.CompilerParams(vmem_limit_bytes=VMEM_LIMIT),
        name="pack",
    )(j, *[pltpu.with_memory_space_constraint(x, pltpu.HBM) for x in (field, mean, kl)])
    sent = [piece.reshape(lay.piece, width) for piece in sent]
    return sent, halo.reshape(CORES, lay.main, width)


def unpack(pieces, j, shape, lay):
    rows = lay.rows

    def kernel(j_ref, *refs):
        piece_refs, out_ref, sems = refs[:-2], refs[-2], refs[-1]
        copies = []
        for r, piece_ref in zip(pieces, piece_refs):
            start = pl.multiple_of(jnp.bitwise_xor(j_ref[0], r) * rows, 8)
            made = pltpu.make_async_copy(
                piece_ref, out_ref.at[:, pl.ds(start, rows), :], sems.at[r]
            )
            made.start()
            copies.append(made)
        for made in copies:
            made.wait()

    return pl.pallas_call(
        kernel,
        out_shape=jax.ShapeDtypeStruct(shape, jnp.float32),
        in_specs=smem(1) + vmem(lay.group),
        out_specs=pl.BlockSpec(memory_space=pltpu.HBM),
        scratch_shapes=[pltpu.SemaphoreType.DMA((lay.group,))],
        compiler_params=pltpu.CompilerParams(vmem_limit_bytes=VMEM_LIMIT),
        name="unpack",
    )(j, *pieces.values())


def coupling_lists(pattern, coupling, slot_mode):
    masked = (coupling * pattern.astype(jnp.float32))[1:]
    terms, modes = masked.shape[0], masked.shape[1]
    number = jnp.arange(modes, dtype=jnp.int32)
    one_hot = (slot_mode[:, None] == number[None, :]).astype(jnp.float32)
    coupled = jnp.einsum(
        "sa,kab,tb->kst", one_hot, masked, one_hot, precision=lax.Precision.HIGHEST
    )
    there = coupled != 0.0
    column = number[None, None, :]
    first = jnp.min(jnp.where(there, column, modes), 2)
    last = jnp.max(jnp.where(there, column, -1), 2)
    active = first < modes
    earlier = column < number[None, :, None]
    rank = jnp.sum(jnp.where(active[:, None, :] & earlier, 1, 0), 2)
    place = jnp.arange(ACTIVE, dtype=jnp.int32)[None, :, None]
    chosen = active[:, None, :] & (rank[:, None, :] == place)
    sources = jnp.sum(jnp.where(chosen, column, 0), 2)

    base = ACTIVE * jnp.arange(terms, dtype=jnp.int32)[:, None]
    products, factors, valid = [], [], []
    for chosen_t, is_valid in ((first, active), (last, last > first)):
        before = active[:, None, :] & (column < chosen_t[:, :, None])
        products.append(base + jnp.sum(jnp.where(before, 1, 0), 2))
        factors.append(jnp.sum(jnp.where(column == chosen_t[:, :, None], coupled, 0.0), 2))
        valid.append(is_valid)
    products = jnp.concatenate(products, 0)
    factors = jnp.concatenate(factors, 0)
    valid = jnp.concatenate(valid, 0)
    index = jnp.arange(2 * terms, dtype=jnp.int32)
    order = index[None, :] < index[:, None]
    rank = jnp.sum(jnp.where(valid[None] & order[:, :, None], 1, 0), 1)
    place = jnp.arange(MOST, dtype=jnp.int32)[:, None, None]
    chosen = valid[None] & (rank[None] == place)
    take = jnp.sum(jnp.where(chosen, products[None], 0), 1)
    factor = jnp.sum(jnp.where(chosen, factors[None], 0.0), 1)
    return jnp.concatenate([sources.reshape(-1), take.T.reshape(-1)]), factor.T.reshape(-1)


def tree_sum(values):
    while len(values) > 1:
        values = [sum(values[n : n + 2][1:], values[n]) for n in range(0, len(values), 2)]
    return values[0]


def stencil(pieces, others, halos, lists, j, name, lay):
    rows, width = lay.rows, lay.width
    full = (rows, width)
    arrays = list({id(array): array for array, _ in halos}.values())
    products = (lay.terms - 1) * ACTIVE

    def kernel(j_ref, index_ref, factor_ref, *refs):
        piece_refs, refs = refs[: lay.modes], refs[lay.modes :]
        other_refs, refs = refs[: lay.modes], refs[lay.modes :]
        halo_refs, refs = refs[: len(arrays)], refs[len(arrays) :]
        out_refs, (near_ref, product_ref) = refs[: lay.modes], refs[lay.modes :]
        lane = lax.broadcasted_iota(jnp.int32, full, 1)
        line = lax.broadcasted_iota(jnp.int32, full, 0)
        mode = lax.rem(j_ref[0], lay.modes)
        ref_of = {id(array): ref for array, ref in zip(arrays, halo_refs)}
        halo_parts = [(ref_of[id(array)], n) for array, n in halos]

        def to_right(value):
            return pltpu.roll(value, width - 1, 1)

        def to_left(value):
            return pltpu.roll(value, 1, 1)

        for block in range(lay.modes):
            piece_ref, other_ref = piece_refs[block], other_refs[block]
            halo_ref, n = halo_parts[block]
            for i in range(lay.fields):
                own = i < lay.quota
                at, rows_i = lay.place(block, i), slice(i * rows, (i + 1) * rows)
                edge = lay.main + 2 * i
                here = piece_ref[rows_i, :]
                right = to_right(here)
                near_ref[at, 0] = here
                near_ref[at, 1] = jnp.where(lane == width - 1, 0.0, here - right) if own else right
                high, low = piece_ref[edge + 1 : edge + 2, :], piece_ref[edge : edge + 1, :]
                near_ref[at, 2] = jnp.where(line == rows - 1, high, pltpu.roll(here, rows - 1, 0))
                near_ref[at, 3] = jnp.where(line == 0, low, pltpu.roll(here, 1, 0))
                near_ref[at, 4] = other_ref[rows_i, :]
                near_ref[at, 5] = halo_ref[n, rows_i, :]

        def operator_of(term):
            at = lay.term_place(term, mode)
            here, right, *rest = [near_ref[at, n] for n in range(6)]
            across = jnp.where(lane == width - 1, 0.0, 0.5 * (here + right))
            ends = jnp.where((lane == 0) | (lane == width - 1), 0.5 * here, 0.0)
            faces = [0.5 * (here + n) for n in rest]
            diagonal = tree_sum([ends, *faces])

            def operator(t):
                flux = across * near_ref[t, 1]
                rest = [face * near_ref[t, n + 2] for n, face in enumerate(faces)]
                return (flux - to_left(flux)) + (diagonal * near_ref[t, 0] - tree_sum(rest))

            return operator

        def apply(term, carry):
            operator = operator_of(term)
            first = (term - 1) * ACTIVE
            for n in range(ACTIVE):
                product_ref[first + n] = operator(index_ref[first + n])
            return carry

        lax.fori_loop(1, lay.terms, apply, 0)

        operator = operator_of(0)
        for block in range(lay.modes):
            for i in range(lay.quota):
                s = block * lay.quota + i
                values = [operator(s)]
                for n in range(MOST):
                    e = s * MOST + n
                    values.append(factor_ref[e] * product_ref[index_ref[products + e]])
                out_refs[block][i] = tree_sum(values)

    return pl.pallas_call(
        kernel,
        out_shape=[jax.ShapeDtypeStruct((lay.quota, rows, width), jnp.float32)] * lay.modes,
        in_specs=smem(3) + vmem(2 * lay.modes + len(arrays)),
        out_specs=vmem(lay.modes),
        scratch_shapes=[
            pltpu.VMEM((lay.places, 6, rows, width), jnp.float32),
            pltpu.VMEM((products, rows, width), jnp.float32),
        ],
        compiler_params=pltpu.CompilerParams(vmem_limit_bytes=VMEM_LIMIT),
        name=name,
    )(j, *lists, *pieces, *others, *arrays)


def after(value, *done):
    return lax.optimization_barrier((value, *done))[0]


def on_device(chaos_field, mean_field, kl_fields, pattern, coupling, slot_mode):
    spaces, modes = lax.axis_size("space"), lax.axis_size("mode")
    quota, _, height, width = chaos_field.shape
    terms = kl_fields.shape[0] + 1
    lay = Layout(quota, terms, modes, height, width)
    axes = ("space", "mode")
    devices = spaces * modes
    space = lax.axis_index("space").astype(jnp.int32)
    mode = lax.axis_index("mode").astype(jnp.int32)
    j = (lax.rem(space, PLANES) * modes + mode).reshape(1)

    def swap(piece, r):
        if r == 0:
            return piece
        return lax.ppermute(piece, axes, [(d, d ^ r) for d in range(devices)])

    def shift(fields, crossing):
        pairs = []
        for d in range(devices):
            upper = (d // modes) % PLANES == (0 if crossing else 1)
            other = d + lay.group if upper else d - lay.group
            if 0 <= other < devices:
                pairs.append((d, other))
        return lax.ppermute(fields, axes, pairs)

    def mains(pieces):
        return jnp.stack([piece[: lay.main] for piece in pieces])

    field, kl = chaos_field[:, 0], kl_fields[:, 0]
    sent, chip_rows = pack(field, mean_field, kl, j, lay)
    half = modes // 2
    pieces = sent[:1] + [None] * (lay.group - 1)
    for r in [*range(half, modes), *range(modes, modes + half)]:
        pieces[r] = swap(sent[r], r)
    chip_halo = shift(chip_rows, False)
    for r in range(1, half):
        pieces[r] = swap(after(sent[r], chip_halo), r)
    first, last = modes + half, lay.group - 1
    pieces[first] = swap(after(sent[first], *pieces[half:first]), first)
    pieces[last] = swap(after(sent[last], *pieces[half:first]), last)
    core_halo = swap(chip_halo, 1)
    number = jnp.arange(modes, dtype=jnp.int32)
    mine = jnp.bitwise_xor(number, mode)[:, None, None] == number[None, :, None]
    slot_mode = jnp.sum(jnp.where(mine, slot_mode.reshape(1, modes, quota), 0), 1).reshape(-1)
    lists = coupling_lists(pattern, coupling, slot_mode)
    pieces[half] = after(pieces[half], *lists)
    pieces[first] = after(pieces[first], core_halo, *pieces[1:half])
    own_halo = shift(mains(pieces[half:modes]), False)
    own_halos = [(chip_halo, 0), (core_halo, 1), (own_halo, 0), (own_halo, 1)]
    crossing_halos = []
    for r in (modes, first):
        halo = shift(mains(pieces[r : r + half]), True)
        crossing_halos += [(halo, 0), (halo, 1)]

    own, crossing = pieces[:modes], pieces[modes:]
    crossing_out = stencil(crossing, own, own_halos, lists, j, "stencil_crossing", lay)
    own_j = after(j, *crossing_out)
    own_out = stencil(own, crossing, crossing_halos, lists, own_j, "stencil_own", lay)
    out = [*own_out, *crossing_out]
    for r in range(modes, modes + half):
        out[r] = after(out[r], *own_out)
    first = [*range(modes + half, lay.group)]
    rest = [r + n for n in range(half) for r in (half, modes)] + [*range(half)]
    back = {r: swap(out[r], r) for r in first + rest}
    return unpack(back, j, (quota, height, width), lay).reshape(chaos_field.shape)


def solution(mesh):
    in_specs = (
        P("mode", "space", None, None),
        P("space", None, None),
        P(None, "space", None, None),
        P(),
        P(),
        P(),
    )
    out_specs = P("mode", "space", None, None)
    return jax.shard_map(
        on_device, mesh=mesh, in_specs=in_specs, out_specs=out_specs, check_vma=False
    )
```

```python
import jax
import jax.numpy as jnp
from jax import lax
from jax.experimental import pallas as pl
from jax.experimental.pallas import tpu as pltpu
from jax.sharding import PartitionSpec as P

VMEM_LIMIT = 40 * 1024 * 1024
PLANES = 2
ACTIVE = 49
MOST = 8


class Layout:
    def __init__(self, quota, terms, modes, height, width):
        self.modes = modes
        self.group = PLANES * modes
        self.rows = height // self.group
        self.width = width
        self.terms = terms
        self.quota = quota
        self.slots = quota * modes
        self.share = -(-terms // modes)
        self.fields = quota + self.share
        self.main = self.fields * self.rows
        self.parts = self.fields + -(-2 * self.fields // self.rows)
        self.piece = self.parts * self.rows
        self.places = self.fields * modes

    def edge(self, i):
        return self.fields + 2 * i // self.rows, 2 * i % self.rows

    def place(self, block, i):
        if i < self.quota:
            return block * self.quota + i
        return self.slots + block * self.share + (i - self.quota)

    def term_place(self, term, mode):
        owner = lax.div(term, self.share)
        block = jnp.bitwise_xor(owner, mode)
        return self.slots + block * self.share + (term - owner * self.share)


def vmem(count):
    return [pl.BlockSpec(memory_space=pltpu.VMEM)] * count


def smem(count):
    return [pl.BlockSpec(memory_space=pltpu.SMEM)] * count


def pack(field, mean, kl, j, crossing, lay):
    kl_terms = kl.shape[0]
    rows, width, modes, quota = lay.rows, lay.width, lay.modes, lay.quota
    half = modes * rows
    tile = 8

    def kernel(j_ref, field_ref, mean_ref, kl_ref, *refs):
        out_refs, (stage_ref, past_ref, in_sems) = refs[:modes], refs[modes:]
        plane = j_ref[0] // modes
        mode = j_ref[0] - plane * modes
        side = 1 - plane if crossing else plane
        start = side * half
        beside = pl.multiple_of(half - side * tile, tile)

        def load(n, begin=True):
            if n < modes:
                at, target = pl.ds(pl.multiple_of(start + n * rows, tile), rows), stage_ref.at[n]
            else:
                at, target = pl.ds(beside, tile), past_ref
            copies = [
                pltpu.make_async_copy(
                    field_ref.at[:, at, :], target.at[pl.ds(0, quota)], in_sems.at[n, 0]
                )
            ]
            if begin:
                copies[0].start()
            for i in range(lay.share):
                term = mode * lay.share + i
                into, sem = target.at[quota + i], in_sems.at[n, 1 + i]
                if not begin:
                    copies.append(pltpu.make_async_copy(mean_ref.at[0, at, :], into, sem))
                    continue

                @pl.when(term == 0)
                def _():
                    pltpu.make_async_copy(mean_ref.at[0, at, :], into, sem).start()

                @pl.when(term > 0)
                def _():
                    source = kl_ref.at[jnp.clip(term - 1, 0, kl_terms - 1), at, :]
                    pltpu.make_async_copy(source, into, sem).start()

            return copies

        for n in range(modes + 1):
            load(n)
        for n in range(modes + 1):
            for made in load(n, begin=False):
                made.wait()
        low_there = jnp.where(side == 0, 0.0, 1.0)
        high_there = jnp.where(side == PLANES - 1, 0.0, 1.0)
        for n in range(modes):
            for i in range(lay.fields):
                if n > 0:
                    low = stage_ref[n - 1, i, rows - 1 :]
                else:
                    low = past_ref[i, tile - 1 :] * low_there
                if n < modes - 1:
                    high = stage_ref[n + 1, i, :1]
                else:
                    high = past_ref[i, :1] * high_there
                part, line = lay.edge(i)
                stage_ref[n, part, line : line + 1] = low
                stage_ref[n, part, line + 1 : line + 2] = high
            part, line = lay.edge(lay.fields)
            if part < lay.parts:
                stage_ref[n, part, line:] = jnp.zeros((rows - line, width), jnp.float32)
        for n, out_ref in enumerate(out_refs):
            to = jnp.bitwise_xor(mode, n)
            for part in range(lay.parts):
                out_ref[part] = stage_ref[to, part]

    shape = (lay.parts, rows, width)
    sent = pl.pallas_call(
        kernel,
        out_shape=[pltpu.VMEM(shape, jnp.float32)] * modes,
        in_specs=smem(1) + [pl.BlockSpec(memory_space=pltpu.HBM)] * 3,
        out_specs=vmem(modes),
        scratch_shapes=[
            pltpu.VMEM((modes, *shape), jnp.float32),
            pltpu.VMEM((lay.fields, tile, width), jnp.float32),
            pltpu.SemaphoreType.DMA((modes + 1, 1 + lay.share)),
        ],
        compiler_params=pltpu.CompilerParams(vmem_limit_bytes=VMEM_LIMIT),
        name="pack_crossing" if crossing else "pack_own",
    )(j, *[pltpu.with_memory_space_constraint(x, pltpu.HBM) for x in (field, mean, kl)])
    return [piece.reshape(lay.piece, width) for piece in sent]


def unpack(pieces, j, shape, lay):
    rows = lay.rows

    def kernel(j_ref, *refs):
        piece_refs, out_ref, sems = refs[:-2], refs[-2], refs[-1]
        copies = []
        for r, piece_ref in zip(pieces, piece_refs):
            start = pl.multiple_of(jnp.bitwise_xor(j_ref[0], r) * rows, 8)
            made = pltpu.make_async_copy(
                piece_ref, out_ref.at[:, pl.ds(start, rows), :], sems.at[r]
            )
            made.start()
            copies.append(made)
        for made in copies:
            made.wait()

    return pl.pallas_call(
        kernel,
        out_shape=jax.ShapeDtypeStruct(shape, jnp.float32),
        in_specs=smem(1) + vmem(lay.group),
        out_specs=pl.BlockSpec(memory_space=pltpu.HBM),
        scratch_shapes=[pltpu.SemaphoreType.DMA((lay.group,))],
        compiler_params=pltpu.CompilerParams(vmem_limit_bytes=VMEM_LIMIT),
        name="unpack",
    )(j, *pieces.values())


def coupling_lists(pattern, coupling, slot_mode):
    masked = (coupling * pattern.astype(jnp.float32))[1:]
    terms, modes = masked.shape[0], masked.shape[1]
    number = jnp.arange(modes, dtype=jnp.int32)
    one_hot = (slot_mode[:, None] == number[None, :]).astype(jnp.float32)
    coupled = jnp.einsum(
        "sa,kab,tb->kst", one_hot, masked, one_hot, precision=lax.Precision.HIGHEST
    )
    there = coupled != 0.0
    column = number[None, None, :]
    first = jnp.min(jnp.where(there, column, modes), 2)
    last = jnp.max(jnp.where(there, column, -1), 2)
    active = first < modes
    earlier = column < number[None, :, None]
    rank = jnp.sum(jnp.where(active[:, None, :] & earlier, 1, 0), 2)
    place = jnp.arange(ACTIVE, dtype=jnp.int32)[None, :, None]
    chosen = active[:, None, :] & (rank[:, None, :] == place)
    sources = jnp.sum(jnp.where(chosen, column, 0), 2)

    base = ACTIVE * jnp.arange(terms, dtype=jnp.int32)[:, None]
    products, factors, valid = [], [], []
    for chosen_t, is_valid in ((first, active), (last, last > first)):
        before = active[:, None, :] & (column < chosen_t[:, :, None])
        products.append(base + jnp.sum(jnp.where(before, 1, 0), 2))
        factors.append(jnp.sum(jnp.where(column == chosen_t[:, :, None], coupled, 0.0), 2))
        valid.append(is_valid)
    products = jnp.concatenate(products, 0)
    factors = jnp.concatenate(factors, 0)
    valid = jnp.concatenate(valid, 0)
    index = jnp.arange(2 * terms, dtype=jnp.int32)
    order = index[None, :] < index[:, None]
    rank = jnp.sum(jnp.where(valid[None] & order[:, :, None], 1, 0), 1)
    place = jnp.arange(MOST, dtype=jnp.int32)[:, None, None]
    chosen = valid[None] & (rank[None] == place)
    take = jnp.sum(jnp.where(chosen, products[None], 0), 1)
    factor = jnp.sum(jnp.where(chosen, factors[None], 0.0), 1)
    return jnp.concatenate([sources.reshape(-1), take.T.reshape(-1)]), factor.T.reshape(-1)


def tree_sum(values):
    while len(values) > 1:
        values = [sum(values[n : n + 2][1:], values[n]) for n in range(0, len(values), 2)]
    return values[0]


def stencil(pieces, others, halos, lists, j, name, lay):
    rows, width = lay.rows, lay.width
    full = (rows, width)
    arrays = list({id(array): array for array, _ in halos}.values())
    products = (lay.terms - 1) * ACTIVE

    def kernel(j_ref, index_ref, factor_ref, *refs):
        piece_refs, refs = refs[: lay.modes], refs[lay.modes :]
        other_refs, refs = refs[: lay.modes], refs[lay.modes :]
        halo_refs, refs = refs[: len(arrays)], refs[len(arrays) :]
        out_refs, (near_ref, product_ref) = refs[: lay.modes], refs[lay.modes :]
        lane = lax.broadcasted_iota(jnp.int32, full, 1)
        line = lax.broadcasted_iota(jnp.int32, full, 0)
        mode = lax.rem(j_ref[0], lay.modes)
        ref_of = {id(array): ref for array, ref in zip(arrays, halo_refs)}
        halo_parts = [(ref_of[id(array)], n) for array, n in halos]

        def to_right(value):
            return pltpu.roll(value, width - 1, 1)

        def to_left(value):
            return pltpu.roll(value, 1, 1)

        for block in range(lay.modes):
            piece_ref, other_ref = piece_refs[block], other_refs[block]
            halo_ref, n = halo_parts[block]
            for i in range(lay.fields):
                own = i < lay.quota
                at, rows_i = lay.place(block, i), slice(i * rows, (i + 1) * rows)
                edge = lay.main + 2 * i
                here = piece_ref[rows_i, :]
                right = to_right(here)
                near_ref[at, 0] = here
                near_ref[at, 1] = jnp.where(lane == width - 1, 0.0, here - right) if own else right
                high, low = piece_ref[edge + 1 : edge + 2, :], piece_ref[edge : edge + 1, :]
                near_ref[at, 2] = jnp.where(line == rows - 1, high, pltpu.roll(here, rows - 1, 0))
                near_ref[at, 3] = jnp.where(line == 0, low, pltpu.roll(here, 1, 0))
                near_ref[at, 4] = other_ref[rows_i, :]
                near_ref[at, 5] = halo_ref[n, rows_i, :]

        def operator_of(term):
            at = lay.term_place(term, mode)
            here, right, *rest = [near_ref[at, n] for n in range(6)]
            across = jnp.where(lane == width - 1, 0.0, 0.5 * (here + right))
            ends = jnp.where((lane == 0) | (lane == width - 1), 0.5 * here, 0.0)
            faces = [0.5 * (here + n) for n in rest]
            diagonal = tree_sum([ends, *faces])

            def operator(t):
                flux = across * near_ref[t, 1]
                rest = [face * near_ref[t, n + 2] for n, face in enumerate(faces)]
                return (flux - to_left(flux)) + (diagonal * near_ref[t, 0] - tree_sum(rest))

            return operator

        def apply(term, carry):
            operator = operator_of(term)
            first = (term - 1) * ACTIVE
            for n in range(ACTIVE):
                product_ref[first + n] = operator(index_ref[first + n])
            return carry

        lax.fori_loop(1, lay.terms, apply, 0)

        operator = operator_of(0)
        for block in range(lay.modes):
            for i in range(lay.quota):
                s = block * lay.quota + i
                values = [operator(s)]
                for n in range(MOST):
                    e = s * MOST + n
                    values.append(factor_ref[e] * product_ref[index_ref[products + e]])
                out_refs[block][i] = tree_sum(values)

    return pl.pallas_call(
        kernel,
        out_shape=[jax.ShapeDtypeStruct((lay.quota, rows, width), jnp.float32)] * lay.modes,
        in_specs=smem(3) + vmem(2 * lay.modes + len(arrays)),
        out_specs=vmem(lay.modes),
        scratch_shapes=[
            pltpu.VMEM((lay.places, 6, rows, width), jnp.float32),
            pltpu.VMEM((products, rows, width), jnp.float32),
        ],
        compiler_params=pltpu.CompilerParams(vmem_limit_bytes=VMEM_LIMIT),
        name=name,
    )(j, *lists, *pieces, *others, *arrays)


def after(value, *done):
    return lax.optimization_barrier((value, *done))[0]


def on_device(chaos_field, mean_field, kl_fields, pattern, coupling, slot_mode):
    spaces, modes = lax.axis_size("space"), lax.axis_size("mode")
    quota, _, height, width = chaos_field.shape
    terms = kl_fields.shape[0] + 1
    lay = Layout(quota, terms, modes, height, width)
    axes = ("space", "mode")
    devices = spaces * modes
    space = lax.axis_index("space").astype(jnp.int32)
    mode = lax.axis_index("mode").astype(jnp.int32)
    j = (lax.rem(space, PLANES) * modes + mode).reshape(1)

    def swap(piece, r):
        if r == 0:
            return piece
        return lax.ppermute(piece, axes, [(d, d ^ r) for d in range(devices)])

    def shift(pieces, crossing):
        pairs = []
        for d in range(devices):
            upper = (d // modes) % PLANES == (0 if crossing else 1)
            other = d + lay.group if upper else d - lay.group
            if 0 <= other < devices:
                pairs.append((d, other))
        main = jnp.stack([piece[: lay.main] for piece in pieces])
        return lax.ppermute(main, axes, pairs)

    field, kl = chaos_field[:, 0], kl_fields[:, 0]
    sent = [None] * lay.group
    sent[:modes] = pack(field, mean_field, kl, j, False, lay)
    sent[modes:] = pack(field, mean_field, kl, after(j, *sent[:modes]), True, lay)
    half = modes // 2
    pieces = sent[:1] + [None] * (lay.group - 1)
    for r in [*range(half, modes), *range(1, half), *range(modes, modes + half)]:
        pieces[r] = swap(sent[r], r)
    for r in range(modes + half, lay.group):
        pieces[r] = swap(after(sent[r], *pieces[half:modes]), r)
    number = jnp.arange(modes, dtype=jnp.int32)
    mine = jnp.bitwise_xor(number, mode)[:, None, None] == number[None, :, None]
    slot_mode = jnp.sum(jnp.where(mine, slot_mode.reshape(1, modes, quota), 0), 1).reshape(-1)
    lists = coupling_lists(pattern, coupling, slot_mode)
    pieces[half] = after(pieces[half], *lists)
    own_halo = shift(pieces[:modes], False)
    own_halos = [(own_halo, n) for n in range(modes)]
    crossing_halos = []
    for r in (modes, modes + half):
        halo = shift(pieces[r : r + half], True)
        crossing_halos += [(halo, n) for n in range(half)]

    own, crossing = pieces[:modes], pieces[modes:]
    crossing_out = stencil(crossing, own, own_halos, lists, j, "stencil_crossing", lay)
    own_j = after(j, *crossing_out)
    own_out = stencil(own, crossing, crossing_halos, lists, own_j, "stencil_own", lay)
    out = [*own_out, *crossing_out]
    for r in range(modes, modes + half):
        out[r] = after(out[r], *own_out)
    first = [*range(modes + half, lay.group)]
    rest = [r + n for n in range(half) for r in (half, modes)] + [*range(half)]
    back = {r: swap(out[r], r) for r in first + rest}
    return unpack(back, j, (quota, height, width), lay).reshape(chaos_field.shape)


def solution(mesh):
    in_specs = (
        P("mode", "space", None, None),
        P("space", None, None),
        P(None, "space", None, None),
        P(),
        P(),
        P(),
    )
    out_specs = P("mode", "space", None, None)
    return jax.shard_map(
        on_device, mesh=mesh, in_specs=in_specs, out_specs=out_specs, check_vma=False
    )
```

```python
import jax
import jax.numpy as jnp
from jax import lax
from jax.experimental import pallas as pl
from jax.experimental.pallas import tpu as pltpu
from jax.sharding import PartitionSpec as P

VMEM_LIMIT = 40 * 1024 * 1024
PLANES = 2
ACTIVE = 49
MOST = 8


class Layout:
    def __init__(self, quota, terms, modes, height, width):
        self.modes = modes
        self.group = PLANES * modes
        self.rows = height // self.group
        self.width = width
        self.terms = terms
        self.quota = quota
        self.slots = quota * modes
        self.share = -(-terms // modes)
        self.fields = quota + self.share
        self.main = self.fields * self.rows
        self.parts = self.fields + -(-2 * self.fields // self.rows)
        self.piece = self.parts * self.rows
        self.places = self.fields * modes

    def edge(self, i):
        return self.fields + 2 * i // self.rows, 2 * i % self.rows

    def place(self, block, i):
        if i < self.quota:
            return block * self.quota + i
        return self.slots + block * self.share + (i - self.quota)

    def term_place(self, term, mode):
        owner = lax.div(term, self.share)
        block = jnp.bitwise_xor(owner, mode)
        return self.slots + block * self.share + (term - owner * self.share)


def vmem(count):
    return [pl.BlockSpec(memory_space=pltpu.VMEM)] * count


def smem(count):
    return [pl.BlockSpec(memory_space=pltpu.SMEM)] * count


def pack(field, mean, kl, j, crossing, lay):
    kl_terms = kl.shape[0]
    rows, width, modes, quota = lay.rows, lay.width, lay.modes, lay.quota
    half = modes * rows
    tile = 8

    def kernel(j_ref, field_ref, mean_ref, kl_ref, *refs):
        out_refs, (stage_ref, past_ref, in_sems) = refs[:modes], refs[modes:]
        plane = j_ref[0] // modes
        mode = j_ref[0] - plane * modes
        side = 1 - plane if crossing else plane
        start = side * half
        beside = pl.multiple_of(half - side * tile, tile)

        def load(n, begin=True):
            if n < modes:
                at, target = pl.ds(pl.multiple_of(start + n * rows, tile), rows), stage_ref.at[n]
            else:
                at, target = pl.ds(beside, tile), past_ref
            copies = [
                pltpu.make_async_copy(
                    field_ref.at[:, at, :], target.at[pl.ds(0, quota)], in_sems.at[n, 0]
                )
            ]
            if begin:
                copies[0].start()
            for i in range(lay.share):
                term = mode * lay.share + i
                into, sem = target.at[quota + i], in_sems.at[n, 1 + i]
                if not begin:
                    copies.append(pltpu.make_async_copy(mean_ref.at[0, at, :], into, sem))
                    continue

                @pl.when(term == 0)
                def _():
                    pltpu.make_async_copy(mean_ref.at[0, at, :], into, sem).start()

                @pl.when(term > 0)
                def _():
                    source = kl_ref.at[jnp.clip(term - 1, 0, kl_terms - 1), at, :]
                    pltpu.make_async_copy(source, into, sem).start()

            return copies

        for n in range(modes + 1):
            load(n)
        for n in range(modes + 1):
            for made in load(n, begin=False):
                made.wait()
        low_there = jnp.where(side == 0, 0.0, 1.0)
        high_there = jnp.where(side == PLANES - 1, 0.0, 1.0)
        for n in range(modes):
            for i in range(lay.fields):
                if n > 0:
                    low = stage_ref[n - 1, i, rows - 1 :]
                else:
                    low = past_ref[i, tile - 1 :] * low_there
                if n < modes - 1:
                    high = stage_ref[n + 1, i, :1]
                else:
                    high = past_ref[i, :1] * high_there
                part, line = lay.edge(i)
                stage_ref[n, part, line : line + 1] = low
                stage_ref[n, part, line + 1 : line + 2] = high
            part, line = lay.edge(lay.fields)
            if part < lay.parts:
                stage_ref[n, part, line:] = jnp.zeros((rows - line, width), jnp.float32)
        for n, out_ref in enumerate(out_refs):
            to = jnp.bitwise_xor(mode, n)
            for part in range(lay.parts):
                out_ref[part] = stage_ref[to, part]

    shape = (lay.parts, rows, width)
    sent = pl.pallas_call(
        kernel,
        out_shape=[pltpu.VMEM(shape, jnp.float32)] * modes,
        in_specs=smem(1) + [pl.BlockSpec(memory_space=pltpu.HBM)] * 3,
        out_specs=vmem(modes),
        scratch_shapes=[
            pltpu.VMEM((modes, *shape), jnp.float32),
            pltpu.VMEM((lay.fields, tile, width), jnp.float32),
            pltpu.SemaphoreType.DMA((modes + 1, 1 + lay.share)),
        ],
        compiler_params=pltpu.CompilerParams(vmem_limit_bytes=VMEM_LIMIT),
        name="pack_crossing" if crossing else "pack_own",
    )(j, *[pltpu.with_memory_space_constraint(x, pltpu.HBM) for x in (field, mean, kl)])
    return [piece.reshape(lay.piece, width) for piece in sent]


def unpack(pieces, j, shape, lay, whole=None):
    rows = lay.rows
    there = [] if whole is None else [whole]

    def kernel(j_ref, *refs):
        piece_refs, out_ref, sems = refs[: len(pieces)], refs[-2], refs[-1]
        copies = []
        for n, (r, piece_ref) in enumerate(zip(pieces, piece_refs)):
            start = pl.multiple_of(jnp.bitwise_xor(j_ref[0], r) * rows, 8)
            made = pltpu.make_async_copy(
                piece_ref, out_ref.at[:, pl.ds(start, rows), :], sems.at[n]
            )
            made.start()
            copies.append(made)
        for made in copies:
            made.wait()

    return pl.pallas_call(
        kernel,
        out_shape=pltpu.HBM(shape, jnp.float32),
        in_specs=smem(1) + vmem(len(pieces)) + [pl.BlockSpec(memory_space=pltpu.HBM)] * len(there),
        out_specs=pl.BlockSpec(memory_space=pltpu.HBM),
        scratch_shapes=[pltpu.SemaphoreType.DMA((len(pieces),))],
        input_output_aliases={1 + len(pieces): 0} if there else {},
        compiler_params=pltpu.CompilerParams(vmem_limit_bytes=VMEM_LIMIT),
        name="unpack_last" if there else "unpack_first",
    )(j, *pieces.values(), *there)


def coupling_lists(pattern, coupling, slot_mode):
    masked = (coupling * pattern.astype(jnp.float32))[1:]
    terms, modes = masked.shape[0], masked.shape[1]
    number = jnp.arange(modes, dtype=jnp.int32)
    one_hot = (slot_mode[:, None] == number[None, :]).astype(jnp.float32)
    coupled = jnp.einsum(
        "sa,kab,tb->kst", one_hot, masked, one_hot, precision=lax.Precision.HIGHEST
    )
    there = coupled != 0.0
    column = number[None, None, :]
    first = jnp.min(jnp.where(there, column, modes), 2)
    last = jnp.max(jnp.where(there, column, -1), 2)
    active = first < modes
    earlier = column < number[None, :, None]
    rank = jnp.sum(jnp.where(active[:, None, :] & earlier, 1, 0), 2)
    place = jnp.arange(ACTIVE, dtype=jnp.int32)[None, :, None]
    chosen = active[:, None, :] & (rank[:, None, :] == place)
    sources = jnp.sum(jnp.where(chosen, column, 0), 2)

    base = ACTIVE * jnp.arange(terms, dtype=jnp.int32)[:, None]
    products, factors, valid = [], [], []
    for chosen_t, is_valid in ((first, active), (last, last > first)):
        before = active[:, None, :] & (column < chosen_t[:, :, None])
        products.append(base + jnp.sum(jnp.where(before, 1, 0), 2))
        factors.append(jnp.sum(jnp.where(column == chosen_t[:, :, None], coupled, 0.0), 2))
        valid.append(is_valid)
    products = jnp.concatenate(products, 0)
    factors = jnp.concatenate(factors, 0)
    valid = jnp.concatenate(valid, 0)
    index = jnp.arange(2 * terms, dtype=jnp.int32)
    order = index[None, :] < index[:, None]
    rank = jnp.sum(jnp.where(valid[None] & order[:, :, None], 1, 0), 1)
    place = jnp.arange(MOST, dtype=jnp.int32)[:, None, None]
    chosen = valid[None] & (rank[None] == place)
    take = jnp.sum(jnp.where(chosen, products[None], 0), 1)
    factor = jnp.sum(jnp.where(chosen, factors[None], 0.0), 1)
    return jnp.concatenate([sources.reshape(-1), take.T.reshape(-1)]), factor.T.reshape(-1)


def tree_sum(values):
    while len(values) > 1:
        values = [sum(values[n : n + 2][1:], values[n]) for n in range(0, len(values), 2)]
    return values[0]


def stencil(pieces, others, halos, lists, j, name, lay):
    rows, width = lay.rows, lay.width
    full = (rows, width)
    arrays = list({id(array): array for array, _ in halos}.values())
    products = (lay.terms - 1) * ACTIVE

    def kernel(j_ref, index_ref, factor_ref, *refs):
        piece_refs, refs = refs[: lay.modes], refs[lay.modes :]
        other_refs, refs = refs[: lay.modes], refs[lay.modes :]
        halo_refs, refs = refs[: len(arrays)], refs[len(arrays) :]
        out_refs, (near_ref, product_ref) = refs[: lay.modes], refs[lay.modes :]
        lane = lax.broadcasted_iota(jnp.int32, full, 1)
        line = lax.broadcasted_iota(jnp.int32, full, 0)
        mode = lax.rem(j_ref[0], lay.modes)
        ref_of = {id(array): ref for array, ref in zip(arrays, halo_refs)}
        halo_parts = [(ref_of[id(array)], n) for array, n in halos]

        def to_right(value):
            return pltpu.roll(value, width - 1, 1)

        def to_left(value):
            return pltpu.roll(value, 1, 1)

        for block in range(lay.modes):
            piece_ref, other_ref = piece_refs[block], other_refs[block]
            halo_ref, n = halo_parts[block]
            for i in range(lay.fields):
                own = i < lay.quota
                at, rows_i = lay.place(block, i), slice(i * rows, (i + 1) * rows)
                edge = lay.main + 2 * i
                here = piece_ref[rows_i, :]
                right = to_right(here)
                near_ref[at, 0] = here
                near_ref[at, 1] = jnp.where(lane == width - 1, 0.0, here - right) if own else right
                high, low = piece_ref[edge + 1 : edge + 2, :], piece_ref[edge : edge + 1, :]
                near_ref[at, 2] = jnp.where(line == rows - 1, high, pltpu.roll(here, rows - 1, 0))
                near_ref[at, 3] = jnp.where(line == 0, low, pltpu.roll(here, 1, 0))
                near_ref[at, 4] = other_ref[rows_i, :]
                near_ref[at, 5] = halo_ref[n, rows_i, :]

        def operator_of(term):
            at = lay.term_place(term, mode)
            here, right, *rest = [near_ref[at, n] for n in range(6)]
            across = jnp.where(lane == width - 1, 0.0, 0.5 * (here + right))
            ends = jnp.where((lane == 0) | (lane == width - 1), 0.5 * here, 0.0)
            faces = [0.5 * (here + n) for n in rest]
            diagonal = tree_sum([ends, *faces])

            def operator(t):
                flux = across * near_ref[t, 1]
                rest = [face * near_ref[t, n + 2] for n, face in enumerate(faces)]
                return (flux - to_left(flux)) + (diagonal * near_ref[t, 0] - tree_sum(rest))

            return operator

        def apply(term, carry):
            operator = operator_of(term)
            first = (term - 1) * ACTIVE
            for n in range(ACTIVE):
                product_ref[first + n] = operator(index_ref[first + n])
            return carry

        lax.fori_loop(1, lay.terms, apply, 0)

        operator = operator_of(0)
        for block in range(lay.modes):
            for i in range(lay.quota):
                s = block * lay.quota + i
                values = [operator(s)]
                for n in range(MOST):
                    e = s * MOST + n
                    values.append(factor_ref[e] * product_ref[index_ref[products + e]])
                out_refs[block][i] = tree_sum(values)

    return pl.pallas_call(
        kernel,
        out_shape=[jax.ShapeDtypeStruct((lay.quota, rows, width), jnp.float32)] * lay.modes,
        in_specs=smem(3) + vmem(2 * lay.modes + len(arrays)),
        out_specs=vmem(lay.modes),
        scratch_shapes=[
            pltpu.VMEM((lay.places, 6, rows, width), jnp.float32),
            pltpu.VMEM((products, rows, width), jnp.float32),
        ],
        compiler_params=pltpu.CompilerParams(vmem_limit_bytes=VMEM_LIMIT),
        name=name,
    )(j, *lists, *pieces, *others, *arrays)


def after(value, *done):
    return lax.optimization_barrier((value, *done))[0]


def on_device(chaos_field, mean_field, kl_fields, pattern, coupling, slot_mode):
    spaces, modes = lax.axis_size("space"), lax.axis_size("mode")
    quota, _, height, width = chaos_field.shape
    terms = kl_fields.shape[0] + 1
    lay = Layout(quota, terms, modes, height, width)
    axes = ("space", "mode")
    devices = spaces * modes
    space = lax.axis_index("space").astype(jnp.int32)
    mode = lax.axis_index("mode").astype(jnp.int32)
    j = (lax.rem(space, PLANES) * modes + mode).reshape(1)

    def swap(piece, r):
        if r == 0:
            return piece
        return lax.ppermute(piece, axes, [(d, d ^ r) for d in range(devices)])

    def shift(pieces, crossing):
        pairs = []
        for d in range(devices):
            upper = (d // modes) % PLANES == (0 if crossing else 1)
            other = d + lay.group if upper else d - lay.group
            if 0 <= other < devices:
                pairs.append((d, other))
        main = jnp.stack([piece[: lay.main] for piece in pieces])
        return lax.ppermute(main, axes, pairs)

    field, kl = chaos_field[:, 0], kl_fields[:, 0]
    sent = [None] * lay.group
    sent[:modes] = pack(field, mean_field, kl, j, False, lay)
    sent[modes:] = pack(field, mean_field, kl, after(j, *sent[:modes]), True, lay)
    half = modes // 2
    pieces = sent[:1] + [None] * (lay.group - 1)
    for r in [*range(half, modes), *range(1, half), *range(modes, modes + half)]:
        pieces[r] = swap(sent[r], r)
    for r in range(modes + half, lay.group):
        pieces[r] = swap(after(sent[r], *pieces[half:modes]), r)
    number = jnp.arange(modes, dtype=jnp.int32)
    mine = jnp.bitwise_xor(number, mode)[:, None, None] == number[None, :, None]
    slot_mode = jnp.sum(jnp.where(mine, slot_mode.reshape(1, modes, quota), 0), 1).reshape(-1)
    lists = coupling_lists(pattern, coupling, slot_mode)
    pieces[half] = after(pieces[half], *lists)
    own_halo = shift(pieces[:modes], False)
    own_halos = [(own_halo, n) for n in range(modes)]
    crossing_halos = []
    for r in (modes, modes + half):
        halo = shift(pieces[r : r + half], True)
        crossing_halos += [(halo, n) for n in range(half)]

    own, crossing = pieces[:modes], pieces[modes:]
    crossing_out = stencil(crossing, own, own_halos, lists, j, "stencil_crossing", lay)
    own_j = after(j, *crossing_out)
    own_out = stencil(own, crossing, crossing_halos, lists, own_j, "stencil_own", lay)
    out = [*own_out, *crossing_out]
    first = range(modes + half, lay.group)
    back = {r: swap(out[r], r) for r in first}
    for r in range(half, modes):
        back[r] = swap(out[r], r)
    for n in range(half):
        ahead = [back[r] for r in first[:n]]
        ahead = [*own_out, *ahead] if n else []
        back[modes + n] = swap(after(out[modes + n], *ahead), modes + n)
    for r in range(half):
        back[r] = swap(after(out[r], *[back[r] for r in first]) if r else out[r], r)
    last = range(half, modes + half)
    shape = (quota, height, width)
    whole = unpack({r: back[r] for r in back if r not in last}, j, shape, lay)
    whole = unpack({r: back[r] for r in last}, j, shape, lay, whole)
    return whole.reshape(chaos_field.shape)


def solution(mesh):
    in_specs = (
        P("mode", "space", None, None),
        P("space", None, None),
        P(None, "space", None, None),
        P(),
        P(),
        P(),
    )
    out_specs = P("mode", "space", None, None)
    return jax.shard_map(
        on_device, mesh=mesh, in_specs=in_specs, out_specs=out_specs, check_vma=False
    )
```

```python
import jax
import jax.numpy as jnp
from jax import lax
from jax.experimental import pallas as pl
from jax.experimental.pallas import tpu as pltpu
from jax.sharding import PartitionSpec as P

VMEM_LIMIT = 40 * 1024 * 1024
PLANES = 2
ACTIVE = 49
MOST = 8
FEW = 3
MANY = 28


class Layout:
    def __init__(self, quota, terms, modes, height, width):
        self.modes = modes
        self.group = PLANES * modes
        self.rows = height // self.group
        self.width = width
        self.terms = terms
        self.quota = quota
        self.slots = quota * modes
        self.share = -(-terms // modes)
        self.fields = quota + self.share
        self.main = self.fields * self.rows
        self.parts = self.fields + -(-2 * self.fields // self.rows)
        self.piece = self.parts * self.rows
        self.places = self.fields * modes

    def edge(self, i):
        return self.fields + 2 * i // self.rows, 2 * i % self.rows

    def place(self, block, i):
        if i < self.quota:
            return block * self.quota + i
        return self.slots + block * self.share + (i - self.quota)

    def term_place(self, term, mode):
        owner = lax.div(term, self.share)
        block = jnp.bitwise_xor(owner, mode)
        return self.slots + block * self.share + (term - owner * self.share)


def vmem(count):
    return [pl.BlockSpec(memory_space=pltpu.VMEM)] * count


def smem(count):
    return [pl.BlockSpec(memory_space=pltpu.SMEM)] * count


def pack(field, mean, kl, j, crossing, lay):
    kl_terms = kl.shape[0]
    rows, width, modes, quota = lay.rows, lay.width, lay.modes, lay.quota
    half = modes * rows
    tile = 8

    def kernel(j_ref, field_ref, mean_ref, kl_ref, *refs):
        out_refs, (stage_ref, past_ref, in_sems) = refs[:modes], refs[modes:]
        plane = j_ref[0] // modes
        mode = j_ref[0] - plane * modes
        side = 1 - plane if crossing else plane
        start = side * half
        beside = pl.multiple_of(half - side * tile, tile)

        def load(n, begin=True):
            if n < modes:
                at, target = pl.ds(pl.multiple_of(start + n * rows, tile), rows), stage_ref.at[n]
            else:
                at, target = pl.ds(beside, tile), past_ref
            copies = [
                pltpu.make_async_copy(
                    field_ref.at[:, at, :], target.at[pl.ds(0, quota)], in_sems.at[n, 0]
                )
            ]
            if begin:
                copies[0].start()
            for i in range(lay.share):
                term = mode * lay.share + i
                into, sem = target.at[quota + i], in_sems.at[n, 1 + i]
                if not begin:
                    copies.append(pltpu.make_async_copy(mean_ref.at[0, at, :], into, sem))
                    continue

                @pl.when(term == 0)
                def _():
                    pltpu.make_async_copy(mean_ref.at[0, at, :], into, sem).start()

                @pl.when(term > 0)
                def _():
                    source = kl_ref.at[jnp.clip(term - 1, 0, kl_terms - 1), at, :]
                    pltpu.make_async_copy(source, into, sem).start()

            return copies

        for n in range(modes + 1):
            load(n)
        for n in range(modes + 1):
            for made in load(n, begin=False):
                made.wait()
        low_there = jnp.where(side == 0, 0.0, 1.0)
        high_there = jnp.where(side == PLANES - 1, 0.0, 1.0)
        for n in range(modes):
            for i in range(lay.fields):
                if n > 0:
                    low = stage_ref[n - 1, i, rows - 1 :]
                else:
                    low = past_ref[i, tile - 1 :] * low_there
                if n < modes - 1:
                    high = stage_ref[n + 1, i, :1]
                else:
                    high = past_ref[i, :1] * high_there
                part, line = lay.edge(i)
                stage_ref[n, part, line : line + 1] = low
                stage_ref[n, part, line + 1 : line + 2] = high
            part, line = lay.edge(lay.fields)
            if part < lay.parts:
                stage_ref[n, part, line:] = jnp.zeros((rows - line, width), jnp.float32)
        for n, out_ref in enumerate(out_refs):
            to = jnp.bitwise_xor(mode, n)
            for part in range(lay.parts):
                out_ref[part] = stage_ref[to, part]

    shape = (lay.parts, rows, width)
    sent = pl.pallas_call(
        kernel,
        out_shape=[pltpu.VMEM(shape, jnp.float32)] * modes,
        in_specs=smem(1) + [pl.BlockSpec(memory_space=pltpu.HBM)] * 3,
        out_specs=vmem(modes),
        scratch_shapes=[
            pltpu.VMEM((modes, *shape), jnp.float32),
            pltpu.VMEM((lay.fields, tile, width), jnp.float32),
            pltpu.SemaphoreType.DMA((modes + 1, 1 + lay.share)),
        ],
        compiler_params=pltpu.CompilerParams(vmem_limit_bytes=VMEM_LIMIT),
        name="pack_crossing" if crossing else "pack_own",
    )(j, *[pltpu.with_memory_space_constraint(x, pltpu.HBM) for x in (field, mean, kl)])
    return [piece.reshape(lay.piece, width) for piece in sent]


def unpack(pieces, j, shape, lay, whole=None):
    rows = lay.rows
    there = [] if whole is None else [whole]

    def kernel(j_ref, *refs):
        piece_refs, out_ref, sems = refs[: len(pieces)], refs[-2], refs[-1]
        copies = []
        for n, (r, piece_ref) in enumerate(zip(pieces, piece_refs)):
            start = pl.multiple_of(jnp.bitwise_xor(j_ref[0], r) * rows, 8)
            made = pltpu.make_async_copy(
                piece_ref, out_ref.at[:, pl.ds(start, rows), :], sems.at[n]
            )
            made.start()
            copies.append(made)
        for made in copies:
            made.wait()

    return pl.pallas_call(
        kernel,
        out_shape=pltpu.HBM(shape, jnp.float32),
        in_specs=smem(1) + vmem(len(pieces)) + [pl.BlockSpec(memory_space=pltpu.HBM)] * len(there),
        out_specs=pl.BlockSpec(memory_space=pltpu.HBM),
        scratch_shapes=[pltpu.SemaphoreType.DMA((len(pieces),))],
        input_output_aliases={1 + len(pieces): 0} if there else {},
        compiler_params=pltpu.CompilerParams(vmem_limit_bytes=VMEM_LIMIT),
        name="unpack_last" if there else "unpack_first",
    )(j, *pieces.values(), *there)


def coupling_lists(pattern, coupling, slot_mode):
    masked = (coupling * pattern.astype(jnp.float32))[1:]
    terms, modes = masked.shape[0], masked.shape[1]
    number = jnp.arange(modes, dtype=jnp.int32)
    one_hot = (slot_mode[:, None] == number[None, :]).astype(jnp.float32)
    coupled = jnp.einsum(
        "sa,kab,tb->kst", one_hot, masked, one_hot, precision=lax.Precision.HIGHEST
    )
    there = coupled != 0.0
    column = number[None, None, :]
    first = jnp.min(jnp.where(there, column, modes), 2)
    last = jnp.max(jnp.where(there, column, -1), 2)
    active = first < modes
    earlier = column < number[None, :, None]
    rank = jnp.sum(jnp.where(active[:, None, :] & earlier, 1, 0), 2)
    place = jnp.arange(ACTIVE, dtype=jnp.int32)[None, :, None]
    chosen = active[:, None, :] & (rank[:, None, :] == place)
    sources = jnp.sum(jnp.where(chosen, column, 0), 2)

    base = ACTIVE * jnp.arange(terms, dtype=jnp.int32)[:, None]
    products, factors, valid = [], [], []
    for chosen_t, is_valid in ((first, active), (last, last > first)):
        before = active[:, None, :] & (column < chosen_t[:, :, None])
        products.append(base + jnp.sum(jnp.where(before, 1, 0), 2))
        factors.append(jnp.sum(jnp.where(column == chosen_t[:, :, None], coupled, 0.0), 2))
        valid.append(is_valid)
    products = jnp.concatenate(products, 0)
    factors = jnp.concatenate(factors, 0)
    valid = jnp.concatenate(valid, 0)
    index = jnp.arange(2 * terms, dtype=jnp.int32)
    order = index[None, :] < index[:, None]
    rank = jnp.sum(jnp.where(valid[None] & order[:, :, None], 1, 0), 1)
    place = jnp.arange(MOST, dtype=jnp.int32)[:, None, None]
    chosen = valid[None] & (rank[None] == place)
    take = jnp.sum(jnp.where(chosen, products[None], 0), 1)
    factor = jnp.sum(jnp.where(chosen, factors[None], 0.0), 1)
    return sources, take, factor, jnp.sum(jnp.where(valid, 1, 0), 0)


def kernel_lists(sources, take, factor, count):
    number = jnp.arange(count.shape[0], dtype=jnp.int32)
    many = count > FEW
    rank = jnp.sum(jnp.where(many[None, :] & (number[None, :] < number[:, None]), 1, 0), 1)
    place = jnp.arange(MANY, dtype=jnp.int32)[None, :, None]
    chosen = many[None, None, :] & (rank[None, None, :] == place)
    take_more = jnp.sum(jnp.where(chosen, take[FEW:, None, :], 0), 2)
    factor_more = jnp.sum(jnp.where(chosen, factor[FEW:, None, :], 0.0), 2)
    more = jnp.where(many, rank, MANY)
    indices = [sources, take[:FEW].T, take_more.T, more]
    factors = [factor[:FEW].T, factor_more.T]
    return tuple(
        jnp.concatenate([part.reshape(-1) for part in parts]) for parts in (indices, factors)
    )


def tree_sum(values):
    while len(values) > 1:
        values = [sum(values[n : n + 2][1:], values[n]) for n in range(0, len(values), 2)]
    return values[0]


def stencil(pieces, others, halos, lists, j, name, lay):
    rows, width = lay.rows, lay.width
    full = (rows, width)
    arrays = list({id(array): array for array, _ in halos}.values())
    products = (lay.terms - 1) * ACTIVE

    def kernel(j_ref, index_ref, factor_ref, *refs):
        piece_refs, refs = refs[: lay.modes], refs[lay.modes :]
        other_refs, refs = refs[: lay.modes], refs[lay.modes :]
        halo_refs, refs = refs[: len(arrays)], refs[len(arrays) :]
        out_refs, (near_ref, product_ref, more_ref) = refs[: lay.modes], refs[lay.modes :]
        lane = lax.broadcasted_iota(jnp.int32, full, 1)
        line = lax.broadcasted_iota(jnp.int32, full, 0)
        mode = lax.rem(j_ref[0], lay.modes)
        ref_of = {id(array): ref for array, ref in zip(arrays, halo_refs)}
        halo_parts = [(ref_of[id(array)], n) for array, n in halos]

        def to_right(value):
            return pltpu.roll(value, width - 1, 1)

        def to_left(value):
            return pltpu.roll(value, 1, 1)

        for block in range(lay.modes):
            piece_ref, other_ref = piece_refs[block], other_refs[block]
            halo_ref, n = halo_parts[block]
            for i in range(lay.fields):
                own = i < lay.quota
                at, rows_i = lay.place(block, i), slice(i * rows, (i + 1) * rows)
                edge = lay.main + 2 * i
                here = piece_ref[rows_i, :]
                right = to_right(here)
                near_ref[at, 0] = here
                near_ref[at, 1] = jnp.where(lane == width - 1, 0.0, here - right) if own else right
                high, low = piece_ref[edge + 1 : edge + 2, :], piece_ref[edge : edge + 1, :]
                near_ref[at, 2] = jnp.where(line == rows - 1, high, pltpu.roll(here, rows - 1, 0))
                near_ref[at, 3] = jnp.where(line == 0, low, pltpu.roll(here, 1, 0))
                near_ref[at, 4] = other_ref[rows_i, :]
                near_ref[at, 5] = halo_ref[n, rows_i, :]

        def operator_of(term):
            at = lay.term_place(term, mode)
            here, right, *rest = [near_ref[at, n] for n in range(6)]
            across = jnp.where(lane == width - 1, 0.0, 0.5 * (here + right))
            ends = jnp.where((lane == 0) | (lane == width - 1), 0.5 * here, 0.0)
            faces = [0.5 * (here + n) for n in rest]
            diagonal = tree_sum([ends, *faces])

            def operator(t):
                flux = across * near_ref[t, 1]
                rest = [face * near_ref[t, n + 2] for n, face in enumerate(faces)]
                return (flux - to_left(flux)) + (diagonal * near_ref[t, 0] - tree_sum(rest))

            return operator

        def apply(term, carry):
            operator = operator_of(term)
            first = (term - 1) * ACTIVE
            for n in range(ACTIVE):
                product_ref[first + n] = operator(index_ref[first + n])
            return carry

        lax.fori_loop(1, lay.terms, apply, 0)

        def taken(first, count):
            return [
                factor_ref[e] * product_ref[index_ref[products + e]]
                for e in range(first, first + count)
            ]

        few, rest = FEW * lay.slots, MOST - FEW
        for n in range(MANY):
            more_ref[n] = tree_sum(taken(few + n * rest, rest))
        more_ref[MANY] = jnp.zeros(full, jnp.float32)
        more_at = products + few + MANY * rest
        operator = operator_of(0)
        for block in range(lay.modes):
            for i in range(lay.quota):
                s = block * lay.quota + i
                more = more_ref[index_ref[more_at + s]]
                out_refs[block][i] = tree_sum([operator(s), *taken(FEW * s, FEW), more])

    return pl.pallas_call(
        kernel,
        out_shape=[jax.ShapeDtypeStruct((lay.quota, rows, width), jnp.float32)] * lay.modes,
        in_specs=smem(3) + vmem(2 * lay.modes + len(arrays)),
        out_specs=vmem(lay.modes),
        scratch_shapes=[
            pltpu.VMEM((lay.places, 6, rows, width), jnp.float32),
            pltpu.VMEM((products, rows, width), jnp.float32),
            pltpu.VMEM((MANY + 1, rows, width), jnp.float32),
        ],
        compiler_params=pltpu.CompilerParams(vmem_limit_bytes=VMEM_LIMIT),
        name=name,
    )(j, *lists, *pieces, *others, *arrays)


def after(value, *done):
    return lax.optimization_barrier((value, *done))[0]


def on_device(chaos_field, mean_field, kl_fields, pattern, coupling, slot_mode):
    spaces, modes = lax.axis_size("space"), lax.axis_size("mode")
    quota, _, height, width = chaos_field.shape
    terms = kl_fields.shape[0] + 1
    lay = Layout(quota, terms, modes, height, width)
    axes = ("space", "mode")
    devices = spaces * modes
    space = lax.axis_index("space").astype(jnp.int32)
    mode = lax.axis_index("mode").astype(jnp.int32)
    j = (lax.rem(space, PLANES) * modes + mode).reshape(1)

    def swap(piece, r):
        if r == 0:
            return piece
        return lax.ppermute(piece, axes, [(d, d ^ r) for d in range(devices)])

    def shift(pieces, crossing):
        pairs = []
        for d in range(devices):
            upper = (d // modes) % PLANES == (0 if crossing else 1)
            other = d + lay.group if upper else d - lay.group
            if 0 <= other < devices:
                pairs.append((d, other))
        main = jnp.stack([piece[: lay.main] for piece in pieces])
        return lax.ppermute(main, axes, pairs)

    field, kl = chaos_field[:, 0], kl_fields[:, 0]
    sent = [None] * lay.group
    sent[:modes] = pack(field, mean_field, kl, j, False, lay)
    sent[modes:] = pack(field, mean_field, kl, after(j, *sent[:modes]), True, lay)
    half = modes // 2
    pieces = sent[:1] + [None] * (lay.group - 1)
    for r in [*range(half, modes), *range(1, half), *range(modes, modes + half)]:
        pieces[r] = swap(sent[r], r)
    for r in range(modes + half, lay.group):
        pieces[r] = swap(after(sent[r], *pieces[half:modes]), r)
    number = jnp.arange(modes, dtype=jnp.int32)
    mine = jnp.bitwise_xor(number, mode)[:, None, None] == number[None, :, None]
    slot_mode = jnp.sum(jnp.where(mine, slot_mode.reshape(1, modes, quota), 0), 1).reshape(-1)
    *lists, count = coupling_lists(pattern, coupling, slot_mode)
    pieces[half] = after(pieces[half], *lists, count)
    lists = kernel_lists(*lists, after(count, pieces[modes]))
    own_halo = shift(pieces[:modes], False)
    own_halos = [(own_halo, n) for n in range(modes)]
    early_halo = shift(pieces[modes : modes + half], True)
    crossing_halos = [(early_halo, n) for n in range(half)]
    for r in range(modes + half, lay.group):
        crossing_halos.append((shift(pieces[r : r + 1], True), 0))

    own, crossing = pieces[:modes], pieces[modes:]
    crossing_out = stencil(crossing, own, own_halos, lists, j, "stencil_crossing", lay)
    own_j = after(j, *crossing_out)
    own_out = stencil(own, crossing, crossing_halos, lists, own_j, "stencil_own", lay)
    out = [*own_out, *crossing_out]
    first = range(modes + half, lay.group)
    back = {r: swap(out[r], r) for r in first}
    for r in range(half, modes):
        back[r] = swap(out[r], r)
    for n in range(half):
        ahead = [back[r] for r in first[:n]]
        back[modes + n] = swap(after(out[modes + n], *own_out, *ahead), modes + n)
    for r in range(half):
        back[r] = swap(after(out[r], back[first[-1]]) if r else out[r], r)
    last = range(half, modes + half)
    shape = (quota, height, width)
    whole = unpack({r: back[r] for r in back if r not in last}, j, shape, lay)
    whole = unpack({r: back[r] for r in last}, j, shape, lay, whole)
    return whole.reshape(chaos_field.shape)


def solution(mesh):
    in_specs = (
        P("mode", "space", None, None),
        P("space", None, None),
        P(None, "space", None, None),
        P(),
        P(),
        P(),
    )
    out_specs = P("mode", "space", None, None)
    return jax.shard_map(
        on_device, mesh=mesh, in_specs=in_specs, out_specs=out_specs, check_vma=False
    )
```

```python
import jax
import jax.numpy as jnp
from jax import lax
from jax.experimental import pallas as pl
from jax.experimental.pallas import tpu as pltpu
from jax.sharding import PartitionSpec as P

VMEM_LIMIT = 20 * 1024 * 1024
PLANES = 2
ACTIVE = 49
MOST = 8
FEW = 3
MANY = 28


class Layout:
    def __init__(self, quota, terms, modes, height, width):
        self.modes = modes
        self.group = PLANES * modes
        self.rows = height // self.group
        self.width = width
        self.terms = terms
        self.quota = quota
        self.slots = quota * modes
        self.share = -(-terms // modes)
        self.fields = quota + self.share
        self.main = self.fields * self.rows
        self.parts = self.fields + -(-2 * self.fields // self.rows)
        self.piece = self.parts * self.rows
        self.places = self.fields * modes

    def edge(self, i):
        return self.fields + 2 * i // self.rows, 2 * i % self.rows

    def place(self, block, i):
        if i < self.quota:
            return block * self.quota + i
        return self.slots + block * self.share + (i - self.quota)

    def term_place(self, term, mode):
        owner = lax.div(term, self.share)
        block = jnp.bitwise_xor(owner, mode)
        return self.slots + block * self.share + (term - owner * self.share)


def vmem(count):
    return [pl.BlockSpec(memory_space=pltpu.VMEM)] * count


def smem(count):
    return [pl.BlockSpec(memory_space=pltpu.SMEM)] * count


def pack(field, mean, kl, j, crossing, lay):
    kl_terms = kl.shape[0]
    rows, width, modes, quota = lay.rows, lay.width, lay.modes, lay.quota
    half = modes * rows
    tile = 8

    def kernel(j_ref, field_ref, mean_ref, kl_ref, *refs):
        out_refs, (stage_ref, past_ref, in_sems) = refs[:modes], refs[modes:]
        plane = j_ref[0] // modes
        mode = j_ref[0] - plane * modes
        side = 1 - plane if crossing else plane
        start = side * half
        beside = pl.multiple_of(half - side * tile, tile)

        def load(n, begin=True):
            if n < modes:
                at, target = pl.ds(pl.multiple_of(start + n * rows, tile), rows), stage_ref.at[n]
            else:
                at, target = pl.ds(beside, tile), past_ref
            copies = [
                pltpu.make_async_copy(
                    field_ref.at[:, at, :], target.at[pl.ds(0, quota)], in_sems.at[n, 0]
                )
            ]
            if begin:
                copies[0].start()
            for i in range(lay.share):
                term = mode * lay.share + i
                into, sem = target.at[quota + i], in_sems.at[n, 1 + i]
                if not begin:
                    copies.append(pltpu.make_async_copy(mean_ref.at[0, at, :], into, sem))
                    continue

                @pl.when(term == 0)
                def _():
                    pltpu.make_async_copy(mean_ref.at[0, at, :], into, sem).start()

                @pl.when(term > 0)
                def _():
                    source = kl_ref.at[jnp.clip(term - 1, 0, kl_terms - 1), at, :]
                    pltpu.make_async_copy(source, into, sem).start()

            return copies

        for n in range(modes + 1):
            load(n)
        for n in range(modes + 1):
            for made in load(n, begin=False):
                made.wait()
        low_there = jnp.where(side == 0, 0.0, 1.0)
        high_there = jnp.where(side == PLANES - 1, 0.0, 1.0)
        for n in range(modes):
            for i in range(lay.fields):
                if n > 0:
                    low = stage_ref[n - 1, i, rows - 1 :]
                else:
                    low = past_ref[i, tile - 1 :] * low_there
                if n < modes - 1:
                    high = stage_ref[n + 1, i, :1]
                else:
                    high = past_ref[i, :1] * high_there
                part, line = lay.edge(i)
                stage_ref[n, part, line : line + 1] = low
                stage_ref[n, part, line + 1 : line + 2] = high
            part, line = lay.edge(lay.fields)
            if part < lay.parts:
                stage_ref[n, part, line:] = jnp.zeros((rows - line, width), jnp.float32)
        for n, out_ref in enumerate(out_refs):
            to = jnp.bitwise_xor(mode, n)
            for part in range(lay.parts):
                out_ref[part] = stage_ref[to, part]

    shape = (lay.parts, rows, width)
    sent = pl.pallas_call(
        kernel,
        out_shape=[pltpu.VMEM(shape, jnp.float32)] * modes,
        in_specs=smem(1) + [pl.BlockSpec(memory_space=pltpu.HBM)] * 3,
        out_specs=vmem(modes),
        scratch_shapes=[
            pltpu.VMEM((modes, *shape), jnp.float32),
            pltpu.VMEM((lay.fields, tile, width), jnp.float32),
            pltpu.SemaphoreType.DMA((modes + 1, 1 + lay.share)),
        ],
        compiler_params=pltpu.CompilerParams(vmem_limit_bytes=VMEM_LIMIT),
        name="pack_crossing" if crossing else "pack_own",
    )(j, *[pltpu.with_memory_space_constraint(x, pltpu.HBM) for x in (field, mean, kl)])
    return [piece.reshape(lay.piece, width) for piece in sent]


def unpack(pieces, j, shape, lay, whole=None):
    rows = lay.rows
    there = [] if whole is None else [whole]

    def kernel(j_ref, *refs):
        piece_refs, out_ref, sems = refs[: len(pieces)], refs[-2], refs[-1]
        copies = []
        for n, (r, piece_ref) in enumerate(zip(pieces, piece_refs)):
            start = pl.multiple_of(jnp.bitwise_xor(j_ref[0], r) * rows, 8)
            made = pltpu.make_async_copy(
                piece_ref, out_ref.at[:, pl.ds(start, rows), :], sems.at[n]
            )
            made.start()
            copies.append(made)
        for made in copies:
            made.wait()

    return pl.pallas_call(
        kernel,
        out_shape=pltpu.HBM(shape, jnp.float32),
        in_specs=smem(1) + vmem(len(pieces)) + [pl.BlockSpec(memory_space=pltpu.HBM)] * len(there),
        out_specs=pl.BlockSpec(memory_space=pltpu.HBM),
        scratch_shapes=[pltpu.SemaphoreType.DMA((len(pieces),))],
        input_output_aliases={1 + len(pieces): 0} if there else {},
        compiler_params=pltpu.CompilerParams(vmem_limit_bytes=VMEM_LIMIT),
        name="unpack_last" if there else "unpack_first",
    )(j, *pieces.values(), *there)


def coupling_lists(pattern, coupling, slot_mode):
    masked = (coupling * pattern.astype(jnp.float32))[1:]
    terms, modes = masked.shape[0], masked.shape[1]
    number = jnp.arange(modes, dtype=jnp.int32)
    one_hot = (slot_mode[:, None] == number[None, :]).astype(jnp.float32)
    coupled = jnp.einsum(
        "sa,kab,tb->kst", one_hot, masked, one_hot, precision=lax.Precision.HIGHEST
    )
    there = coupled != 0.0
    column = number[None, None, :]
    first = jnp.min(jnp.where(there, column, modes), 2)
    last = jnp.max(jnp.where(there, column, -1), 2)
    active = first < modes
    earlier = column < number[None, :, None]
    rank = jnp.sum(jnp.where(active[:, None, :] & earlier, 1, 0), 2)
    place = jnp.arange(ACTIVE, dtype=jnp.int32)[None, :, None]
    chosen = active[:, None, :] & (rank[:, None, :] == place)
    sources = jnp.sum(jnp.where(chosen, column, 0), 2)

    base = ACTIVE * jnp.arange(terms, dtype=jnp.int32)[:, None]
    products, factors, valid = [], [], []
    for chosen_t, is_valid in ((first, active), (last, last > first)):
        before = active[:, None, :] & (column < chosen_t[:, :, None])
        products.append(base + jnp.sum(jnp.where(before, 1, 0), 2))
        factors.append(jnp.sum(jnp.where(column == chosen_t[:, :, None], coupled, 0.0), 2))
        valid.append(is_valid)
    products = jnp.concatenate(products, 0)
    factors = jnp.concatenate(factors, 0)
    valid = jnp.concatenate(valid, 0)
    index = jnp.arange(2 * terms, dtype=jnp.int32)
    order = index[None, :] < index[:, None]
    rank = jnp.sum(jnp.where(valid[None] & order[:, :, None], 1, 0), 1)
    place = jnp.arange(MOST, dtype=jnp.int32)[:, None, None]
    chosen = valid[None] & (rank[None] == place)
    take = jnp.sum(jnp.where(chosen, products[None], 0), 1)
    factor = jnp.sum(jnp.where(chosen, factors[None], 0.0), 1)
    return sources, take, factor, jnp.sum(jnp.where(valid, 1, 0), 0)


def kernel_lists(sources, take, factor, count):
    number = jnp.arange(count.shape[0], dtype=jnp.int32)
    many = count > FEW
    rank = jnp.sum(jnp.where(many[None, :] & (number[None, :] < number[:, None]), 1, 0), 1)
    place = jnp.arange(MANY, dtype=jnp.int32)[None, :, None]
    chosen = many[None, None, :] & (rank[None, None, :] == place)
    take_more = jnp.sum(jnp.where(chosen, take[FEW:, None, :], 0), 2)
    factor_more = jnp.sum(jnp.where(chosen, factor[FEW:, None, :], 0.0), 2)
    more = jnp.where(many, rank, MANY)
    indices = [sources, take[:FEW].T, take_more.T, more]
    factors = [factor[:FEW].T, factor_more.T]
    return tuple(
        jnp.concatenate([part.reshape(-1) for part in parts]) for parts in (indices, factors)
    )


def tree_sum(values):
    while len(values) > 1:
        values = [sum(values[n : n + 2][1:], values[n]) for n in range(0, len(values), 2)]
    return values[0]


def stencil(pieces, others, halos, lists, j, name, lay):
    rows, width = lay.rows, lay.width
    full = (rows, width)
    arrays = list({id(array): array for array, _ in halos}.values())
    products = (lay.terms - 1) * ACTIVE

    def kernel(j_ref, index_ref, factor_ref, *refs):
        piece_refs, refs = refs[: lay.modes], refs[lay.modes :]
        other_refs, refs = refs[: lay.modes], refs[lay.modes :]
        halo_refs, refs = refs[: len(arrays)], refs[len(arrays) :]
        out_refs, (near_ref, product_ref, more_ref) = refs[: lay.modes], refs[lay.modes :]
        lane = lax.broadcasted_iota(jnp.int32, full, 1)
        line = lax.broadcasted_iota(jnp.int32, full, 0)
        mode = lax.rem(j_ref[0], lay.modes)
        ref_of = {id(array): ref for array, ref in zip(arrays, halo_refs)}
        halo_parts = [(ref_of[id(array)], n) for array, n in halos]

        def to_right(value):
            return pltpu.roll(value, width - 1, 1)

        def to_left(value):
            return pltpu.roll(value, 1, 1)

        for block in range(lay.modes):
            piece_ref, other_ref = piece_refs[block], other_refs[block]
            halo_ref, n = halo_parts[block]
            for i in range(lay.fields):
                own = i < lay.quota
                at, rows_i = lay.place(block, i), slice(i * rows, (i + 1) * rows)
                edge = lay.main + 2 * i
                here = piece_ref[rows_i, :]
                right = to_right(here)
                near_ref[at, 0] = here
                near_ref[at, 1] = jnp.where(lane == width - 1, 0.0, here - right) if own else right
                high, low = piece_ref[edge + 1 : edge + 2, :], piece_ref[edge : edge + 1, :]
                near_ref[at, 2] = jnp.where(line == rows - 1, high, pltpu.roll(here, rows - 1, 0))
                near_ref[at, 3] = jnp.where(line == 0, low, pltpu.roll(here, 1, 0))
                near_ref[at, 4] = other_ref[rows_i, :]
                near_ref[at, 5] = halo_ref[n, rows_i, :]

        def operator_of(term):
            at = lay.term_place(term, mode)
            here, right, *rest = [near_ref[at, n] for n in range(6)]
            across = jnp.where(lane == width - 1, 0.0, 0.5 * (here + right))
            ends = jnp.where((lane == 0) | (lane == width - 1), 0.5 * here, 0.0)
            faces = [0.5 * (here + n) for n in rest]
            diagonal = tree_sum([ends, *faces])

            def operator(t):
                flux = across * near_ref[t, 1]
                rest = [face * near_ref[t, n + 2] for n, face in enumerate(faces)]
                return (flux - to_left(flux)) + (diagonal * near_ref[t, 0] - tree_sum(rest))

            return operator

        def apply(term, carry):
            operator = operator_of(term)
            first = (term - 1) * ACTIVE
            for n in range(ACTIVE):
                product_ref[first + n] = operator(index_ref[first + n])
            return carry

        lax.fori_loop(1, lay.terms, apply, 0)

        def taken(first, count):
            return [
                factor_ref[e] * product_ref[index_ref[products + e]]
                for e in range(first, first + count)
            ]

        few, rest = FEW * lay.slots, MOST - FEW
        for n in range(MANY):
            more_ref[n] = tree_sum(taken(few + n * rest, rest))
        more_ref[MANY] = jnp.zeros(full, jnp.float32)
        more_at = products + few + MANY * rest
        operator = operator_of(0)
        for block in range(lay.modes):
            for i in range(lay.quota):
                s = block * lay.quota + i
                more = more_ref[index_ref[more_at + s]]
                out_refs[block][i] = tree_sum([operator(s), *taken(FEW * s, FEW), more])

    return pl.pallas_call(
        kernel,
        out_shape=[jax.ShapeDtypeStruct((lay.quota, rows, width), jnp.float32)] * lay.modes,
        in_specs=smem(3) + vmem(2 * lay.modes + len(arrays)),
        out_specs=vmem(lay.modes),
        scratch_shapes=[
            pltpu.VMEM((lay.places, 6, rows, width), jnp.float32),
            pltpu.VMEM((products, rows, width), jnp.float32),
            pltpu.VMEM((MANY + 1, rows, width), jnp.float32),
        ],
        compiler_params=pltpu.CompilerParams(vmem_limit_bytes=VMEM_LIMIT),
        name=name,
    )(j, *lists, *pieces, *others, *arrays)


def after(value, *done):
    return lax.optimization_barrier((value, *done))[0]


def on_device(chaos_field, mean_field, kl_fields, pattern, coupling, slot_mode):
    spaces, modes = lax.axis_size("space"), lax.axis_size("mode")
    quota, _, height, width = chaos_field.shape
    terms = kl_fields.shape[0] + 1
    lay = Layout(quota, terms, modes, height, width)
    axes = ("space", "mode")
    devices = spaces * modes
    space = lax.axis_index("space").astype(jnp.int32)
    mode = lax.axis_index("mode").astype(jnp.int32)
    j = (lax.rem(space, PLANES) * modes + mode).reshape(1)

    def swap(piece, r):
        if r == 0:
            return piece
        return lax.ppermute(piece, axes, [(d, d ^ r) for d in range(devices)])

    def shift(pieces, crossing):
        pairs = []
        for d in range(devices):
            upper = (d // modes) % PLANES == (0 if crossing else 1)
            other = d + lay.group if upper else d - lay.group
            if 0 <= other < devices:
                pairs.append((d, other))
        main = jnp.stack([piece[: lay.main] for piece in pieces])
        return lax.ppermute(main, axes, pairs)

    field, kl = chaos_field[:, 0], kl_fields[:, 0]
    sent = [None] * lay.group
    sent[:modes] = pack(field, mean_field, kl, j, False, lay)
    sent[modes:] = pack(field, mean_field, kl, after(j, *sent[:modes]), True, lay)
    half = modes // 2
    pieces = sent[:1] + [None] * (lay.group - 1)
    for r in [*range(half, modes), *range(1, half), *range(modes, modes + half)]:
        pieces[r] = swap(sent[r], r)
    for r in range(modes + half, lay.group):
        pieces[r] = swap(after(sent[r], *pieces[half:modes]), r)
    number = jnp.arange(modes, dtype=jnp.int32)
    mine = jnp.bitwise_xor(number, mode)[:, None, None] == number[None, :, None]
    slot_mode = jnp.sum(jnp.where(mine, slot_mode.reshape(1, modes, quota), 0), 1).reshape(-1)
    *lists, count = coupling_lists(pattern, coupling, slot_mode)
    pieces[half] = after(pieces[half], *lists, count)
    lists = kernel_lists(*lists, after(count, pieces[modes]))
    own_halo = shift(pieces[:modes], False)
    own_halos = [(own_halo, n) for n in range(modes)]
    early_halo = shift(pieces[modes : modes + half], True)
    crossing_halos = [(early_halo, n) for n in range(half)]
    for r in range(modes + half, lay.group):
        crossing_halos.append((shift(pieces[r : r + 1], True), 0))

    own, crossing = pieces[:modes], pieces[modes:]
    crossing_out = stencil(crossing, own, own_halos, lists, j, "stencil_crossing", lay)
    own_j = after(j, *crossing_out)
    own_out = stencil(own, crossing, crossing_halos, lists, own_j, "stencil_own", lay)
    out = [*own_out, *crossing_out]
    first = range(modes + half, lay.group)
    back = {r: swap(out[r], r) for r in first}
    for r in range(half, modes):
        back[r] = swap(out[r], r)
    for n in range(half):
        ahead = [back[r] for r in first[:n]]
        back[modes + n] = swap(after(out[modes + n], *own_out, *ahead), modes + n)
    for r in range(half):
        back[r] = swap(after(out[r], back[first[-1]]) if r else out[r], r)
    last = range(half, modes + half)
    shape = (quota, height, width)
    whole = unpack({r: back[r] for r in back if r not in last}, j, shape, lay)
    whole = unpack({r: back[r] for r in last}, j, shape, lay, whole)
    return whole.reshape(chaos_field.shape)


def solution(mesh):
    in_specs = (
        P("mode", "space", None, None),
        P("space", None, None),
        P(None, "space", None, None),
        P(),
        P(),
        P(),
    )
    out_specs = P("mode", "space", None, None)
    return jax.shard_map(
        on_device, mesh=mesh, in_specs=in_specs, out_specs=out_specs, check_vma=False
    )
```

```python
import jax
import jax.numpy as jnp
from jax import lax
from jax.experimental import pallas as pl
from jax.experimental.pallas import tpu as pltpu
from jax.sharding import PartitionSpec as P

VMEM_LIMIT = 20 * 1024 * 1024
PLANES = 2
ACTIVE = 49
MOST = 8
FEW = 3
MANY = 28


class Layout:
    def __init__(self, quota, terms, modes, height, width):
        self.modes = modes
        self.group = PLANES * modes
        self.rows = height // self.group
        self.width = width
        self.terms = terms
        self.quota = quota
        self.slots = quota * modes
        self.share = -(-terms // modes)
        self.fields = quota + self.share
        self.main = self.fields * self.rows
        self.parts = self.fields + -(-2 * self.fields // self.rows)
        self.piece = self.parts * self.rows
        self.places = self.fields * modes

    def edge(self, i):
        return self.fields + 2 * i // self.rows, 2 * i % self.rows

    def place(self, block, i):
        if i < self.quota:
            return block * self.quota + i
        return self.slots + block * self.share + (i - self.quota)

    def term_place(self, term, mode):
        owner = lax.div(term, self.share)
        block = jnp.bitwise_xor(owner, mode)
        return self.slots + block * self.share + (term - owner * self.share)


def vmem(count):
    return [pl.BlockSpec(memory_space=pltpu.VMEM)] * count


def smem(count):
    return [pl.BlockSpec(memory_space=pltpu.SMEM)] * count


def pack(field, mean, kl, j, crossing, lay):
    kl_terms = kl.shape[0]
    rows, width, modes, quota = lay.rows, lay.width, lay.modes, lay.quota
    half = modes * rows
    tile = 8

    def kernel(j_ref, field_ref, mean_ref, kl_ref, *refs):
        out_refs, (stage_ref, past_ref, in_sems) = refs[:modes], refs[modes:]
        plane = j_ref[0] // modes
        mode = j_ref[0] - plane * modes
        side = 1 - plane if crossing else plane
        start = side * half
        beside = pl.multiple_of(half - side * tile, tile)

        def load(n, begin=True):
            if n < modes:
                at, target = pl.ds(pl.multiple_of(start + n * rows, tile), rows), stage_ref.at[n]
            else:
                at, target = pl.ds(beside, tile), past_ref
            copies = [
                pltpu.make_async_copy(
                    field_ref.at[:, at, :], target.at[pl.ds(0, quota)], in_sems.at[n, 0]
                )
            ]
            if begin:
                copies[0].start()
            for i in range(lay.share):
                term = mode * lay.share + i
                into, sem = target.at[quota + i], in_sems.at[n, 1 + i]
                if not begin:
                    copies.append(pltpu.make_async_copy(mean_ref.at[0, at, :], into, sem))
                    continue

                @pl.when(term == 0)
                def _():
                    pltpu.make_async_copy(mean_ref.at[0, at, :], into, sem).start()

                @pl.when(term > 0)
                def _():
                    source = kl_ref.at[jnp.clip(term - 1, 0, kl_terms - 1), at, :]
                    pltpu.make_async_copy(source, into, sem).start()

            return copies

        for n in range(modes + 1):
            load(n)
        for n in range(modes + 1):
            for made in load(n, begin=False):
                made.wait()
        low_there = jnp.where(side == 0, 0.0, 1.0)
        high_there = jnp.where(side == PLANES - 1, 0.0, 1.0)
        for n in range(modes):
            for i in range(lay.fields):
                if n > 0:
                    low = stage_ref[n - 1, i, rows - 1 :]
                else:
                    low = past_ref[i, tile - 1 :] * low_there
                if n < modes - 1:
                    high = stage_ref[n + 1, i, :1]
                else:
                    high = past_ref[i, :1] * high_there
                part, line = lay.edge(i)
                stage_ref[n, part, line : line + 1] = low
                stage_ref[n, part, line + 1 : line + 2] = high
            part, line = lay.edge(lay.fields)
            if part < lay.parts:
                stage_ref[n, part, line:] = jnp.zeros((rows - line, width), jnp.float32)
        for n, out_ref in enumerate(out_refs):
            to = jnp.bitwise_xor(mode, n)
            for part in range(lay.parts):
                out_ref[part] = stage_ref[to, part]

    shape = (lay.parts, rows, width)
    sent = pl.pallas_call(
        kernel,
        out_shape=[pltpu.VMEM(shape, jnp.float32)] * modes,
        in_specs=smem(1) + [pl.BlockSpec(memory_space=pltpu.HBM)] * 3,
        out_specs=vmem(modes),
        scratch_shapes=[
            pltpu.VMEM((modes, *shape), jnp.float32),
            pltpu.VMEM((lay.fields, tile, width), jnp.float32),
            pltpu.SemaphoreType.DMA((modes + 1, 1 + lay.share)),
        ],
        compiler_params=pltpu.CompilerParams(vmem_limit_bytes=VMEM_LIMIT),
        name="pack_crossing" if crossing else "pack_own",
    )(j, *[pltpu.with_memory_space_constraint(x, pltpu.HBM) for x in (field, mean, kl)])
    return [piece.reshape(lay.piece, width) for piece in sent]


def unpack(pieces, j, shape, lay, whole=None):
    rows = lay.rows
    there = [] if whole is None else [whole]

    def kernel(j_ref, *refs):
        piece_refs, out_ref, sems = refs[: len(pieces)], refs[-2], refs[-1]
        copies = []
        for n, (r, piece_ref) in enumerate(zip(pieces, piece_refs)):
            start = pl.multiple_of(jnp.bitwise_xor(j_ref[0], r) * rows, 8)
            made = pltpu.make_async_copy(
                piece_ref, out_ref.at[:, pl.ds(start, rows), :], sems.at[n]
            )
            made.start()
            copies.append(made)
        for made in copies:
            made.wait()

    return pl.pallas_call(
        kernel,
        out_shape=pltpu.HBM(shape, jnp.float32),
        in_specs=smem(1) + vmem(len(pieces)) + [pl.BlockSpec(memory_space=pltpu.HBM)] * len(there),
        out_specs=pl.BlockSpec(memory_space=pltpu.HBM),
        scratch_shapes=[pltpu.SemaphoreType.DMA((len(pieces),))],
        input_output_aliases={1 + len(pieces): 0} if there else {},
        compiler_params=pltpu.CompilerParams(vmem_limit_bytes=VMEM_LIMIT),
        name="unpack_last" if there else "unpack_first",
    )(j, *pieces.values(), *there)


def mains(pieces, lay):
    def kernel(*refs):
        for n in range(len(pieces)):
            refs[-1][n] = refs[n][: lay.main, :]

    return pl.pallas_call(
        kernel,
        out_shape=pltpu.VMEM((len(pieces), lay.main, lay.width), jnp.float32),
        in_specs=vmem(len(pieces)),
        out_specs=vmem(1)[0],
        compiler_params=pltpu.CompilerParams(vmem_limit_bytes=VMEM_LIMIT),
        name="mains",
    )(*pieces)


def coupling_lists(pattern, coupling, slot_mode):
    masked = (coupling * pattern.astype(jnp.float32))[1:]
    terms, modes = masked.shape[0], masked.shape[1]
    number = jnp.arange(modes, dtype=jnp.int32)
    one_hot = (slot_mode[:, None] == number[None, :]).astype(jnp.float32)
    coupled = jnp.einsum(
        "sa,kab,tb->kst", one_hot, masked, one_hot, precision=lax.Precision.HIGHEST
    )
    there = coupled != 0.0
    column = number[None, None, :]
    first = jnp.min(jnp.where(there, column, modes), 2)
    last = jnp.max(jnp.where(there, column, -1), 2)
    active = first < modes
    earlier = column < number[None, :, None]
    rank = jnp.sum(jnp.where(active[:, None, :] & earlier, 1, 0), 2)
    place = jnp.arange(ACTIVE, dtype=jnp.int32)[None, :, None]
    chosen = active[:, None, :] & (rank[:, None, :] == place)
    sources = jnp.sum(jnp.where(chosen, column, 0), 2)

    base = ACTIVE * jnp.arange(terms, dtype=jnp.int32)[:, None]
    products, factors, valid = [], [], []
    for chosen_t, is_valid in ((first, active), (last, last > first)):
        before = active[:, None, :] & (column < chosen_t[:, :, None])
        products.append(base + jnp.sum(jnp.where(before, 1, 0), 2))
        factors.append(jnp.sum(jnp.where(column == chosen_t[:, :, None], coupled, 0.0), 2))
        valid.append(is_valid)
    products = jnp.concatenate(products, 0)
    factors = jnp.concatenate(factors, 0)
    valid = jnp.concatenate(valid, 0)
    index = jnp.arange(2 * terms, dtype=jnp.int32)
    order = index[None, :] < index[:, None]
    rank = jnp.sum(jnp.where(valid[None] & order[:, :, None], 1, 0), 1)
    place = jnp.arange(MOST, dtype=jnp.int32)[:, None, None]
    chosen = valid[None] & (rank[None] == place)
    take = jnp.sum(jnp.where(chosen, products[None], 0), 1)
    factor = jnp.sum(jnp.where(chosen, factors[None], 0.0), 1)
    return sources, take, factor, jnp.sum(jnp.where(valid, 1, 0), 0)


def kernel_lists(sources, take, factor, count):
    number = jnp.arange(count.shape[0], dtype=jnp.int32)
    many = count > FEW
    rank = jnp.sum(jnp.where(many[None, :] & (number[None, :] < number[:, None]), 1, 0), 1)
    place = jnp.arange(MANY, dtype=jnp.int32)[None, :, None]
    chosen = many[None, None, :] & (rank[None, None, :] == place)
    take_more = jnp.sum(jnp.where(chosen, take[FEW:, None, :], 0), 2)
    factor_more = jnp.sum(jnp.where(chosen, factor[FEW:, None, :], 0.0), 2)
    more = jnp.where(many, rank, MANY)
    indices = [sources, take[:FEW].T, take_more.T, more]
    factors = [factor[:FEW].T, factor_more.T]
    return tuple(
        jnp.concatenate([part.reshape(-1) for part in parts]) for parts in (indices, factors)
    )


def tree_sum(values):
    while len(values) > 1:
        values = [sum(values[n : n + 2][1:], values[n]) for n in range(0, len(values), 2)]
    return values[0]


def stencil(pieces, others, halos, lists, j, name, lay):
    rows, width = lay.rows, lay.width
    full = (rows, width)
    arrays = list({id(array): array for array, _ in halos}.values())
    products = (lay.terms - 1) * ACTIVE

    def kernel(j_ref, index_ref, factor_ref, *refs):
        piece_refs, refs = refs[: lay.modes], refs[lay.modes :]
        other_refs, refs = refs[: lay.modes], refs[lay.modes :]
        halo_refs, refs = refs[: len(arrays)], refs[len(arrays) :]
        out_refs, (near_ref, product_ref, more_ref) = refs[: lay.modes], refs[lay.modes :]
        lane = lax.broadcasted_iota(jnp.int32, full, 1)
        line = lax.broadcasted_iota(jnp.int32, full, 0)
        mode = lax.rem(j_ref[0], lay.modes)
        ref_of = {id(array): ref for array, ref in zip(arrays, halo_refs)}
        halo_parts = [(ref_of[id(array)], n) for array, n in halos]

        def to_right(value):
            return pltpu.roll(value, width - 1, 1)

        def to_left(value):
            return pltpu.roll(value, 1, 1)

        for block in range(lay.modes):
            piece_ref, other_ref = piece_refs[block], other_refs[block]
            halo_ref, n = halo_parts[block]
            for i in range(lay.fields):
                own = i < lay.quota
                at, rows_i = lay.place(block, i), slice(i * rows, (i + 1) * rows)
                edge = lay.main + 2 * i
                here = piece_ref[rows_i, :]
                right = to_right(here)
                near_ref[at, 0] = here
                near_ref[at, 1] = jnp.where(lane == width - 1, 0.0, here - right) if own else right
                high, low = piece_ref[edge + 1 : edge + 2, :], piece_ref[edge : edge + 1, :]
                near_ref[at, 2] = jnp.where(line == rows - 1, high, pltpu.roll(here, rows - 1, 0))
                near_ref[at, 3] = jnp.where(line == 0, low, pltpu.roll(here, 1, 0))
                near_ref[at, 4] = other_ref[rows_i, :]
                near_ref[at, 5] = halo_ref[n, rows_i, :]

        def operator_of(term):
            at = lay.term_place(term, mode)
            here, right, *rest = [near_ref[at, n] for n in range(6)]
            across = jnp.where(lane == width - 1, 0.0, 0.5 * (here + right))
            ends = jnp.where((lane == 0) | (lane == width - 1), 0.5 * here, 0.0)
            faces = [0.5 * (here + n) for n in rest]
            diagonal = tree_sum([ends, *faces])

            def operator(t):
                flux = across * near_ref[t, 1]
                rest = [face * near_ref[t, n + 2] for n, face in enumerate(faces)]
                return (flux - to_left(flux)) + (diagonal * near_ref[t, 0] - tree_sum(rest))

            return operator

        def apply(term, carry):
            operator = operator_of(term)
            first = (term - 1) * ACTIVE
            for n in range(ACTIVE):
                product_ref[first + n] = operator(index_ref[first + n])
            return carry

        lax.fori_loop(1, lay.terms, apply, 0)

        def taken(first, count):
            return [
                factor_ref[e] * product_ref[index_ref[products + e]]
                for e in range(first, first + count)
            ]

        few, rest = FEW * lay.slots, MOST - FEW
        for n in range(MANY):
            more_ref[n] = tree_sum(taken(few + n * rest, rest))
        more_ref[MANY] = jnp.zeros(full, jnp.float32)
        more_at = products + few + MANY * rest
        operator = operator_of(0)
        for block in range(lay.modes):
            for i in range(lay.quota):
                s = block * lay.quota + i
                more = more_ref[index_ref[more_at + s]]
                out_refs[block][i] = tree_sum([operator(s), *taken(FEW * s, FEW), more])

    return pl.pallas_call(
        kernel,
        out_shape=[jax.ShapeDtypeStruct((lay.quota, rows, width), jnp.float32)] * lay.modes,
        in_specs=smem(3) + vmem(2 * lay.modes + len(arrays)),
        out_specs=vmem(lay.modes),
        scratch_shapes=[
            pltpu.VMEM((lay.places, 6, rows, width), jnp.float32),
            pltpu.VMEM((products, rows, width), jnp.float32),
            pltpu.VMEM((MANY + 1, rows, width), jnp.float32),
        ],
        compiler_params=pltpu.CompilerParams(vmem_limit_bytes=VMEM_LIMIT),
        name=name,
    )(j, *lists, *pieces, *others, *arrays)


def after(value, *done):
    return lax.optimization_barrier((value, *done))[0]


def on_device(chaos_field, mean_field, kl_fields, pattern, coupling, slot_mode):
    spaces, modes = lax.axis_size("space"), lax.axis_size("mode")
    quota, _, height, width = chaos_field.shape
    terms = kl_fields.shape[0] + 1
    lay = Layout(quota, terms, modes, height, width)
    axes = ("space", "mode")
    devices = spaces * modes
    space = lax.axis_index("space").astype(jnp.int32)
    mode = lax.axis_index("mode").astype(jnp.int32)
    j = (lax.rem(space, PLANES) * modes + mode).reshape(1)

    def swap(piece, r):
        if r == 0:
            return piece
        return lax.ppermute(piece, axes, [(d, d ^ r) for d in range(devices)])

    def shift(pieces, crossing):
        pairs = []
        for d in range(devices):
            upper = (d // modes) % PLANES == (0 if crossing else 1)
            other = d + lay.group if upper else d - lay.group
            if 0 <= other < devices:
                pairs.append((d, other))
        return lax.ppermute(mains(pieces, lay), axes, pairs)

    field, kl = chaos_field[:, 0], kl_fields[:, 0]
    sent = [None] * lay.group
    sent[:modes] = pack(field, mean_field, kl, j, False, lay)
    sent[modes:] = pack(field, mean_field, kl, after(j, *sent[:modes]), True, lay)
    half = modes // 2
    pieces = sent[:1] + [None] * (lay.group - 1)
    for r in [*range(half, modes), *range(1, half), *range(modes, modes + half)]:
        pieces[r] = swap(sent[r], r)
    for r in range(modes + half, lay.group):
        pieces[r] = swap(after(sent[r], *pieces[half:modes]), r)
    number = jnp.arange(modes, dtype=jnp.int32)
    mine = jnp.bitwise_xor(number, mode)[:, None, None] == number[None, :, None]
    slot_mode = jnp.sum(jnp.where(mine, slot_mode.reshape(1, modes, quota), 0), 1).reshape(-1)
    *lists, count = coupling_lists(pattern, coupling, slot_mode)
    pieces[half] = after(pieces[half], *lists, count)
    lists = kernel_lists(*lists, after(count, pieces[modes]))
    own_halo = shift(pieces[:modes], False)
    own_halos = [(own_halo, n) for n in range(modes)]
    early_halo = shift(pieces[modes : modes + half], True)
    crossing_halos = [(early_halo, n) for n in range(half)]
    for r in range(modes + half, lay.group):
        crossing_halos.append((shift(pieces[r : r + 1], True), 0))

    own, crossing = pieces[:modes], pieces[modes:]
    crossing_out = stencil(crossing, own, own_halos, lists, j, "stencil_crossing", lay)
    own_j = after(j, *crossing_out)
    own_out = stencil(own, crossing, crossing_halos, lists, own_j, "stencil_own", lay)
    out = [*own_out, *crossing_out]
    first = range(modes + half, lay.group)
    back = {r: swap(out[r], r) for r in first}
    for r in range(half, modes):
        back[r] = swap(out[r], r)
    for n in range(half):
        ahead = [back[r] for r in first[:n]]
        back[modes + n] = swap(after(out[modes + n], *own_out, *ahead), modes + n)
    for r in range(half):
        back[r] = swap(after(out[r], back[first[-1]]) if r else out[r], r)
    last = range(half, modes + half)
    shape = (quota, height, width)
    whole = unpack({r: back[r] for r in back if r not in last}, j, shape, lay)
    whole = unpack({r: back[r] for r in last}, j, shape, lay, whole)
    return whole.reshape(chaos_field.shape)


def solution(mesh):
    in_specs = (
        P("mode", "space", None, None),
        P("space", None, None),
        P(None, "space", None, None),
        P(),
        P(),
        P(),
    )
    out_specs = P("mode", "space", None, None)
    return jax.shard_map(
        on_device, mesh=mesh, in_specs=in_specs, out_specs=out_specs, check_vma=False
    )
```

```python
import jax
import jax.numpy as jnp
from jax import lax
from jax.experimental import pallas as pl
from jax.experimental.pallas import tpu as pltpu
from jax.sharding import PartitionSpec as P

VMEM_LIMIT = 20 * 1024 * 1024
PLANES = 2
ACTIVE = 49
MOST = 8
FEW = 3
MANY = 28


class Layout:
    def __init__(self, quota, terms, modes, height, width):
        self.modes = modes
        self.group = PLANES * modes
        self.rows = height // self.group
        self.width = width
        self.terms = terms
        self.quota = quota
        self.slots = quota * modes
        self.share = -(-terms // modes)
        self.fields = quota + self.share
        self.main = self.fields * self.rows
        self.parts = self.fields + -(-2 * self.fields // self.rows)
        self.piece = self.parts * self.rows
        self.places = self.fields * modes

    def edge(self, i):
        return self.fields + 2 * i // self.rows, 2 * i % self.rows

    def place(self, block, i):
        if i < self.quota:
            return block * self.quota + i
        return self.slots + block * self.share + (i - self.quota)

    def term_place(self, term, mode):
        owner = lax.div(term, self.share)
        block = jnp.bitwise_xor(owner, mode)
        return self.slots + block * self.share + (term - owner * self.share)


def vmem(count):
    return [pl.BlockSpec(memory_space=pltpu.VMEM)] * count


def smem(count):
    return [pl.BlockSpec(memory_space=pltpu.SMEM)] * count


def pack(field, mean, kl, j, crossing, lay):
    kl_terms = kl.shape[0]
    rows, width, modes, quota = lay.rows, lay.width, lay.modes, lay.quota
    half = modes * rows
    tile = 8

    def kernel(j_ref, field_ref, mean_ref, kl_ref, *refs):
        out_refs, (stage_ref, past_ref, in_sems) = refs[:modes], refs[modes:]
        plane = j_ref[0] // modes
        mode = j_ref[0] - plane * modes
        side = 1 - plane if crossing else plane
        start = side * half
        beside = pl.multiple_of(half - side * tile, tile)

        def load(n, begin=True):
            if n < modes:
                at, target = pl.ds(pl.multiple_of(start + n * rows, tile), rows), stage_ref.at[n]
            else:
                at, target = pl.ds(beside, tile), past_ref
            copies = [
                pltpu.make_async_copy(
                    field_ref.at[:, at, :], target.at[pl.ds(0, quota)], in_sems.at[n, 0]
                )
            ]
            if begin:
                copies[0].start()
            for i in range(lay.share):
                term = mode * lay.share + i
                into, sem = target.at[quota + i], in_sems.at[n, 1 + i]
                if not begin:
                    copies.append(pltpu.make_async_copy(mean_ref.at[0, at, :], into, sem))
                    continue

                @pl.when(term == 0)
                def _():
                    pltpu.make_async_copy(mean_ref.at[0, at, :], into, sem).start()

                @pl.when(term > 0)
                def _():
                    source = kl_ref.at[jnp.clip(term - 1, 0, kl_terms - 1), at, :]
                    pltpu.make_async_copy(source, into, sem).start()

            return copies

        for n in range(modes + 1):
            load(n)
        for n in range(modes + 1):
            for made in load(n, begin=False):
                made.wait()
        low_there = jnp.where(side == 0, 0.0, 1.0)
        high_there = jnp.where(side == PLANES - 1, 0.0, 1.0)
        for n in range(modes):
            for i in range(lay.fields):
                if n > 0:
                    low = stage_ref[n - 1, i, rows - 1 :]
                else:
                    low = past_ref[i, tile - 1 :] * low_there
                if n < modes - 1:
                    high = stage_ref[n + 1, i, :1]
                else:
                    high = past_ref[i, :1] * high_there
                part, line = lay.edge(i)
                stage_ref[n, part, line : line + 1] = low
                stage_ref[n, part, line + 1 : line + 2] = high
            part, line = lay.edge(lay.fields)
            if part < lay.parts:
                stage_ref[n, part, line:] = jnp.zeros((rows - line, width), jnp.float32)
        for n, out_ref in enumerate(out_refs):
            to = jnp.bitwise_xor(mode, n)
            for part in range(lay.parts):
                out_ref[part] = stage_ref[to, part]

    shape = (lay.parts, rows, width)
    sent = pl.pallas_call(
        kernel,
        out_shape=[pltpu.VMEM(shape, jnp.float32)] * modes,
        in_specs=smem(1) + [pl.BlockSpec(memory_space=pltpu.HBM)] * 3,
        out_specs=vmem(modes),
        scratch_shapes=[
            pltpu.VMEM((modes, *shape), jnp.float32),
            pltpu.VMEM((lay.fields, tile, width), jnp.float32),
            pltpu.SemaphoreType.DMA((modes + 1, 1 + lay.share)),
        ],
        compiler_params=pltpu.CompilerParams(vmem_limit_bytes=VMEM_LIMIT),
        name="pack_crossing" if crossing else "pack_own",
    )(j, *[pltpu.with_memory_space_constraint(x, pltpu.HBM) for x in (field, mean, kl)])
    return [piece.reshape(lay.piece, width) for piece in sent]


def unpack(pieces, j, shape, lay, whole=None):
    rows = lay.rows
    there = [] if whole is None else [whole]

    def kernel(j_ref, *refs):
        piece_refs, out_ref, sems = refs[: len(pieces)], refs[-2], refs[-1]
        copies = []
        for n, (r, piece_ref) in enumerate(zip(pieces, piece_refs)):
            start = pl.multiple_of(jnp.bitwise_xor(j_ref[0], r) * rows, 8)
            made = pltpu.make_async_copy(
                piece_ref, out_ref.at[:, pl.ds(start, rows), :], sems.at[n]
            )
            made.start()
            copies.append(made)
        for made in copies:
            made.wait()

    return pl.pallas_call(
        kernel,
        out_shape=pltpu.HBM(shape, jnp.float32),
        in_specs=smem(1) + vmem(len(pieces)) + [pl.BlockSpec(memory_space=pltpu.HBM)] * len(there),
        out_specs=pl.BlockSpec(memory_space=pltpu.HBM),
        scratch_shapes=[pltpu.SemaphoreType.DMA((len(pieces),))],
        input_output_aliases={1 + len(pieces): 0} if there else {},
        compiler_params=pltpu.CompilerParams(vmem_limit_bytes=VMEM_LIMIT),
        name="unpack_last" if there else "unpack_first",
    )(j, *pieces.values(), *there)


def mains(pieces, lay):
    def kernel(*refs):
        for n in range(len(pieces)):
            refs[-1][n] = refs[n][: lay.main, :]

    return pl.pallas_call(
        kernel,
        out_shape=pltpu.VMEM((len(pieces), lay.main, lay.width), jnp.float32),
        in_specs=vmem(len(pieces)),
        out_specs=vmem(1)[0],
        compiler_params=pltpu.CompilerParams(vmem_limit_bytes=VMEM_LIMIT),
        name="mains",
    )(*pieces)


def coupling_lists(pattern, coupling, slot_mode):
    masked = (coupling * pattern.astype(jnp.float32))[1:]
    terms, modes = masked.shape[0], masked.shape[1]
    number = jnp.arange(modes, dtype=jnp.int32)
    one_hot = (slot_mode[:, None] == number[None, :]).astype(jnp.float32)
    coupled = jnp.einsum(
        "sa,kab,tb->kst", one_hot, masked, one_hot, precision=lax.Precision.HIGHEST
    )
    there = coupled != 0.0
    column = number[None, None, :]
    first = jnp.min(jnp.where(there, column, modes), 2)
    last = jnp.max(jnp.where(there, column, -1), 2)
    active = first < modes
    earlier = column < number[None, :, None]
    rank = jnp.sum(jnp.where(active[:, None, :] & earlier, 1, 0), 2)
    place = jnp.arange(ACTIVE, dtype=jnp.int32)[None, :, None]
    chosen = active[:, None, :] & (rank[:, None, :] == place)
    sources = jnp.sum(jnp.where(chosen, column, 0), 2)

    base = ACTIVE * jnp.arange(terms, dtype=jnp.int32)[:, None]
    products, factors, valid = [], [], []
    for chosen_t, is_valid in ((first, active), (last, last > first)):
        before = active[:, None, :] & (column < chosen_t[:, :, None])
        products.append(base + jnp.sum(jnp.where(before, 1, 0), 2))
        factors.append(jnp.sum(jnp.where(column == chosen_t[:, :, None], coupled, 0.0), 2))
        valid.append(is_valid)
    products = jnp.concatenate(products, 0)
    factors = jnp.concatenate(factors, 0)
    valid = jnp.concatenate(valid, 0)
    index = jnp.arange(2 * terms, dtype=jnp.int32)
    order = index[None, :] < index[:, None]
    rank = jnp.sum(jnp.where(valid[None] & order[:, :, None], 1, 0), 1)
    place = jnp.arange(MOST, dtype=jnp.int32)[:, None, None]
    chosen = valid[None] & (rank[None] == place)
    take = jnp.sum(jnp.where(chosen, products[None], 0), 1)
    factor = jnp.sum(jnp.where(chosen, factors[None], 0.0), 1)
    return sources, take, factor, jnp.sum(jnp.where(valid, 1, 0), 0)


def kernel_lists(sources, take, factor, count):
    number = jnp.arange(count.shape[0], dtype=jnp.int32)
    many = count > FEW
    rank = jnp.sum(jnp.where(many[None, :] & (number[None, :] < number[:, None]), 1, 0), 1)
    place = jnp.arange(MANY, dtype=jnp.int32)[None, :, None]
    chosen = many[None, None, :] & (rank[None, None, :] == place)
    take_more = jnp.sum(jnp.where(chosen, take[FEW:, None, :], 0), 2)
    factor_more = jnp.sum(jnp.where(chosen, factor[FEW:, None, :], 0.0), 2)
    more = jnp.where(many, rank, MANY)
    indices = [sources, take[:FEW].T, take_more.T, more]
    factors = [factor[:FEW].T, factor_more.T]
    return tuple(
        jnp.concatenate([part.reshape(-1) for part in parts]) for parts in (indices, factors)
    )


def tree_sum(values):
    while len(values) > 1:
        values = [sum(values[n : n + 2][1:], values[n]) for n in range(0, len(values), 2)]
    return values[0]


def stencil(pieces, others, halos, lists, j, name, lay):
    rows, width = lay.rows, lay.width
    full = (rows, width)
    arrays = list({id(array): array for array, _ in halos}.values())
    products = (lay.terms - 1) * ACTIVE

    def kernel(j_ref, index_ref, factor_ref, *refs):
        piece_refs, refs = refs[: lay.modes], refs[lay.modes :]
        other_refs, refs = refs[: lay.modes], refs[lay.modes :]
        halo_refs, refs = refs[: len(arrays)], refs[len(arrays) :]
        out_refs, (near_ref, product_ref, more_ref) = refs[: lay.modes], refs[lay.modes :]
        lane = lax.broadcasted_iota(jnp.int32, full, 1)
        line = lax.broadcasted_iota(jnp.int32, full, 0)
        mode = lax.rem(j_ref[0], lay.modes)
        ref_of = {id(array): ref for array, ref in zip(arrays, halo_refs)}
        halo_parts = [(ref_of[id(array)], n) for array, n in halos]

        def to_right(value):
            return pltpu.roll(value, width - 1, 1)

        def to_left(value):
            return pltpu.roll(value, 1, 1)

        for block in range(lay.modes):
            piece_ref, other_ref = piece_refs[block], other_refs[block]
            halo_ref, n = halo_parts[block]
            for i in range(lay.fields):
                own = i < lay.quota
                at, rows_i = lay.place(block, i), slice(i * rows, (i + 1) * rows)
                edge = lay.main + 2 * i
                here = piece_ref[rows_i, :]
                right = to_right(here)
                near_ref[at, 0] = here
                near_ref[at, 1] = jnp.where(lane == width - 1, 0.0, here - right) if own else right
                high, low = piece_ref[edge + 1 : edge + 2, :], piece_ref[edge : edge + 1, :]
                near_ref[at, 2] = jnp.where(line == rows - 1, high, pltpu.roll(here, rows - 1, 0))
                near_ref[at, 3] = jnp.where(line == 0, low, pltpu.roll(here, 1, 0))
                near_ref[at, 4] = other_ref[rows_i, :]
                near_ref[at, 5] = halo_ref[n, rows_i, :]

        def operator_of(term):
            at = lay.term_place(term, mode)
            here, right, *rest = [near_ref[at, n] for n in range(6)]
            across = jnp.where(lane == width - 1, 0.0, 0.5 * (here + right))
            ends = jnp.where((lane == 0) | (lane == width - 1), 0.5 * here, 0.0)
            faces = [0.5 * (here + n) for n in rest]
            diagonal = tree_sum([ends, *faces])

            def operator(t):
                flux = across * near_ref[t, 1]
                rest = [face * near_ref[t, n + 2] for n, face in enumerate(faces)]
                return (flux - to_left(flux)) + (diagonal * near_ref[t, 0] - tree_sum(rest))

            return operator

        def apply(term, carry):
            operator = operator_of(term)
            first = (term - 1) * ACTIVE
            for n in range(ACTIVE):
                product_ref[first + n] = operator(index_ref[first + n])
            return carry

        lax.fori_loop(1, lay.terms, apply, 0)

        def taken(first, count):
            return [
                factor_ref[e] * product_ref[index_ref[products + e]]
                for e in range(first, first + count)
            ]

        few, rest = FEW * lay.slots, MOST - FEW
        for n in range(MANY):
            more_ref[n] = tree_sum(taken(few + n * rest, rest))
        more_ref[MANY] = jnp.zeros(full, jnp.float32)
        more_at = products + few + MANY * rest
        operator = operator_of(0)
        for block in range(lay.modes):
            for i in range(lay.quota):
                s = block * lay.quota + i
                more = more_ref[index_ref[more_at + s]]
                out_refs[block][i] = tree_sum([operator(s), *taken(FEW * s, FEW), more])

    return pl.pallas_call(
        kernel,
        out_shape=[jax.ShapeDtypeStruct((lay.quota, rows, width), jnp.float32)] * lay.modes,
        in_specs=smem(3) + vmem(2 * lay.modes + len(arrays)),
        out_specs=vmem(lay.modes),
        scratch_shapes=[
            pltpu.VMEM((lay.places, 6, rows, width), jnp.float32),
            pltpu.VMEM((products, rows, width), jnp.float32),
            pltpu.VMEM((MANY + 1, rows, width), jnp.float32),
        ],
        compiler_params=pltpu.CompilerParams(vmem_limit_bytes=VMEM_LIMIT),
        name=name,
    )(j, *lists, *pieces, *others, *arrays)


def after(value, *done):
    return lax.optimization_barrier((value, *done))[0]


def on_device(chaos_field, mean_field, kl_fields, pattern, coupling, slot_mode):
    spaces, modes = lax.axis_size("space"), lax.axis_size("mode")
    quota, _, height, width = chaos_field.shape
    terms = kl_fields.shape[0] + 1
    lay = Layout(quota, terms, modes, height, width)
    axes = ("space", "mode")
    devices = spaces * modes
    space = lax.axis_index("space").astype(jnp.int32)
    mode = lax.axis_index("mode").astype(jnp.int32)
    j = (lax.rem(space, PLANES) * modes + mode).reshape(1)

    def swap(piece, r):
        if r == 0:
            return piece
        return lax.ppermute(piece, axes, [(d, d ^ r) for d in range(devices)])

    def shift(pieces, crossing):
        pairs = []
        for d in range(devices):
            upper = (d // modes) % PLANES == (0 if crossing else 1)
            other = d + lay.group if upper else d - lay.group
            if 0 <= other < devices:
                pairs.append((d, other))
        return lax.ppermute(mains(pieces, lay), axes, pairs)

    field, kl = chaos_field[:, 0], kl_fields[:, 0]
    sent = [None] * lay.group
    sent[:modes] = pack(field, mean_field, kl, j, False, lay)
    sent[modes:] = pack(field, mean_field, kl, after(j, *sent[:modes]), True, lay)
    half = modes // 2
    pieces = sent[:1] + [None] * (lay.group - 1)
    for r in [*range(half, modes), *range(1, half), *range(modes, modes + half)]:
        pieces[r] = swap(sent[r], r)
    for r in range(modes + half, lay.group):
        pieces[r] = swap(after(sent[r], *pieces[half:modes]), r)
    number = jnp.arange(modes, dtype=jnp.int32)
    mine = jnp.bitwise_xor(number, mode)[:, None, None] == number[None, :, None]
    slot_mode = jnp.sum(jnp.where(mine, slot_mode.reshape(1, modes, quota), 0), 1).reshape(-1)
    *lists, count = coupling_lists(pattern, coupling, slot_mode)
    pieces[half] = after(pieces[half], *lists, count)
    lists = kernel_lists(*lists, after(count, pieces[modes]))
    own_halo = shift(pieces[:modes], False)
    own_halos = [(own_halo, n) for n in range(modes)]
    crossing_halos = []
    for r in (modes, modes + half):
        halo = shift(pieces[r : r + half], True)
        crossing_halos += [(halo, n) for n in range(half)]

    own, crossing = pieces[:modes], pieces[modes:]
    crossing_out = stencil(crossing, own, own_halos, lists, j, "stencil_crossing", lay)
    own_j = after(j, *crossing_out)
    own_out = stencil(own, crossing, crossing_halos, lists, own_j, "stencil_own", lay)
    out = [*own_out, *crossing_out]
    first = range(modes + half, lay.group)
    back = {r: swap(out[r], r) for r in first}
    for r in range(half, modes):
        back[r] = swap(out[r], r)
    for n in range(half):
        ahead = [back[r] for r in first[:n]]
        ahead = [*own_out, *ahead] if n else []
        back[modes + n] = swap(after(out[modes + n], *ahead), modes + n)
    for r in range(half):
        back[r] = swap(after(out[r], *[back[r] for r in first]) if r else out[r], r)
    last = range(half, modes + half)
    shape = (quota, height, width)
    whole = unpack({r: back[r] for r in back if r not in last}, j, shape, lay)
    whole = unpack({r: back[r] for r in last}, j, shape, lay, whole)
    return whole.reshape(chaos_field.shape)


def solution(mesh):
    in_specs = (
        P("mode", "space", None, None),
        P("space", None, None),
        P(None, "space", None, None),
        P(),
        P(),
        P(),
    )
    out_specs = P("mode", "space", None, None)
    return jax.shard_map(
        on_device, mesh=mesh, in_specs=in_specs, out_specs=out_specs, check_vma=False
    )
```

```python
import jax
import jax.numpy as jnp
from jax import lax
from jax.experimental import pallas as pl
from jax.experimental.pallas import tpu as pltpu
from jax.sharding import PartitionSpec as P

VMEM_LIMIT = 20 * 1024 * 1024
PLANES = 2
ACTIVE = 49
MOST = 8
FEW = 3
MANY = 28


class Layout:
    def __init__(self, quota, terms, modes, height, width):
        self.modes = modes
        self.group = PLANES * modes
        self.rows = height // self.group
        self.width = width
        self.terms = terms
        self.quota = quota
        self.slots = quota * modes
        self.share = -(-terms // modes)
        self.fields = quota + self.share
        self.main = self.fields * self.rows
        self.parts = self.fields + -(-2 * self.fields // self.rows)
        self.piece = self.parts * self.rows
        self.places = self.fields * modes

    def edge(self, i):
        return self.fields + 2 * i // self.rows, 2 * i % self.rows

    def place(self, block, i):
        if i < self.quota:
            return block * self.quota + i
        return self.slots + block * self.share + (i - self.quota)

    def term_place(self, term, mode):
        owner = lax.div(term, self.share)
        block = jnp.bitwise_xor(owner, mode)
        return self.slots + block * self.share + (term - owner * self.share)


def vmem(count):
    return [pl.BlockSpec(memory_space=pltpu.VMEM)] * count


def smem(count):
    return [pl.BlockSpec(memory_space=pltpu.SMEM)] * count


def pack(field, mean, kl, j, crossing, lay):
    kl_terms = kl.shape[0]
    rows, width, modes, quota = lay.rows, lay.width, lay.modes, lay.quota
    half = modes * rows
    tile = 8

    def kernel(j_ref, field_ref, mean_ref, kl_ref, *refs):
        out_refs, (stage_ref, past_ref, in_sems) = refs[:modes], refs[modes:]
        plane = j_ref[0] // modes
        mode = j_ref[0] - plane * modes
        side = 1 - plane if crossing else plane
        start = side * half
        beside = pl.multiple_of(half - side * tile, tile)

        def load(n, begin=True):
            if n < modes:
                at, target = pl.ds(pl.multiple_of(start + n * rows, tile), rows), stage_ref.at[n]
            else:
                at, target = pl.ds(beside, tile), past_ref
            copies = [
                pltpu.make_async_copy(
                    field_ref.at[:, at, :], target.at[pl.ds(0, quota)], in_sems.at[n, 0]
                )
            ]
            if begin:
                copies[0].start()
            for i in range(lay.share):
                term = mode * lay.share + i
                into, sem = target.at[quota + i], in_sems.at[n, 1 + i]
                if not begin:
                    copies.append(pltpu.make_async_copy(mean_ref.at[0, at, :], into, sem))
                    continue

                @pl.when(term == 0)
                def _():
                    pltpu.make_async_copy(mean_ref.at[0, at, :], into, sem).start()

                @pl.when(term > 0)
                def _():
                    source = kl_ref.at[jnp.clip(term - 1, 0, kl_terms - 1), at, :]
                    pltpu.make_async_copy(source, into, sem).start()

            return copies

        for n in range(modes + 1):
            load(n)
        for n in range(modes + 1):
            for made in load(n, begin=False):
                made.wait()
        low_there = jnp.where(side == 0, 0.0, 1.0)
        high_there = jnp.where(side == PLANES - 1, 0.0, 1.0)
        for n in range(modes):
            for i in range(lay.fields):
                if n > 0:
                    low = stage_ref[n - 1, i, rows - 1 :]
                else:
                    low = past_ref[i, tile - 1 :] * low_there
                if n < modes - 1:
                    high = stage_ref[n + 1, i, :1]
                else:
                    high = past_ref[i, :1] * high_there
                part, line = lay.edge(i)
                stage_ref[n, part, line : line + 1] = low
                stage_ref[n, part, line + 1 : line + 2] = high
            part, line = lay.edge(lay.fields)
            if part < lay.parts:
                stage_ref[n, part, line:] = jnp.zeros((rows - line, width), jnp.float32)
        for n, out_ref in enumerate(out_refs):
            to = jnp.bitwise_xor(mode, n)
            for part in range(lay.parts):
                out_ref[part] = stage_ref[to, part]

    shape = (lay.parts, rows, width)
    sent = pl.pallas_call(
        kernel,
        out_shape=[pltpu.VMEM(shape, jnp.float32)] * modes,
        in_specs=smem(1) + [pl.BlockSpec(memory_space=pltpu.HBM)] * 3,
        out_specs=vmem(modes),
        scratch_shapes=[
            pltpu.VMEM((modes, *shape), jnp.float32),
            pltpu.VMEM((lay.fields, tile, width), jnp.float32),
            pltpu.SemaphoreType.DMA((modes + 1, 1 + lay.share)),
        ],
        compiler_params=pltpu.CompilerParams(vmem_limit_bytes=VMEM_LIMIT),
        name="pack_crossing" if crossing else "pack_own",
    )(j, *[pltpu.with_memory_space_constraint(x, pltpu.HBM) for x in (field, mean, kl)])
    return [piece.reshape(lay.piece, width) for piece in sent]


def unpack(pieces, j, shape, lay, whole=None):
    rows = lay.rows
    there = [] if whole is None else [whole]

    def kernel(j_ref, *refs):
        piece_refs, out_ref, sems = refs[: len(pieces)], refs[-2], refs[-1]
        copies = []
        for n, (r, piece_ref) in enumerate(zip(pieces, piece_refs)):
            start = pl.multiple_of(jnp.bitwise_xor(j_ref[0], r) * rows, 8)
            made = pltpu.make_async_copy(
                piece_ref, out_ref.at[:, pl.ds(start, rows), :], sems.at[n]
            )
            made.start()
            copies.append(made)
        for made in copies:
            made.wait()

    return pl.pallas_call(
        kernel,
        out_shape=pltpu.HBM(shape, jnp.float32),
        in_specs=smem(1) + vmem(len(pieces)) + [pl.BlockSpec(memory_space=pltpu.HBM)] * len(there),
        out_specs=pl.BlockSpec(memory_space=pltpu.HBM),
        scratch_shapes=[pltpu.SemaphoreType.DMA((len(pieces),))],
        input_output_aliases={1 + len(pieces): 0} if there else {},
        compiler_params=pltpu.CompilerParams(vmem_limit_bytes=VMEM_LIMIT),
        name="unpack_last" if there else "unpack_first",
    )(j, *pieces.values(), *there)


def mains(pieces, lay):
    def kernel(*refs):
        for n in range(len(pieces)):
            refs[-1][n] = refs[n][: lay.main, :]

    return pl.pallas_call(
        kernel,
        out_shape=pltpu.VMEM((len(pieces), lay.main, lay.width), jnp.float32),
        in_specs=vmem(len(pieces)),
        out_specs=vmem(1)[0],
        compiler_params=pltpu.CompilerParams(vmem_limit_bytes=VMEM_LIMIT),
        name="mains",
    )(*pieces)


def coupling_lists(pattern, coupling, slot_mode):
    masked = (coupling * pattern.astype(jnp.float32))[1:]
    terms, modes = masked.shape[0], masked.shape[1]
    number = jnp.arange(modes, dtype=jnp.int32)
    one_hot = (slot_mode[:, None] == number[None, :]).astype(jnp.float32)
    coupled = jnp.einsum(
        "sa,kab,tb->kst", one_hot, masked, one_hot, precision=lax.Precision.HIGHEST
    )
    there = coupled != 0.0
    column = number[None, None, :]
    first = jnp.min(jnp.where(there, column, modes), 2)
    last = jnp.max(jnp.where(there, column, -1), 2)
    active = first < modes
    earlier = column < number[None, :, None]
    rank = jnp.sum(jnp.where(active[:, None, :] & earlier, 1, 0), 2)
    place = jnp.arange(ACTIVE, dtype=jnp.int32)[None, :, None]
    chosen = active[:, None, :] & (rank[:, None, :] == place)
    sources = jnp.sum(jnp.where(chosen, column, 0), 2)

    base = ACTIVE * jnp.arange(terms, dtype=jnp.int32)[:, None]
    products, factors, valid = [], [], []
    for chosen_t, is_valid in ((first, active), (last, last > first)):
        before = active[:, None, :] & (column < chosen_t[:, :, None])
        products.append(base + jnp.sum(jnp.where(before, 1, 0), 2))
        factors.append(jnp.sum(jnp.where(column == chosen_t[:, :, None], coupled, 0.0), 2))
        valid.append(is_valid)
    products = jnp.concatenate(products, 0)
    factors = jnp.concatenate(factors, 0)
    valid = jnp.concatenate(valid, 0)
    index = jnp.arange(2 * terms, dtype=jnp.int32)
    order = index[None, :] < index[:, None]
    rank = jnp.sum(jnp.where(valid[None] & order[:, :, None], 1, 0), 1)
    place = jnp.arange(MOST, dtype=jnp.int32)[:, None, None]
    chosen = valid[None] & (rank[None] == place)
    take = jnp.sum(jnp.where(chosen, products[None], 0), 1)
    factor = jnp.sum(jnp.where(chosen, factors[None], 0.0), 1)
    return sources, take, factor, jnp.sum(jnp.where(valid, 1, 0), 0)


def kernel_lists(sources, take, factor, count):
    number = jnp.arange(count.shape[0], dtype=jnp.int32)
    many = count > FEW
    rank = jnp.sum(jnp.where(many[None, :] & (number[None, :] < number[:, None]), 1, 0), 1)
    place = jnp.arange(MANY, dtype=jnp.int32)[None, :, None]
    chosen = many[None, None, :] & (rank[None, None, :] == place)
    take_more = jnp.sum(jnp.where(chosen, take[FEW:, None, :], 0), 2)
    factor_more = jnp.sum(jnp.where(chosen, factor[FEW:, None, :], 0.0), 2)
    more = jnp.where(many, rank, MANY)
    indices = [sources, take[:FEW].T, take_more.T, more]
    factors = [factor[:FEW].T, factor_more.T]
    return tuple(
        jnp.concatenate([part.reshape(-1) for part in parts]) for parts in (indices, factors)
    )


def tree_sum(values):
    while len(values) > 1:
        values = [sum(values[n : n + 2][1:], values[n]) for n in range(0, len(values), 2)]
    return values[0]


def stencil(pieces, others, halos, lists, j, name, lay):
    rows, width = lay.rows, lay.width
    full = (rows, width)
    arrays = list({id(array): array for array, _ in halos}.values())
    products = (lay.terms - 1) * ACTIVE

    def kernel(j_ref, index_ref, factor_ref, *refs):
        piece_refs, refs = refs[: lay.modes], refs[lay.modes :]
        other_refs, refs = refs[: lay.modes], refs[lay.modes :]
        halo_refs, refs = refs[: len(arrays)], refs[len(arrays) :]
        out_refs, (near_ref, product_ref, more_ref) = refs[: lay.modes], refs[lay.modes :]
        lane = lax.broadcasted_iota(jnp.int32, full, 1)
        line = lax.broadcasted_iota(jnp.int32, full, 0)
        mode = lax.rem(j_ref[0], lay.modes)
        ref_of = {id(array): ref for array, ref in zip(arrays, halo_refs)}
        halo_parts = [(ref_of[id(array)], n) for array, n in halos]

        def to_right(value):
            return pltpu.roll(value, width - 1, 1)

        def to_left(value):
            return pltpu.roll(value, 1, 1)

        for block in range(lay.modes):
            piece_ref, other_ref = piece_refs[block], other_refs[block]
            halo_ref, n = halo_parts[block]
            for i in range(lay.fields):
                own = i < lay.quota
                at, rows_i = lay.place(block, i), slice(i * rows, (i + 1) * rows)
                edge = lay.main + 2 * i
                here = piece_ref[rows_i, :]
                right = to_right(here)
                near_ref[at, 0] = here
                near_ref[at, 1] = jnp.where(lane == width - 1, 0.0, here - right) if own else right
                high, low = piece_ref[edge + 1 : edge + 2, :], piece_ref[edge : edge + 1, :]
                near_ref[at, 2] = jnp.where(line == rows - 1, high, pltpu.roll(here, rows - 1, 0))
                near_ref[at, 3] = jnp.where(line == 0, low, pltpu.roll(here, 1, 0))
                near_ref[at, 4] = other_ref[rows_i, :]
                near_ref[at, 5] = halo_ref[n, rows_i, :]

        def operator_of(term):
            at = lay.term_place(term, mode)
            here, right, *rest = [near_ref[at, n] for n in range(6)]
            across = jnp.where(lane == width - 1, 0.0, 0.5 * (here + right))
            ends = jnp.where((lane == 0) | (lane == width - 1), 0.5 * here, 0.0)
            faces = [0.5 * (here + n) for n in rest]
            diagonal = tree_sum([ends, *faces])

            def operator(t):
                flux = across * near_ref[t, 1]
                rest = [face * near_ref[t, n + 2] for n, face in enumerate(faces)]
                return (flux - to_left(flux)) + (diagonal * near_ref[t, 0] - tree_sum(rest))

            return operator

        def apply(term, carry):
            operator = operator_of(term)
            first = (term - 1) * ACTIVE
            for n in range(ACTIVE):
                product_ref[first + n] = operator(index_ref[first + n])
            return carry

        lax.fori_loop(1, lay.terms, apply, 0)

        def taken(first, count):
            return [
                factor_ref[e] * product_ref[index_ref[products + e]]
                for e in range(first, first + count)
            ]

        few, rest = FEW * lay.slots, MOST - FEW
        for n in range(MANY):
            more_ref[n] = tree_sum(taken(few + n * rest, rest))
        more_ref[MANY] = jnp.zeros(full, jnp.float32)
        more_at = products + few + MANY * rest
        operator = operator_of(0)
        for block in range(lay.modes):
            for i in range(lay.quota):
                s = block * lay.quota + i
                more = more_ref[index_ref[more_at + s]]
                out_refs[block][i] = tree_sum([operator(s), *taken(FEW * s, FEW), more])

    return pl.pallas_call(
        kernel,
        out_shape=[jax.ShapeDtypeStruct((lay.quota, rows, width), jnp.float32)] * lay.modes,
        in_specs=smem(3) + vmem(2 * lay.modes + len(arrays)),
        out_specs=vmem(lay.modes),
        scratch_shapes=[
            pltpu.VMEM((lay.places, 6, rows, width), jnp.float32),
            pltpu.VMEM((products, rows, width), jnp.float32),
            pltpu.VMEM((MANY + 1, rows, width), jnp.float32),
        ],
        compiler_params=pltpu.CompilerParams(vmem_limit_bytes=VMEM_LIMIT),
        name=name,
    )(j, *lists, *pieces, *others, *arrays)


def after(value, *done):
    return lax.optimization_barrier((value, *done))[0]


def on_device(chaos_field, mean_field, kl_fields, pattern, coupling, slot_mode):
    spaces, modes = lax.axis_size("space"), lax.axis_size("mode")
    quota, _, height, width = chaos_field.shape
    terms = kl_fields.shape[0] + 1
    lay = Layout(quota, terms, modes, height, width)
    axes = ("space", "mode")
    devices = spaces * modes
    space = lax.axis_index("space").astype(jnp.int32)
    mode = lax.axis_index("mode").astype(jnp.int32)
    j = (lax.rem(space, PLANES) * modes + mode).reshape(1)

    def swap(piece, r):
        if r == 0:
            return piece
        return lax.ppermute(piece, axes, [(d, d ^ r) for d in range(devices)])

    def shift(pieces, crossing):
        pairs = []
        for d in range(devices):
            upper = (d // modes) % PLANES == (0 if crossing else 1)
            other = d + lay.group if upper else d - lay.group
            if 0 <= other < devices:
                pairs.append((d, other))
        return lax.ppermute(mains(pieces, lay), axes, pairs)

    field, kl = chaos_field[:, 0], kl_fields[:, 0]
    sent = [None] * lay.group
    sent[:modes] = pack(field, mean_field, kl, j, False, lay)
    sent[modes:] = pack(field, mean_field, kl, after(j, *sent[:modes]), True, lay)
    half = modes // 2
    pieces = sent[:1] + [None] * (lay.group - 1)
    for r in [*range(half, modes), *range(1, half), *range(modes, modes + half)]:
        pieces[r] = swap(sent[r], r)
    for r in range(modes + half, lay.group):
        pieces[r] = swap(after(sent[r], *pieces[half:modes]), r)
    number = jnp.arange(modes, dtype=jnp.int32)
    mine = jnp.bitwise_xor(number, mode)[:, None, None] == number[None, :, None]
    slot_mode = jnp.sum(jnp.where(mine, slot_mode.reshape(1, modes, quota), 0), 1).reshape(-1)
    *lists, count = coupling_lists(pattern, coupling, slot_mode)
    pieces[half] = after(pieces[half], *lists, count)
    lists = kernel_lists(*lists, after(count, pieces[modes]))
    own_halo = shift(pieces[:modes], False)
    own_halos = [(own_halo, n) for n in range(modes)]
    crossing_halos = []
    for r in (modes, modes + half):
        halo = shift(pieces[r : r + half], True)
        crossing_halos += [(halo, n) for n in range(half)]

    own, crossing = pieces[:modes], pieces[modes:]
    crossing_out = stencil(crossing, own, own_halos, lists, j, "stencil_crossing", lay)
    own_j = after(j, *crossing_out)
    own_out = stencil(own, crossing, crossing_halos, lists, own_j, "stencil_own", lay)
    out = [*own_out, *crossing_out]
    first = range(modes + half, lay.group)
    back = {r: swap(out[r], r) for r in first}
    for r in range(half, modes):
        back[r] = swap(out[r], r)
    for n in range(half):
        ahead = [back[r] for r in first[:n]]
        back[modes + n] = swap(after(out[modes + n], *own_out, *ahead), modes + n)
    for r in range(half):
        back[r] = swap(after(out[r], back[first[-1]]) if r else out[r], r)
    last = range(half, modes + half)
    shape = (quota, height, width)
    whole = unpack({r: back[r] for r in back if r not in last}, j, shape, lay)
    whole = unpack({r: back[r] for r in last}, j, shape, lay, whole)
    return whole.reshape(chaos_field.shape)


def solution(mesh):
    in_specs = (
        P("mode", "space", None, None),
        P("space", None, None),
        P(None, "space", None, None),
        P(),
        P(),
        P(),
    )
    out_specs = P("mode", "space", None, None)
    return jax.shard_map(
        on_device, mesh=mesh, in_specs=in_specs, out_specs=out_specs, check_vma=False
    )
```
